128 devices in a mesh: pipe: 2 (over core), dp: 4 (over x), tensor: 16 (over z, y).
Axes of the slice: x: 4, y: 4, z: 4, core: 2. Of those that a mesh axis runs over, the one named last changes fastest.
Arguments:
- inputs: bfloat16 [8, 2048, 1024], P('dp', 'tensor'), may hold values from -6 to 6
- seq_lengths: int32 [8, 4], P('dp'), may hold values from 0 to 2048, as said below
- cotangent: bfloat16 [8, 2048, 1024], P('dp', 'tensor'), may hold values from -6 to 6
- ln_gain: float32 [2, 1024], P('pipe'), may hold values from 0.1 to 1.9
- ln_bias: float32 [2, 1024], P('pipe'), may hold values from -1.75 to 1.75
- w_qkv: bfloat16 [2, 1024, 16, 192], P('pipe', None, 'tensor'), may hold values from -0.1875 to 0.1875
- b_qkv: float32 [2, 16, 192], P('pipe', 'tensor'), may hold values from -1.75 to 1.75
- w_out: bfloat16 [2, 1024, 1024], P('pipe', 'tensor'), may hold values from -0.75 to 0.75
- b_out: float32 [2, 1024], P('pipe'), may hold values from -1.75 to 1.75
- w_up: bfloat16 [2, 1024, 4096], P('pipe', None, 'tensor'), may hold values from -0.1875 to 0.1875
- b_up: float32 [2, 4096], P('pipe', 'tensor'), may hold values from -1.75 to 1.75
- w_down: bfloat16 [2, 4096, 1024], P('pipe', 'tensor'), may hold values from -0.09375 to 0.09375
- b_down: float32 [2, 1024], P('pipe'), may hold values from -1.75 to 1.75
Outputs:
- activations: float32 [2, 8, 2048, 1024], P('pipe', 'dp', 'tensor')
- input_grads: float32 [2, 8, 2048, 1024], P('pipe', 'dp', 'tensor')
- grad_ln_gain: float32 [2, 1024], P('pipe')
- grad_ln_bias: float32 [2, 1024], P('pipe')
- grad_w_qkv: float32 [2, 1024, 16, 192], P('pipe', None, 'tensor')
- grad_b_qkv: float32 [2, 16, 192], P('pipe', 'tensor')
- grad_w_out: float32 [2, 1024, 1024], P('pipe', 'tensor')
- grad_b_out: float32 [2, 1024], P('pipe')
- grad_w_up: float32 [2, 1024, 4096], P('pipe', None, 'tensor')
- grad_b_up: float32 [2, 4096], P('pipe', 'tensor')
- grad_w_down: float32 [2, 4096, 1024], P('pipe', 'tensor')
- grad_b_down: float32 [2, 1024], P('pipe')
The draws below stay inside these ranges and needn't reach their ends.
Inputs may be any that keep to these rules, and one draw needn't show every extreme that they name: `seq_lengths`: each micro-batch packs up to 4 sequences, in slot order, whose lengths are multiples of 512 and sum to 2048; unused slots are 0 and come last. In each group of 2 consecutive micro-batches one is a single sequence of 2048 tokens.
All inputs are finite; a program needn't handle non-finite values.
Results may differ from the reference program's by a relative error of at most 0.035.
Values may be sent and summed in bfloat16 or wider, within the bound.
No kernel may reach another device: no remote copies, remote signals or barrier semaphores. Data moves between devices by JAX's collectives and lax.ppermute only.
A program may use at most 192 MiB of HBM per device.

```python
import jax
import jax.numpy as jnp
from jax import lax

D = 1024
HEADS = 16
HD = 64
FF = 4096
ROT = 16
SEQ = 2048
MICRO = 2
NSEG = 4
LAYERS = 2
BATCH = 8


def draw_seq_lengths(key, part):
    key = jax.random.fold_in(key, 11)
    first_key, second_key = jax.random.split(key)
    patterns = jax.random.randint(first_key, (BATCH,), 0, 8)
    chosen = jax.random.randint(second_key, (BATCH // MICRO,), 0, MICRO)
    whole_row = jnp.arange(BATCH) % MICRO == jnp.repeat(chosen, MICRO)
    patterns = jnp.where(whole_row, 0, patterns)
    first_cut = patterns % 2
    second_cut = patterns // 2 % 2
    third_cut = patterns // 4 % 2
    quarters = jnp.stack([jnp.zeros_like(patterns), first_cut, first_cut + second_cut, first_cut + second_cut + third_cut], axis=1)
    slots = jnp.arange(NSEG)
    tallies = jnp.sum((quarters[:, :, None] == slots[None, None, :]).astype(jnp.int32), axis=1)
    return (tallies * (SEQ // 4)).astype(jnp.int32)


def block_scale(rng, shape, shards, least, high):
    gain = 1.0
    for axis_at, blocks in shards:
        steps = jax.random.uniform(jax.random.fold_in(jax.random.fold_in(rng, 6), axis_at), (blocks,), jnp.float32, least / len(shards), high / len(shards))
        gain = gain * jnp.repeat(jnp.exp(steps), shape[axis_at] // blocks).reshape((-1,) + (1,) * (len(shape) - 1 - axis_at))
    return gain


def gaussian(key, dims, spread, most, shards=(), kind=jnp.bfloat16):
    drawn = spread * jax.random.normal(key, dims, jnp.float32)
    if shards:
        drawn = drawn * block_scale(key, dims, shards, -0.22, 0.18)
    return jnp.clip(drawn, -most, most).astype(kind)


def setup_inputs(seed: int = 0) -> dict:
    splits = jax.random.split(jax.random.key(seed), 14)
    inputs = gaussian(splits[0], (BATCH, SEQ, D), 1.0, 6.0, ((0, 4), (1, 16)))
    seq_lengths = draw_seq_lengths(jax.random.fold_in(splits[13], 71), 0)
    cotangent = gaussian(splits[2], (BATCH, SEQ, D), 1.0, 6.0, ((0, 4), (1, 16)))
    ln_gain = jnp.clip(1.0 + 0.18 * jax.random.normal(splits[3], (LAYERS, D), jnp.float32), 0.1, 1.9)
    ln_bias = gaussian(splits[4], (LAYERS, D), 0.3, 1.75, ((0, 2),), jnp.float32)
    w_qkv = gaussian(splits[5], (LAYERS, D, HEADS, 3 * HD), D ** -0.5, 0.1875, ((0, 2), (2, 16)))
    b_qkv = gaussian(splits[6], (LAYERS, HEADS, 3 * HD), 0.3, 1.75, ((0, 2), (1, 16)), jnp.float32)
    w_out = gaussian(splits[7], (LAYERS, D, D), (D // 16) ** -0.5, 0.75, ((0, 2), (1, 16)))
    b_out = gaussian(splits[8], (LAYERS, D), 0.3, 1.75, ((0, 2),), jnp.float32)
    w_up = gaussian(splits[9], (LAYERS, D, FF), D ** -0.5, 0.1875, ((0, 2), (2, 16)))
    b_up = gaussian(splits[10], (LAYERS, FF), 0.3, 1.75, ((0, 2), (1, 16)), jnp.float32)
    w_down = gaussian(splits[11], (LAYERS, FF, D), FF ** -0.5, 0.09375, ((0, 2), (1, 16)))
    b_down = gaussian(splits[12], (LAYERS, D), 0.3, 1.75, ((0, 2),), jnp.float32)
    return {"inputs": inputs, "seq_lengths": seq_lengths, "cotangent": cotangent, "ln_gain": ln_gain, "ln_bias": ln_bias, "w_qkv": w_qkv, "b_qkv": b_qkv, "w_out": w_out, "b_out": b_out, "w_up": w_up, "b_up": b_up, "w_down": w_down, "b_down": b_down}


@jax.custom_vjp
def low(v):
    return lax.optimization_barrier(v.astype(jnp.bfloat16)).astype(jnp.float32)

@jax.custom_vjp
def low_back(v):
    return v

def low_keep(v):
    return (low(v), None)

def low_pass(kept, grad):
    return (grad,)

def back_keep(v):
    return (v, None)

def back_low(kept, grad):
    return (low(grad),)
low.defvjp(low_keep, low_pass)
low_back.defvjp(back_keep, back_low)
EPSILON = 1e-05
NEGATIVE = -1e+30
ROOT_HALF = 0.7071067811865476

def layout(lengths):
    endings = jnp.cumsum(lengths)
    places = jnp.arange(SEQ, dtype=jnp.int32)
    passed = places[:, None] >= endings[None, :]
    return lax.optimization_barrier(jnp.sum(jnp.where(passed, lengths[None, :], 0), axis=1)).astype(jnp.int32)

def rotary_tables(starts):
    places = jnp.arange(SEQ, dtype=jnp.int32)
    inverse = jnp.power(10000.0, -2.0 * jnp.arange(ROT // 2, dtype=jnp.float32) / ROT)
    phases = (places - starts).astype(jnp.float32)[:, None] * inverse[None, :]
    return (jnp.cos(phases)[:, None, :], jnp.sin(phases)[:, None, :])

def rotate(tensor, cosine_table, sine_table):
    half_rot = ROT // 2
    former = tensor[..., :half_rot]
    latter = tensor[..., half_rot:ROT]
    return jnp.concatenate([former * cosine_table - latter * sine_table, latter * cosine_table + former * sine_table, tensor[..., ROT:]], axis=-1)

@jax.checkpoint
def one_head(query_head, key_head, value_head, starts):
    places = jnp.arange(SEQ, dtype=jnp.int32)
    scores = low_back(jnp.dot(query_head, key_head.T, precision=lax.Precision.HIGHEST) * HD ** (-0.5))
    allowed = (places[None, :] <= places[:, None]) & (places[None, :] >= starts[:, None])
    scores = jnp.where(allowed, scores, NEGATIVE)
    highest = lax.optimization_barrier(jnp.max(scores, axis=-1, keepdims=True))
    exponent = jnp.exp(scores - highest)
    probability = exponent / lax.optimization_barrier(jnp.sum(exponent, axis=-1, keepdims=True))
    return jnp.dot(low(probability), value_head, precision=lax.Precision.HIGHEST)

def block(row_input, layer_params, starts):
    norm_gain, norm_shift, weight_qkv, bias_qkv, weight_out, bias_out, weight_up, bias_up, weight_down, bias_down = layer_params
    cosine_table, sine_table = rotary_tables(starts)
    average = lax.optimization_barrier(jnp.mean(row_input, axis=-1, keepdims=True))
    centred = row_input - average
    variance = lax.optimization_barrier(jnp.mean(centred * centred, axis=-1, keepdims=True))
    normed = low(centred * lax.rsqrt(variance + EPSILON) * norm_gain + norm_shift)
    mixed = jnp.dot(normed, weight_qkv.reshape(D, 3 * D), precision=lax.Precision.HIGHEST).reshape(SEQ, HEADS, 3 * HD)
    joined = low_back(mixed + bias_qkv)
    queries = low(rotate(joined[..., :HD], cosine_table, sine_table))
    keys_all = low(rotate(joined[..., HD:2 * HD], cosine_table, sine_table))
    values_all = low(joined[..., 2 * HD:])
    heads_out = lax.map(lambda triple: one_head(triple[0], triple[1], triple[2], starts), (queries.transpose(1, 0, 2), keys_all.transpose(1, 0, 2), values_all.transpose(1, 0, 2)))
    attended = low(low_back(heads_out.transpose(1, 0, 2).reshape(SEQ, D)))
    branch_attn = jnp.dot(attended, weight_out, precision=lax.Precision.HIGHEST)
    inner_pre = low_back(jnp.dot(normed, weight_up, precision=lax.Precision.HIGHEST) + bias_up)
    activated = low(0.5 * inner_pre * (1.0 + lax.erf(inner_pre * ROOT_HALF)))
    branch_mlp = jnp.dot(activated, weight_down, precision=lax.Precision.HIGHEST)
    return row_input + branch_attn + branch_mlp + bias_out + bias_down

def section_rows(rows_in, layer_params, all_starts):
    checked = jax.checkpoint(block)
    return lax.map(lambda pair: checked(pair[0], layer_params, pair[1]), (rows_in, all_starts))

def reference(inputs, seq_lengths, cotangent, ln_gain, ln_bias, w_qkv, b_qkv, w_out, b_out, w_up, b_up, w_down, b_down):
    all_starts = jax.vmap(layout)(seq_lengths)
    stacked = (ln_gain, ln_bias, w_qkv, b_qkv, w_out, b_out, w_up, b_up, w_down, b_down)
    per_layer = [tuple((member[layer_index].astype(jnp.float32) for member in stacked)) for layer_index in range(LAYERS)]
    current = inputs.astype(jnp.float32)
    outputs = []
    pullers = []
    for layer_index in range(LAYERS):
        result, puller = jax.vjp(lambda rows_in, layer_params: section_rows(rows_in, layer_params, all_starts), current, per_layer[layer_index])
        outputs.append(result)
        pullers.append(puller)
        current = low(result)
    grads_in = [None] * LAYERS
    grads_par = [None] * LAYERS
    upstream = cotangent.astype(jnp.float32)
    for layer_index in reversed(range(LAYERS)):
        grad_rows, grad_params = pullers[layer_index](upstream)
        grads_in[layer_index] = grad_rows
        grads_par[layer_index] = grad_params
        upstream = low(grad_rows)
    gathered = [jnp.stack([grads_par[layer_index][member] for layer_index in range(LAYERS)]) for member in range(10)]
    return (jnp.stack(outputs), jnp.stack(grads_in), gathered[0], gathered[1], gathered[2], gathered[3], gathered[4], gathered[5], gathered[6], gathered[7], gathered[8], gathered[9])
```

```python
import jax
import jax.numpy as jnp
from jax import lax
from jax.sharding import Mesh, PartitionSpec as P

HD = 64
ROT = 16
EPSILON = 1e-05
NEGATIVE = -1e30
ROOT_HALF = 0.7071067811865476
INV_ROOT_TAU = 0.3989422804014327
DEVICES = ("pipe", "z", "y")
BF = jnp.bfloat16
F32 = jnp.float32


def table(rule):
    pairs = []
    for core in range(2):
        for z in range(4):
            for y in range(4):
                target = rule(core, z, y)
                if target is not None:
                    to_core, to_z, to_y = target
                    pairs.append((core * 16 + z * 4 + y, to_core * 16 + to_z % 4 * 4 + to_y))
    return pairs


def by_core(first, second):
    return table(lambda core, z, y: (first if core == 0 else second)(core, z, y))


def along_z(steps):
    return lambda core, z, y: (core, z + steps, y)


def to_pair(core, z, y):
    return (core, z, 3 - y)


def nowhere(core, z, y):
    return None


SIBLING = table(lambda core, z, y: (1 - core, z, y))
OVER = by_core(nowhere, lambda core, z, y: (1, z, y ^ 1))
BACK_OVER = by_core(nowhere, lambda core, z, y: (0, z, y ^ 1))
SWAP = by_core(lambda core, z, y: (1, z, y ^ 1), lambda core, z, y: (0, z, y))
GATHER_NEAR = (
    by_core(along_z(1), to_pair),
    by_core(along_z(-1), nowhere),
    by_core(along_z(2), nowhere),
)
GATHER_FAR = (
    by_core(to_pair, along_z(1)),
    by_core(to_pair, along_z(-1)),
    by_core(nowhere, along_z(2)),
)
SCATTER_FAR = (
    by_core(to_pair, along_z(-1)),
    by_core(to_pair, along_z(1)),
    by_core(nowhere, along_z(2)),
)
SCATTER_NEAR = (
    by_core(along_z(-1), to_pair),
    by_core(along_z(1), nowhere),
    by_core(along_z(2), nowhere),
)


def send(value, pairs):
    return lax.ppermute(value, DEVICES, pairs)


def gathered_blocks(z, y):
    def index(steps, column):
        return (z + steps) % 4 * 4 + column

    first = [
        index(0, y),
        index(-1, y),
        index(0, 3 - y),
        index(-1, 3 - y),
        index(1, 3 - y),
        index(2, 3 - y),
        index(1, y),
        index(2, y),
    ]
    second = [index(steps, column) for steps in (0, -1, 1, 2) for column in (y ^ 1, (3 - y) ^ 1)]
    return jnp.stack(first), jnp.stack(second)


def gather(rows, on_first):
    near = [send(rows, pairs) for pairs in GATHER_NEAR]
    first = jnp.concatenate([rows, near[0]])
    rest = jnp.concatenate([near[1], near[2]])
    far = [
        send(first, GATHER_FAR[0]),
        send(jnp.where(on_first, rest, first), GATHER_FAR[1]),
        send(first, GATHER_FAR[2]),
    ]
    own = [first, far[0], far[1], jnp.where(on_first, rest, far[2])]
    return own + [send(chunk, SIBLING) for chunk in own]


def scatter(chunks, on_first):
    n = chunks[0].shape[0] // 2
    others = [send(chunk, SIBLING) for chunk in chunks[4:]]
    summed = [a.astype(F32) + b.astype(F32) for a, b in zip(chunks[:4], others)]
    far = [send(summed[k + 1].astype(BF), SCATTER_FAR[k]).astype(F32) for k in range(3)]
    first = summed[0] + far[0] + far[2] + jnp.where(on_first, 0.0, far[1])
    rest = (summed[3] + far[1]).astype(BF)
    near = [
        send(first[n:].astype(BF), SCATTER_NEAR[0]),
        send(rest[:n], SCATTER_NEAR[1]),
        send(rest[n:], SCATTER_NEAR[2]),
    ]
    return first[:n] + near[0].astype(F32) + near[1].astype(F32) + near[2].astype(F32)


def start_rows(lengths, total_rows):
    endings = jnp.cumsum(lengths)
    places = jnp.arange(total_rows, dtype=jnp.int32)
    passed = places[:, None] >= endings[None, :]
    return jnp.sum(jnp.where(passed, lengths[None, :], 0), axis=1)


def rotary_tables(starts):
    places = jnp.arange(starts.shape[0], dtype=jnp.int32)
    inverse = jnp.power(10000.0, -2.0 * jnp.arange(ROT // 2, dtype=F32) / ROT)
    phases = (places - starts).astype(F32)[:, None] * inverse[None, :]
    return (jnp.cos(phases)[:, None, :], jnp.sin(phases)[:, None, :])


def rotate(tensor, cosine_table, sine_table):
    half_rot = ROT // 2
    former = tensor[..., :half_rot]
    latter = tensor[..., half_rot:ROT]
    return jnp.concatenate(
        [
            former * cosine_table - latter * sine_table,
            latter * cosine_table + former * sine_table,
            tensor[..., ROT:],
        ],
        axis=-1,
    )


def causal_mask(starts, first_row, block_rows):
    key_end = first_row + block_rows
    key_places = jnp.arange(key_end, dtype=jnp.int32)
    row_places = key_places[first_row:key_end]
    row_starts = starts[first_row:key_end]
    return (key_places[None, :] <= row_places[:, None]) & (
        key_places[None, :] >= row_starts[:, None]
    )


def dot(left, right, left_axis=1, right_axis=0):
    return lax.dot_general(
        left, right, (((left_axis,), (right_axis,)), ((), ())), preferred_element_type=F32
    )


def attend(queries, keys, values, starts):
    total_rows = queries.shape[0]
    block_rows = min(512, total_rows)
    pieces, log_sums = [], []
    for first_row in range(0, total_rows, block_rows):
        key_end = first_row + block_rows
        allowed = causal_mask(starts, first_row, block_rows)
        scores = dot(queries[first_row:key_end], keys[:key_end], 1, 1) * HD ** (-0.5)
        scores = jnp.where(allowed, scores, NEGATIVE)
        highest = jnp.max(scores, axis=-1, keepdims=True)
        exponent = jnp.exp(scores - highest)
        totals = jnp.sum(exponent, axis=-1, keepdims=True)
        pieces.append(dot((exponent / totals).astype(BF), values[:key_end]))
        log_sums.append(highest + jnp.log(totals))
    return jnp.concatenate(pieces), jnp.concatenate(log_sums)


def attend_back(queries, keys, values, grad_heads, log_sums, starts):
    total_rows = queries.shape[0]
    block_rows = min(512, total_rows)
    scale = HD ** (-0.5)
    grad_keys = jnp.zeros(queries.shape, F32)
    grad_values = jnp.zeros(queries.shape, F32)
    pieces = []
    for first_row in range(0, total_rows, block_rows):
        key_end = first_row + block_rows
        allowed = causal_mask(starts, first_row, block_rows)
        query_block = queries[first_row:key_end]
        grad_block = grad_heads[first_row:key_end]
        scores = dot(query_block, keys[:key_end], 1, 1) * scale
        scores = jnp.where(allowed, scores, NEGATIVE)
        probability = jnp.exp(scores - log_sums[first_row:key_end])
        grad_values = grad_values.at[:key_end].add(dot(probability.astype(BF), grad_block, 0, 0))
        grad_probs = dot(grad_block, values[:key_end], 1, 1)
        grad_scores = (
            probability * (grad_probs - jnp.sum(probability * grad_probs, axis=-1, keepdims=True))
        ).astype(BF)
        pieces.append(dot(grad_scores, keys[:key_end]) * scale)
        grad_keys = grad_keys.at[:key_end].add(dot(grad_scores, query_block, 0, 0) * scale)
    return jnp.concatenate(pieces), grad_keys, grad_values


def reorder(value, blocks):
    shape = value.shape
    return value.reshape((16, shape[0] // 16) + shape[1:])[blocks].reshape(shape)


def normalize(rows):
    average = jnp.mean(rows, axis=-1, keepdims=True)
    centred = rows - average
    inverse_std = lax.rsqrt(jnp.mean(centred * centred, axis=-1, keepdims=True) + EPSILON)
    return centred * inverse_std, inverse_std


def forward(rows, layer, place):
    on_first, places, blocks, starts, cosine_table, sine_table = place
    rows_f = rows.astype(F32)
    scaled, unused_std = normalize(rows_f)
    chunks = gather(scaled.astype(BF), on_first)
    features = jnp.concatenate(chunks)
    joined = dot(features, layer["qkv_scaled"], 1, 1) + layer["bias_qkv"]
    inner = dot(features, layer["up_scaled"]) + layer["bias_up"]
    wave = 1.0 + lax.erf(inner * ROOT_HALF)
    activated = (0.5 * inner * wave).astype(BF)
    slope = (0.5 * wave + inner * jnp.exp(-0.5 * inner * inner) * INV_ROOT_TAU).astype(BF)
    ordered = reorder(joined, places)
    queries = rotate(ordered[:, :HD], cosine_table, sine_table).astype(BF)
    keys = rotate(ordered[:, HD : 2 * HD], cosine_table, sine_table).astype(BF)
    values = ordered[:, 2 * HD :].astype(BF)
    heads_out, log_sums = attend(queries, keys, values, starts)
    attended = reorder(heads_out.astype(BF), blocks)
    partial = (dot(attended, layer["out"]) + dot(activated, layer["down"])).astype(BF)
    n = partial.shape[0] // 8
    branches = scatter([partial[k * n : (k + 1) * n] for k in range(8)], on_first)
    result = rows_f + branches + layer["bias_after"]
    return result, (features, queries, keys, values, log_sums, attended, activated, slope)


def backward(grad_rows, grad_full, rows, layer, saved, place):
    on_first, places, blocks, starts, cosine_table, sine_table = place
    features, queries, keys, values, log_sums, attended, activated, slope = saved
    grad_inner = (dot(grad_full, layer["down"], 1, 1) * slope.astype(F32)).astype(BF)
    grad_attended = dot(grad_full, layer["out"], 1, 1).astype(BF)
    grad_heads = reorder(grad_attended, places)
    grad_queries, grad_keys, grad_values = attend_back(
        queries, keys, values, grad_heads, log_sums, starts
    )
    grad_joined = jnp.concatenate(
        [
            rotate(grad_queries, cosine_table, -sine_table),
            rotate(grad_keys, cosine_table, -sine_table),
            grad_values,
        ],
        axis=-1,
    ).astype(BF)
    grad_joined = reorder(grad_joined, blocks)
    partial = (
        dot(grad_joined, layer["qkv_scaled"]) + dot(grad_inner, layer["up_scaled"], 1, 1)
    ).astype(BF)
    n = partial.shape[0] // 8
    grad_normed = scatter([partial[k * n : (k + 1) * n] for k in range(8)], on_first)
    scaled, inverse_std = normalize(rows.astype(F32))
    grad_input = grad_rows.astype(F32) + inverse_std * (
        grad_normed
        - jnp.mean(grad_normed, axis=-1, keepdims=True)
        - scaled * jnp.mean(grad_normed * scaled, axis=-1, keepdims=True)
    )

    raw_qkv = dot(grad_joined, features, 0, 0)
    raw_up = dot(features, grad_inner, 0, 0)
    grad_b_qkv = jnp.sum(grad_joined.astype(F32), axis=0)
    grad_b_up = jnp.sum(grad_inner.astype(F32), axis=0)
    gain, shift = layer["gain"], layer["shift"]
    grad_qkv = raw_qkv * gain[None, :] + grad_b_qkv[:, None] * shift[None, :]
    grad_up = raw_up * gain[:, None] + shift[:, None] * grad_b_up[None, :]
    grad_out = dot(attended, grad_full, 0, 0)
    grad_down = dot(activated, grad_full, 0, 0)
    qkv, up = layer["qkv"].astype(F32), layer["up"].astype(F32)
    grad_gain = jnp.sum(raw_qkv * qkv, axis=0) + jnp.sum(raw_up * up, axis=1)
    grad_shift = jnp.sum(grad_b_qkv[:, None] * qkv, axis=0) + jnp.sum(
        grad_b_up[None, :] * up, axis=1
    )
    biases = jnp.concatenate([grad_b_qkv, grad_b_up, jnp.zeros((1024 - 448,), F32)])
    tall = jnp.concatenate([grad_qkv, grad_out, grad_down, jnp.pad(biases[None], ((0, 15), (0, 0)))])
    vectors = jnp.stack([grad_gain, grad_shift, jnp.sum(grad_rows.astype(F32), axis=0)])
    return grad_input, tall, grad_up, vectors


def ring_sum(value, axis):
    pieces = [
        lax.ppermute(value, axis, [(i, (i + steps) % 4) for i in range(4)]) for steps in (1, 2, 3)
    ]
    return value + pieces[0] + pieces[1] + pieces[2]


def body(
    inputs,
    seq_lengths,
    cotangent,
    ln_gain,
    ln_bias,
    w_qkv,
    b_qkv,
    w_out,
    b_out,
    w_up,
    b_up,
    w_down,
    b_down,
):
    core, z, y = (lax.axis_index(name) for name in DEVICES)
    on_first = core == 0
    micro = jnp.where((y == 0) | (y == 3), 0, 1)
    on_micro_0 = micro == 0

    def pick(value, index):
        return lax.dynamic_index_in_dim(value, index, 0, keepdims=False)

    rows_0 = jnp.where(on_first, pick(inputs, micro), send(pick(inputs, 1 - micro), OVER))
    grad_rows_1 = jnp.where(on_first, pick(cotangent, micro), send(pick(cotangent, 1 - micro), OVER))

    tall = jnp.concatenate([w_qkv[0].reshape(1024, 192).T, w_out[0], w_down[0]])
    mine = (tall, w_up[0], jnp.concatenate([b_qkv[0].reshape(1, 192), b_up], axis=1))
    swapped = [send(member, SWAP) for member in mine]
    over = [send(member, OVER) for member in mine]
    norms = jnp.concatenate([ln_gain, ln_bias, b_out + b_down])
    other_norms = send(norms, SIBLING)

    def layer_of(members, norm):
        tall, up, biases = members
        gain, shift, bias_after = norm[0], norm[1], norm[2]
        qkv, out, down = tall[:192], tall[192:256], tall[256:]
        qkv_f, up_f = qkv.astype(F32), up.astype(F32)
        return {
            "gain": gain,
            "shift": shift,
            "qkv": qkv,
            "up": up,
            "out": out,
            "down": down,
            "bias_after": bias_after,
            "qkv_scaled": (qkv_f * gain[None, :]).astype(BF),
            "up_scaled": (up_f * gain[:, None]).astype(BF),
            "bias_qkv": biases[0, :192] + jnp.sum(qkv_f * shift[None, :], axis=1),
            "bias_up": biases[0, 192:] + jnp.sum(up_f * shift[:, None], axis=0),
        }

    layer_0 = layer_of(
        [jnp.where(on_first, a, b) for a, b in zip(mine, swapped)],
        jnp.where(on_first, norms, other_norms),
    )
    layer_1 = layer_of(
        [jnp.where(on_first, a, b) for a, b in zip(swapped, over)],
        jnp.where(on_first, other_norms, norms),
    )

    starts = start_rows(pick(seq_lengths, micro), 2048)
    cosine_table, sine_table = rotary_tables(starts)
    cosine_table, sine_table = cosine_table[:, 0], sine_table[:, 0]
    first, second = gathered_blocks(z, y)
    blocks = jnp.where(
        on_first, jnp.concatenate([first, second]), jnp.concatenate([second, first])
    )
    places = jnp.argsort(blocks)
    place = (on_first, places, blocks, starts, cosine_table, sine_table)

    result_0, saved_0 = forward(rows_0, layer_0, place)
    rows_1 = result_0.astype(BF)
    result_1, saved_1 = forward(rows_1, layer_1, place)
    grad_full_1 = jnp.concatenate(gather(grad_rows_1, on_first))
    grad_input_1, tall_1, up_1, vectors_1 = backward(
        grad_rows_1, grad_full_1, rows_1, layer_1, saved_1, place
    )

    def sum_1(value):
        value = value.astype(BF)
        return (send(value, SIBLING).astype(F32) + send(value, OVER).astype(F32)).astype(BF)

    def sum_0(value):
        return (value + send(value.astype(BF), BACK_OVER).astype(F32)).astype(BF)

    total_1 = lax.psum((sum_1(tall_1), sum_1(up_1)), "dp")

    grad_rows_0 = grad_input_1.astype(BF)
    grad_full_0 = jnp.concatenate(gather(grad_rows_0, on_first))
    grad_input_0, tall_0, up_0, vectors_0 = backward(
        grad_rows_0, grad_full_0, rows_0, layer_0, saved_0, place
    )
    total_0 = lax.psum((sum_0(tall_0), sum_0(up_0)), "dp")
    tall, up = (jnp.where(on_first, a, b).astype(F32) for a, b in zip(total_0, total_1))

    vectors = jnp.concatenate([vectors_0, vectors_1])
    vectors = vectors + send(vectors, SIBLING)
    for axis in ("y", "z", "dp"):
        vectors = ring_sum(vectors, axis)
    vectors = jnp.where(on_first, vectors[:3], vectors[3:])

    def outputs_of(value_0, value_1):
        here = jnp.where(on_first, value_0, send(value_1, SIBLING))
        there = jnp.where(on_first, send(value_0, BACK_OVER), send(value_1, OVER))
        return jnp.stack(
            [jnp.where(on_micro_0, here, there), jnp.where(on_micro_0, there, here)]
        )[None]

    return (
        outputs_of(result_0, result_1),
        outputs_of(grad_input_0, grad_input_1),
        vectors[0:1],
        vectors[1:2],
        tall[:192].T.reshape(1, 1024, 1, 192),
        tall[512, :192].reshape(1, 1, 192),
        tall[192:256][None],
        vectors[2:3],
        up[None],
        tall[512:513, 192:448],
        tall[256:512][None],
        vectors[2:3],
    )


def solution(mesh):
    rows = P("dp", ("z", "y"), None)
    layer_rows = P("pipe", "dp", ("z", "y"), None)
    heads = P("pipe", None, ("z", "y"), None)
    split = P("pipe", ("z", "y"), None)
    units = P("pipe", None, ("z", "y"))
    whole = P("pipe", None)
    unit_bias = P("pipe", ("z", "y"))
    return jax.shard_map(
        body,
        mesh=Mesh(mesh.devices.reshape(2, 4, 4, 4), ("pipe", "dp", "z", "y")),
        in_specs=(
            rows,
            P("dp", None),
            rows,
            whole,
            whole,
            heads,
            split,
            split,
            whole,
            units,
            unit_bias,
            split,
            whole,
        ),
        out_specs=(
            layer_rows,
            layer_rows,
            whole,
            whole,
            heads,
            split,
            split,
            whole,
            units,
            unit_bias,
            split,
            whole,
        ),
        check_vma=False,
    )
```

```python
import functools

import jax
import jax.numpy as jnp
from jax import lax
from jax.experimental import pallas as pl
from jax.experimental.pallas import tpu as pltpu
from jax.sharding import Mesh, PartitionSpec as P

HD = 64
ROT = 16
FF_HERE = 256
QKV = 3 * HD
IN = FF_HERE + QKV
OUT = FF_HERE + HD
PACKED = IN + 16 + OUT
SUMMED = 832
F_LIMIT = 16
B_LIMIT = 26
ROWS = 2048
BLOCK = 128
SPAN = 512
SPANS = ROWS // SPAN
PER_SPAN = SPAN // BLOCK
EPSILON = 1e-05
NEGATIVE = -1e30
ROOT_HALF = 0.7071067811865476
INV_ROOT_TAU = 0.3989422804014327
DEVICES = ("pipe", "z", "y")
BF = jnp.bfloat16
F32 = jnp.float32


def table(rule):
    pairs = []
    for core in range(2):
        for z in range(4):
            for y in range(4):
                target = rule(core, z, y)
                if target is not None:
                    to_core, to_z, to_y = target
                    pairs.append((core * 16 + z * 4 + y, to_core * 16 + to_z % 4 * 4 + to_y))
    return pairs


def by_core(first, second):
    return table(lambda core, z, y: (first if core == 0 else second)(core, z, y))


def step(steps, flip=0):
    return lambda core, z, y: (core, z + steps, y ^ flip)


def nowhere(core, z, y):
    return None


PAIR = 3
SIBLING = table(lambda core, z, y: (1 - core, z, y))
OVER = by_core(nowhere, step(0, 1))
BACK_OVER = by_core(nowhere, lambda core, z, y: (0, z, y ^ 1))
SWAP = by_core(lambda core, z, y: (1, z, y ^ 1), lambda core, z, y: (0, z, y))
RING = (1, -1, 2)


def send(value, pairs):
    return lax.ppermute(value, DEVICES, pairs)


def gathered_blocks(core, z, y):
    def of(own):
        columns = (y ^ own, y ^ own ^ PAIR)
        steps = [0] + [-hops for hops in RING]
        return [(z + hops) % 4 * 4 + column for column in columns for hops in steps]

    first, second = jnp.stack(of(0)), jnp.stack(of(1))
    return jnp.where(
        core == 0, jnp.concatenate([first, second]), jnp.concatenate([second, first])
    ).astype(jnp.int32)


def with_sibling(blocks):
    return blocks + [send(block, SIBLING) for block in blocks]


def gather(rows):
    pair = send(rows, table(step(0, PAIR)))
    own = [send(rows, table(step(hops))) for hops in RING]
    far = [send(pair, table(step(hops))) for hops in RING]
    return with_sibling([rows] + own + [pair] + far)


def gather_arguments(rows, on_first):
    near = send(rows, by_core(step(0, PAIR), step(0, 1)))
    beside = send(rows, by_core(nowhere, step(0, 2)))
    own = [send(rows, by_core(step(hops), step(hops, 1))) for hops in RING]
    here, pair = jnp.where(on_first, rows, near), jnp.where(on_first, near, beside)
    far = [send(pair, table(step(hops))) for hops in RING]
    return with_sibling([here] + own + [pair] + far)


def scatter(blocks):
    steps = [(-hops, 0) for hops in RING] + [(0, PAIR)] + [(-hops, PAIR) for hops in RING]
    return [send(block, table(step(hops, flip))) for block, (hops, flip) in zip(blocks, steps)]


def start_rows(lengths, total_rows):
    endings = jnp.cumsum(lengths)
    places = jnp.arange(total_rows, dtype=jnp.int32)
    passed = places[:, None] >= endings[None, :]
    return jnp.sum(jnp.where(passed, lengths[None, :], 0), axis=1)


def normalize(rows):
    average = jnp.mean(rows, axis=-1, keepdims=True)
    centred = rows - average
    inverse_std = lax.rsqrt(jnp.mean(centred * centred, axis=-1, keepdims=True) + EPSILON)
    return centred * inverse_std, inverse_std


def normalize_back(grad_rows, grad_scaled, rows):
    scaled, inverse_std = normalize(rows.astype(F32))
    return grad_rows.astype(F32) + inverse_std * (
        grad_scaled
        - jnp.mean(grad_scaled, axis=-1, keepdims=True)
        - scaled * jnp.mean(grad_scaled * scaled, axis=-1, keepdims=True)
    )


def block_of(index):
    return pl.ds(pl.multiple_of(index * BLOCK, BLOCK), BLOCK)


def dot(left, right, left_axis=1, right_axis=0):
    return lax.dot_general(
        left, right, (((left_axis,), (right_axis,)), ((), ())), preferred_element_type=F32
    )


def started(parts, sems, first):
    copies = [pltpu.make_async_copy(*part, sems.at[first + k]) for k, part in enumerate(parts)]
    for copy in copies:
        copy.start()
    return copies


def finished(copies):
    for copy in copies:
        copy.wait()


def stacked(refs, group, first):
    return jnp.concatenate(
        [refs[group * PER_SPAN + k][first : first + BLOCK] for k in range(PER_SPAN)]
    )


def half_of(refs, group):
    place = group % (SPANS // 2) * SPAN
    return refs[group // (SPANS // 2)].at[pl.ds(place, SPAN)]


def turned(pairs):
    lane = lax.broadcasted_iota(jnp.int32, pairs.shape, 1) % HD
    return jnp.where(
        lane < ROT // 2, -pltpu.roll(pairs, 2 * HD - ROT // 2, 1), pltpu.roll(pairs, ROT // 2, 1)
    )


def halves(pairs):
    lane = lax.broadcasted_iota(jnp.int32, pairs.shape, 1)
    queries = jnp.where(lane < HD, pairs * HD ** (-0.5), 0.0)
    return queries.astype(BF), pltpu.roll(pairs, HD, 1).astype(BF)


def penalty(segments_ref, query_span, key_span):
    return jnp.where(key_span >= segments_ref[query_span], 0.0, -NEGATIVE).astype(F32)


def seen(scores):
    keys = lax.broadcasted_iota(jnp.int32, scores.shape, 0)
    queries = lax.broadcasted_iota(jnp.int32, scores.shape, 1)
    return jnp.where(keys <= queries, scores, NEGATIVE)


def forward_kernel(*refs):
    blocks_ref, segments_ref = refs[:2]
    chunk_refs, refs = refs[2:18], refs[18:]
    w_in_ref, bias_ref, w_out_ref, cosine_ref, sine_ref = refs[:5]
    half_refs, log_sums_ref, refs = refs[5:7], refs[7], refs[8:]
    count = len(refs) - 9
    kept_hbm, kept_refs, refs = refs[:count], refs[count : count + 4], refs[count + 4 :]
    mixed_ref, slope_ref, pairs_ref, values_ref = kept_refs
    queries_ref, keys_ref, turned_values_ref, ordered_ref, sems = refs
    copies = []
    if len(kept_hbm) == 5:
        parts = [
            (ref, kept_hbm[4].at[pl.ds(k * BLOCK, BLOCK)]) for k, ref in enumerate(chunk_refs)
        ]
        copies = started(parts, sems, 0)
    for group in range(SPANS):
        rows = slice(group * SPAN, (group + 1) * SPAN)
        projected = dot(stacked(chunk_refs, group, 0), w_in_ref[...], 1, 1) + bias_ref[...]
        inner = projected[:, :FF_HERE]
        wave = 1.0 + lax.erf(inner * ROOT_HALF)
        mixed_ref[rows, :FF_HERE] = (0.5 * inner * wave).astype(BF)
        slope = 0.5 * wave + inner * jnp.exp(-0.5 * inner * inner) * INV_ROOT_TAU
        slope_ref[rows] = slope.astype(BF)
        for k in range(PER_SPAN):
            joined = projected[k * BLOCK : (k + 1) * BLOCK, FF_HERE:]
            place = block_of(blocks_ref[group * PER_SPAN + k])
            pairs = joined[:, : 2 * HD]
            pairs = pairs * cosine_ref[place] + turned(pairs) * sine_ref[place]
            pairs_ref[place] = pairs.astype(BF)
            queries_ref[place], keys_ref[place] = halves(pairs.astype(BF).astype(F32))
            values = joined[:, 2 * HD :]
            values_ref[place] = values.astype(BF)
            turned_values_ref[:, place] = values.T.astype(BF)
    for i in range(SPANS):
        span = slice(i * SPAN, (i + 1) * SPAN)
        queries = queries_ref[span]
        scores, offsets, highest = [], [], None
        for j in range(i + 1):
            block = dot(keys_ref[j * SPAN : (j + 1) * SPAN], queries, 1, 1)
            block = seen(block) if i == j else block
            offset = 0.0 if i == j else penalty(segments_ref, i, j)
            top = jnp.max(block, axis=0, keepdims=True) - offset
            highest = top if highest is None else jnp.maximum(highest, top)
            scores.append(block)
            offsets.append(offset)
        total, summed = 0.0, 0.0
        for j in range(i + 1):
            exponent = jnp.exp(scores[j] - (highest + offsets[j]))
            total = total + jnp.sum(exponent, axis=0, keepdims=True)
            summed = summed + dot(
                turned_values_ref[:, j * SPAN : (j + 1) * SPAN], exponent.astype(BF)
            )
        log_sums_ref[:, span] = highest + jnp.log(total)
        ordered_ref[span] = (summed / total).T.astype(BF)
    for group in range(SPANS):
        for k in range(PER_SPAN):
            index = group * PER_SPAN + k
            here = slice(index * BLOCK, (index + 1) * BLOCK)
            mixed_ref[here, FF_HERE:] = ordered_ref[block_of(blocks_ref[index])]
        rows = slice(group * SPAN, (group + 1) * SPAN)
        half_of(half_refs, group)[...] = dot(mixed_ref[rows], w_out_ref[...]).astype(BF)
    copies += started(list(zip(kept_refs, kept_hbm)), sems, 16)
    finished(copies)


def backward_kernel(separate, n_earlier, *refs):
    blocks_ref, segments_ref = refs[:2]
    chunk_refs, refs = refs[2:18], refs[18:]
    w_in_ref, w_out_ref, kept_ref, norm_ref, log_sums_ref, cosine_ref, sine_ref = refs[:7]
    count = 5 if separate else 4
    first = 0 if separate else BLOCK
    saved_hbm, refs = refs[7 : 7 + count], refs[7 + count + n_earlier :]
    half_refs, grads_ref, vectors_ref, refs = refs[:2], refs[2], refs[3], refs[4:]
    saved_refs, refs = refs[:count], refs[count:]
    mixed_ref, slope_ref, pairs_ref, values_ref = saved_refs[:4]
    features_ref = saved_refs[-1]
    grad_in_ref, queries_ref, keys_ref, turned_keys_ref, grad_heads_ref, products_ref = refs[:6]
    grad_queries_ref, grad_keys_ref, grad_values_ref, sems = refs[6:]
    copies = started(list(zip(saved_hbm, saved_refs)), sems, 0)
    finished(copies[:4])
    for group in range(SPANS):
        rows = slice(group * SPAN, (group + 1) * SPAN)
        grad_mixed = dot(stacked(chunk_refs, group, first), w_out_ref[...], 1, 1)
        grad_in_ref[rows, :FF_HERE] = (
            grad_mixed[:, :FF_HERE] * slope_ref[rows].astype(F32)
        ).astype(BF)
        for k in range(PER_SPAN):
            index = group * PER_SPAN + k
            here, place = slice(index * BLOCK, (index + 1) * BLOCK), block_of(blocks_ref[index])
            grad_heads = grad_mixed[k * BLOCK : (k + 1) * BLOCK, FF_HERE:].astype(BF)
            grad_heads_ref[place] = grad_heads
            product = grad_heads.astype(F32) * mixed_ref[here, FF_HERE:].astype(F32)
            products_ref[:, place] = jnp.sum(product.T, axis=0, keepdims=True)
            queries_ref[here], keys = halves(pairs_ref[here].astype(F32))
            keys_ref[here] = keys
            turned_keys_ref[:, here] = keys[:, :HD].astype(F32).T.astype(BF)
    grad_queries_ref[...] = jnp.zeros_like(grad_queries_ref)
    for j in range(SPANS):
        key_span = slice(j * SPAN, (j + 1) * SPAN)
        keys, values = keys_ref[key_span], values_ref[key_span]
        grad_keys, grad_values = 0.0, 0.0
        for i in range(j, SPANS):
            span = slice(i * SPAN, (i + 1) * SPAN)
            queries, grad_heads = queries_ref[span], grad_heads_ref[span]
            scores = dot(keys, queries, 1, 1)
            scores = seen(scores) if i == j else scores
            offset = 0.0 if i == j else penalty(segments_ref, i, j)
            probability = jnp.exp(scores - (log_sums_ref[:, span] + offset))
            grad_values += dot(probability.astype(BF), grad_heads)
            grad_probs = dot(values, grad_heads, 1, 1)
            grad_scores = (probability * (grad_probs - products_ref[:, span])).astype(BF)
            grad_keys += dot(grad_scores, queries)
            grad_queries_ref[:, span] += dot(turned_keys_ref[:, key_span], grad_scores)
        grad_keys_ref[key_span] = grad_keys
        grad_values_ref[key_span] = grad_values
    for group in range(SPANS):
        for k in range(PER_SPAN):
            index = group * PER_SPAN + k
            here, place = slice(index * BLOCK, (index + 1) * BLOCK), block_of(blocks_ref[index])
            grad_queries = (grad_queries_ref[:, place] * HD ** (-0.5)).T
            grad_pairs = jnp.concatenate([grad_queries, grad_keys_ref[place, :HD]], axis=1)
            grad_pairs = grad_pairs * cosine_ref[place] - turned(grad_pairs) * sine_ref[place]
            grad_in_ref[here, FF_HERE : FF_HERE + 2 * HD] = grad_pairs.astype(BF)
            grad_in_ref[here, FF_HERE + 2 * HD :] = grad_values_ref[place].astype(BF)
        rows = slice(group * SPAN, (group + 1) * SPAN)
        half_of(half_refs, group)[...] = dot(grad_in_ref[rows], w_in_ref[...]).astype(BF)
    finished(copies[4:])
    raw, after, columns = 0.0, 0.0, 0.0
    ones = jnp.ones((SPAN, BLOCK), BF)
    total = jnp.zeros((1, IN), F32)
    for group in range(SPANS):
        rows = slice(group * SPAN, (group + 1) * SPAN)
        grad_in = grad_in_ref[rows]
        features = features_ref[rows] if separate else stacked(chunk_refs, group, 0)
        raw += dot(grad_in, features, 0, 0)
        columns += dot(grad_in, ones, 0, 0)
        total += jnp.sum(grad_in.astype(F32), axis=0, keepdims=True)
        after += dot(mixed_ref[rows], stacked(chunk_refs, group, first), 0, 0)
    kept = kept_ref[...].astype(F32)
    gain, shift = norm_ref[0:1], norm_ref[1:2]
    column = columns[:, :1]
    grads_ref[:IN] = (raw * gain + column * shift).astype(BF)
    grads_ref[IN : IN + 16] = jnp.zeros((16, 1024), BF)
    grads_ref[IN : IN + 1, :IN] = total.astype(BF)
    grads_ref[IN + 16 : PACKED] = after.astype(BF)
    grads_ref[PACKED:] = jnp.zeros((SUMMED - PACKED, 1024), BF)
    vectors_ref[0:1] = jnp.sum(raw * kept, axis=0, keepdims=True)
    vectors_ref[1:2] = jnp.sum(column * kept, axis=0, keepdims=True)


def pack_kernel(
    up_hbm, qkv_hbm, down_hbm, out_hbm, biases_ref, norms_ref, unused_ref, packed_hbm, up_ref, packed_ref, sems
):
    parts = [
        (qkv_hbm, packed_ref.at[pl.ds(FF_HERE, QKV)]),
        (down_hbm, packed_ref.at[pl.ds(IN + 16, FF_HERE)]),
        (out_hbm, packed_ref.at[pl.ds(IN + 16 + FF_HERE, HD)]),
        (up_hbm, up_ref),
    ]
    copies = [pltpu.make_async_copy(*part, sems.at[k]) for k, part in enumerate(parts)]
    for copy in copies:
        copy.start()
    biases, norms = biases_ref[...], norms_ref[...]
    rows = lax.broadcasted_iota(jnp.int32, (16, 1024), 0)
    small = jnp.zeros((16, 1024), F32)
    for value, high_row, low_row in (
        (biases, 0, 1),
        (norms[0:1], 2, 5),
        (norms[1:2], 3, 6),
        (norms[2:3], 4, 7),
    ):
        high = value.astype(BF).astype(F32)
        small = jnp.where(rows == high_row, high, small)
        small = jnp.where(rows == low_row, value - high, small)
    packed_ref[IN : IN + 16] = small.astype(BF)
    for copy in copies:
        copy.wait()
    packed_ref[:FF_HERE] = up_ref[...].T
    copy = pltpu.make_async_copy(packed_ref, packed_hbm, sems.at[0])
    copy.start()
    copy.wait()


def unpack_kernel(
    flag_ref, first_hbm, second_hbm, w_in_ref, kept_ref, w_out_ref, bias_ref, norm_ref, packed_ref, sem
):
    @pl.when(flag_ref[0] == 1)
    def _():
        copy = pltpu.make_async_copy(first_hbm, packed_ref, sem)
        copy.start()
        copy.wait()

    @pl.when(flag_ref[0] != 1)
    def _():
        copy = pltpu.make_async_copy(second_hbm, packed_ref, sem)
        copy.start()
        copy.wait()

    w_in = packed_ref[:IN]
    small = packed_ref[IN : IN + 16]
    shifts = dot(small, w_in, 1, 1)
    small = small.astype(F32)
    norm_ref[0:3] = small[2:5] + small[5:8]
    bias_ref[...] = small[0:1, :IN] + small[1:2, :IN] + shifts[3:4] + shifts[6:7]
    kept_ref[...] = w_in
    w_in_ref[...] = (w_in.astype(F32) * norm_ref[0:1]).astype(BF)
    w_out_ref[...] = packed_ref[IN + 16 : PACKED]


def split_kernel(place_ref, first_hbm, second_hbm, total_ref, one_ref, three_ref, two_ref, a_ref, b_ref, sems):
    n = SUMMED // 4
    parts = []
    for k, steps in enumerate((0, 1, 3, 2)):
        source = pl.ds(pl.multiple_of(lax.rem(place_ref[0] + steps, 4) * n, 16), n)
        parts.append((first_hbm.at[source], a_ref.at[pl.ds(k * n, n)]))
        parts.append((second_hbm.at[source], b_ref.at[pl.ds(k * n, n)]))
    finished(started(parts, sems, 0))
    for k, ref in enumerate((total_ref, one_ref, three_ref, two_ref)):
        rows = slice(k * n, (k + 1) * n)
        value = a_ref[rows].astype(F32) + b_ref[rows].astype(F32)
        ref[...] = value.astype(ref.dtype)


def finish_kernel(flags_ref, *refs):
    up_ref, qkv_ref, down_ref, out_ref, biases_ref, whole_ref = refs[8:]
    n = SUMMED // 4
    for k in range(4):
        place = lax.rem(flags_ref[1] + 4 - k, 4)
        rows = pl.ds(pl.multiple_of(place * n, 16), n)

        @pl.when(flags_ref[0] == 1)
        def _():
            whole_ref[rows] = refs[k][...]

        @pl.when(flags_ref[0] != 1)
        def _():
            whole_ref[rows] = refs[4 + k][...]

    up_ref[...] = whole_ref[:FF_HERE].astype(F32).T
    qkv_ref[...] = whole_ref[FF_HERE:IN].astype(F32)
    biases_ref[...] = whole_ref[IN : IN + 16].astype(F32)[0:8]
    down_ref[...] = whole_ref[IN + 16 : IN + 16 + FF_HERE].astype(F32)
    out_ref[...] = whole_ref[IN + 16 + FF_HERE : PACKED].astype(F32)


def add_kernel(n_sums, with_vectors, *refs):
    sources, refs = refs[: 2 * n_sums], refs[2 * n_sums :]
    if with_vectors:
        vectors = refs[0][...] + refs[1][...]
        rest = vectors - vectors.astype(BF).astype(F32)
    out_refs = refs[-7 - n_sums - with_vectors :]
    if with_vectors:
        out_refs[-1][...] = vectors
    for k in range(8):
        for n in range(n_sums):
            rows = slice(k * BLOCK, (k + 1) * BLOCK)
            value = sources[2 * n][rows].astype(F32) + sources[2 * n + 1][rows].astype(F32)
            if k == 0:
                out_refs[n][...] = value
            else:
                out_refs[n_sums - 1 + k][n * BLOCK : (n + 1) * BLOCK] = value.astype(BF)
        if k and with_vectors:
            tail = jnp.concatenate([vectors, rest]).astype(BF)
            out_refs[n_sums - 1 + k][n_sums * BLOCK :] = tail


def total_of(total_ref, arrived_refs, first):
    total = total_ref[...]
    for ref in arrived_refs:
        total += ref[first : first + BLOCK].astype(F32)
    return total


def close_forward_kernel(first, total_ref, *refs):
    rows_ref, norm_ref, result_ref, rounded_ref, scaled_ref = refs[7:]
    total = total_of(total_ref, refs[:7], first)
    result = rows_ref[...].astype(F32) + total + norm_ref[2:3]
    result_ref[...] = result
    rounded = result.astype(BF)
    rounded_ref[...] = rounded
    scaled_ref[...] = normalize(rounded.astype(F32))[0].astype(BF)


def close_backward_kernel(first, total_ref, *refs):
    rows_ref, grad_rows_ref, grad_ref, rounded_ref = refs[7:]
    total = total_of(total_ref, refs[:7], first)
    grad = normalize_back(grad_rows_ref[...], total, rows_ref[...])
    grad_ref[...] = grad
    rounded_ref[...] = grad.astype(BF)


def vectors_kernel(total_ref, *refs):
    total = total_ref[...]
    for ref in refs[:7]:
        total += ref[BLOCK : BLOCK + 8].astype(F32) + ref[BLOCK + 8 :].astype(F32)
    refs[7][...] = total


def gate_kernel(*refs):
    pass


WHOLE = pl.BlockSpec(memory_space=pltpu.VMEM)
SCALARS = pl.BlockSpec(memory_space=pltpu.SMEM)
FAR = pl.BlockSpec(memory_space=pl.ANY)


def limit(size):
    return pltpu.CompilerParams(vmem_limit_bytes=size * 2**20)


SMALL = limit(12)
HALF = jax.ShapeDtypeStruct((ROWS // 2, 1024), BF)
SAVED = [
    jax.ShapeDtypeStruct((ROWS, width), BF) for width in (OUT, FF_HERE, 2 * HD, HD, 1024)
]


def like(shapes):
    return [pltpu.VMEM(shape.shape, shape.dtype) for shape in shapes]


def forward(chunks, layer, place, save_features):
    saved = SAVED if save_features else SAVED[:4]
    outs = pl.pallas_call(
        forward_kernel,
        out_shape=[HALF] * 2 + [jax.ShapeDtypeStruct((1, ROWS), F32)] + saved,
        in_specs=[SCALARS] * 2 + [WHOLE] * 21,
        out_specs=[WHOLE] * 3 + [FAR] * len(saved),
        scratch_shapes=like(SAVED[:4])
        + [
            pltpu.VMEM((ROWS, 2 * HD), BF),
            pltpu.VMEM((ROWS, 2 * HD), BF),
            pltpu.VMEM((HD, ROWS), BF),
            pltpu.VMEM((ROWS, HD), BF),
            pltpu.SemaphoreType.DMA((20,)),
        ],
        compiler_params=limit(F_LIMIT),
        cost_estimate=pl.CostEstimate(
            flops=12 * 10**9, bytes_accessed=2**24, transcendentals=ROWS * ROWS
        ),
        name="forward",
    )(
        place["blocks"],
        place["segments"],
        *chunks,
        layer["w_in"],
        layer["bias_in"],
        layer["w_out"],
        place["cosine"],
        place["sine"],
    )
    return outs[:2], outs[2:]


def backward(chunks, layer, saved, place, *earlier):
    saved_shapes = SAVED[: len(saved) - 1]
    separate = len(saved) == 6
    return pl.pallas_call(
        functools.partial(backward_kernel, separate, len(earlier)),
        out_shape=[HALF] * 2
        + [
            jax.ShapeDtypeStruct((SUMMED, 1024), BF),
            jax.ShapeDtypeStruct((2, 1024), F32),
        ],
        in_specs=[SCALARS] * 2
        + [WHOLE] * 23
        + [FAR] * (len(saved_shapes) + len(earlier)),
        out_specs=[WHOLE] * 4,
        scratch_shapes=like(saved_shapes)
        + [
            pltpu.VMEM((ROWS, IN), BF),
            pltpu.VMEM((ROWS, 2 * HD), BF),
            pltpu.VMEM((ROWS, 2 * HD), BF),
            pltpu.VMEM((HD, ROWS), BF),
            pltpu.VMEM((ROWS, HD), BF),
            pltpu.VMEM((1, ROWS), F32),
            pltpu.VMEM((HD, ROWS), F32),
            pltpu.VMEM((ROWS, 2 * HD), F32),
            pltpu.VMEM((ROWS, HD), F32),
            pltpu.SemaphoreType.DMA((5,)),
        ],
        compiler_params=limit(B_LIMIT),
        cost_estimate=pl.CostEstimate(
            flops=18 * 10**9, bytes_accessed=2**24, transcendentals=ROWS * ROWS
        ),
        name="backward",
    )(
        place["blocks"],
        place["segments"],
        *chunks,
        layer["w_in"],
        layer["w_out"],
        layer["kept"],
        layer["norm"],
        saved[0],
        place["cosine"],
        place["sine"],
        *saved[1:],
        *earlier,
    )


def pack(weights, biases, norms, earlier):
    return pl.pallas_call(
        pack_kernel,
        out_shape=jax.ShapeDtypeStruct((PACKED, 1024), BF),
        in_specs=[FAR] * 4 + [WHOLE] * 2 + [FAR],
        out_specs=FAR,
        scratch_shapes=[
            pltpu.VMEM((1024, FF_HERE), BF),
            pltpu.VMEM((PACKED, 1024), BF),
            pltpu.SemaphoreType.DMA((4,)),
        ],
        compiler_params=limit(56),
        name="pack",
    )(*weights, biases, norms, earlier)


def unpack(flag, first, second):
    w_in, kept, w_out, bias_in, norm = pl.pallas_call(
        unpack_kernel,
        out_shape=[
            jax.ShapeDtypeStruct((IN, 1024), BF),
            jax.ShapeDtypeStruct((IN, 1024), BF),
            jax.ShapeDtypeStruct((OUT, 1024), BF),
            jax.ShapeDtypeStruct((1, IN), F32),
            jax.ShapeDtypeStruct((3, 1024), F32),
        ],
        in_specs=[SCALARS] + [FAR] * 2,
        out_specs=[WHOLE] * 5,
        scratch_shapes=[pltpu.VMEM((PACKED, 1024), BF), pltpu.SemaphoreType.DMA],
        compiler_params=limit(16),
        name="unpack",
    )(flag, first, second)
    return {"w_in": w_in, "kept": kept, "w_out": w_out, "bias_in": bias_in, "norm": norm}


def split(place, first, second):
    n = SUMMED // 4
    return pl.pallas_call(
        split_kernel,
        out_shape=[jax.ShapeDtypeStruct((n, 1024), kind) for kind in (F32, BF, BF, BF)],
        in_specs=[SCALARS] + [FAR] * 2,
        out_specs=[WHOLE] * 4,
        scratch_shapes=[pltpu.VMEM((SUMMED, 1024), BF)] * 2 + [pltpu.SemaphoreType.DMA((8,))],
        compiler_params=SMALL,
        name="split",
    )(place, first, second)


def finish(flags, quarters):
    return pl.pallas_call(
        finish_kernel,
        out_shape=[
            jax.ShapeDtypeStruct((1024, FF_HERE), F32),
            jax.ShapeDtypeStruct((QKV, 1024), F32),
            jax.ShapeDtypeStruct((FF_HERE, 1024), F32),
            jax.ShapeDtypeStruct((HD, 1024), F32),
            jax.ShapeDtypeStruct((8, 1024), F32),
        ],
        in_specs=[SCALARS] + [WHOLE] * 8,
        out_specs=[WHOLE] * 5,
        scratch_shapes=[pltpu.VMEM((SUMMED, 1024), BF)],
        compiler_params=limit(16),
        name="finish",
    )(flags, *quarters)


def gate(values, *earlier):
    n = len(values)
    return pl.pallas_call(
        gate_kernel,
        out_shape=[jax.ShapeDtypeStruct(value.shape, value.dtype) for value in values],
        in_specs=[FAR] * (n + len(earlier)),
        out_specs=[FAR] * n,
        input_output_aliases={k: k for k in range(n)},
        name="gate",
    )(*values, *earlier)


def add(halves, others, *earlier, vectors=()):
    count = len(halves)
    rows = count * BLOCK + 16 * bool(vectors)
    sources = [value for pair in zip(halves, others) for value in pair]
    return pl.pallas_call(
        functools.partial(add_kernel, count, bool(vectors)),
        out_shape=[jax.ShapeDtypeStruct((BLOCK, 1024), F32)] * count
        + [jax.ShapeDtypeStruct((rows, 1024), BF)] * 7
        + [jax.ShapeDtypeStruct((8, 1024), F32)] * bool(vectors),
        in_specs=[WHOLE] * (2 * count + len(vectors)) + [FAR] * len(earlier),
        out_specs=[WHOLE] * (count + 7 + bool(vectors)),
        compiler_params=SMALL,
        name="add",
    )(*sources, *vectors, *earlier)


def close_forward(total, arrived, first, rows, norm):
    shape = (BLOCK, 1024)
    return pl.pallas_call(
        functools.partial(close_forward_kernel, first),
        out_shape=[
            jax.ShapeDtypeStruct(shape, F32),
            jax.ShapeDtypeStruct(shape, BF),
            jax.ShapeDtypeStruct(shape, BF),
        ],
        in_specs=[WHOLE] * 10,
        out_specs=[WHOLE] * 3,
        compiler_params=SMALL,
        name="close_forward",
    )(total, *arrived, rows, norm)


def close_backward(total, arrived, first, rows, grad_rows):
    shape = (BLOCK, 1024)
    return pl.pallas_call(
        functools.partial(close_backward_kernel, first),
        out_shape=[jax.ShapeDtypeStruct(shape, F32), jax.ShapeDtypeStruct(shape, BF)],
        in_specs=[WHOLE] * 10,
        out_specs=[WHOLE] * 2,
        compiler_params=SMALL,
        name="close_backward",
    )(total, *arrived, rows, grad_rows)


def sum_vectors(total, arrived):
    return pl.pallas_call(
        vectors_kernel,
        out_shape=jax.ShapeDtypeStruct((8, 1024), F32),
        in_specs=[WHOLE] * 8,
        out_specs=WHOLE,
        compiler_params=SMALL,
        name="sum_vectors",
    )(total, *arrived)


def gate(values, *earlier):
    n = len(values)
    return pl.pallas_call(
        gate_kernel,
        out_shape=[jax.ShapeDtypeStruct(value.shape, value.dtype) for value in values],
        in_specs=[FAR] * (n + len(earlier)),
        out_specs=[FAR] * n,
        input_output_aliases={k: k for k in range(n)},
        name="gate",
    )(*values, *earlier)


def rotary_lanes(starts):
    lane = jnp.arange(2 * HD, dtype=jnp.int32) % HD
    inverse = jnp.power(10000.0, -2.0 * (lane % (ROT // 2)).astype(F32) / ROT)
    inverse = jnp.where(lane < ROT, inverse, 0.0)[None, :]
    coarse = (jnp.arange(0, ROWS, 64, dtype=jnp.int32) - starts[::64]).astype(F32)[:, None] * inverse
    fine = jnp.arange(64, dtype=jnp.int32).astype(F32)[:, None] * inverse
    cos_a, sin_a = jnp.cos(coarse)[:, None, :], jnp.sin(coarse)[:, None, :]
    cos_b, sin_b = jnp.cos(fine)[None], jnp.sin(fine)[None]
    shape = (ROWS, 2 * HD)
    return (
        (cos_a * cos_b - sin_a * sin_b).reshape(shape),
        (sin_a * cos_b + cos_a * sin_b).reshape(shape),
    )


def ring_sum(value):
    pieces = [
        lax.ppermute(value, "dp", [(i, (i + steps) % 4) for i in range(4)]) for steps in (1, 3, 2)
    ]
    return value + pieces[0] + pieces[1] + pieces[2]


def quarters_over_dp(first, second, core):
    def move(part, steps):
        pairs = [(core * 4 + i, core * 4 + (i + steps) % 4) for i in range(4)]
        return lax.ppermute(part, ("pipe", "dp"), pairs)

    total, *parts = split(lax.axis_index("dp").astype(jnp.int32)[None], first, second)
    for part, steps in zip(parts, (1, 3, 2)):
        total += move(part, steps).astype(F32)
    total = total.astype(BF)
    return total, [move(total, steps) for steps in (1, 2, 3)]


def body(
    inputs,
    seq_lengths,
    cotangent,
    ln_gain,
    ln_bias,
    w_qkv,
    b_qkv,
    w_out,
    b_out,
    w_up,
    b_up,
    w_down,
    b_down,
):
    core, z, y = (lax.axis_index(name) for name in DEVICES)
    on_first = core == 0
    micro = jnp.where((y == 0) | (y == 3), 0, 1)
    on_micro_0 = micro == 0
    sent = jnp.where(on_first, micro, 1 - micro)

    def pick(value, index):
        return lax.dynamic_index_in_dim(value, index, 0, keepdims=False)

    weights = (w_up[0], w_qkv.reshape(1024, QKV).T, w_down[0], w_out[0])
    biases = jnp.concatenate([b_up, b_qkv[0].reshape(1, QKV), jnp.zeros((1, 1024 - IN), F32)], 1)
    norms = jnp.concatenate([ln_gain, ln_bias, b_out + b_down])
    mine = pack(weights, biases, norms, inputs)
    swapped = send(mine, SWAP)

    (sent_rows,) = gate([pick(inputs, sent)], mine)
    scaled_rows = normalize(sent_rows.astype(F32))[0].astype(BF)
    chunks_0 = gather_arguments(scaled_rows, on_first)

    flag = jnp.where(on_first, 1, 0).astype(jnp.int32)
    layer_0 = unpack(flag[None], mine, swapped)

    later_rows, later_grads = gate([sent_rows, pick(cotangent, sent)], chunks_0[1])
    rows_0 = jnp.where(on_first, later_rows, send(later_rows, OVER))
    grad_rows_1 = jnp.where(on_first, later_grads, send(later_grads, OVER))
    starts = start_rows(pick(seq_lengths, micro), ROWS)
    cosine, sine = rotary_lanes(starts)
    place = {
        "blocks": gathered_blocks(core, z, y),
        "segments": (starts[::SPAN] // SPAN).astype(jnp.int32),
        "cosine": cosine,
        "sine": sine,
    }

    halves_0, saved_0 = forward(chunks_0, layer_0, place, True)
    total, *blocks = add([halves_0[0]], [send(halves_0[1], SIBLING)])
    arrived = scatter(blocks)
    over = send(pack(weights, biases, norms, arrived[0]), OVER)
    layer_1 = unpack(flag[None], swapped, over)
    result_0, rows_1, scaled_rows = close_forward(total, arrived, 0, rows_0, layer_0["norm"])
    chunks_1 = gather(jnp.concatenate([scaled_rows, grad_rows_1]))
    halves_1, saved_1 = forward(chunks_1, layer_1, place, False)

    result_0_there = send(result_0, BACK_OVER)
    *grad_halves_1, grads_1, vectors_1 = backward(
        chunks_1, layer_1, saved_1, place, result_0_there
    )
    others = [send(half, SIBLING) for half in (halves_1[1], grad_halves_1[1])]
    total_1, total, *blocks = add([halves_1[0], grad_halves_1[0]], others)
    arrived = scatter(blocks)
    grad_input_1, grad_rows_0 = close_backward(total, arrived, BLOCK, rows_1, grad_rows_1)
    grad_chunks_0 = gather(grad_rows_0)
    result_1, unused_rounded, unused_rows = close_forward(
        total_1, arrived, 0, rows_1, layer_1["norm"]
    )
    mine_1, quarters_1 = quarters_over_dp(send(grads_1, SIBLING), send(grads_1, OVER), 1)
    result_1_here = send(result_1, SIBLING)
    result_1_there = send(result_1, OVER)
    grad_input_1_here = send(grad_input_1, SIBLING)
    grad_input_1_there = send(grad_input_1, OVER)

    *grad_halves_0, grads_0, vectors_0 = backward(
        grad_chunks_0,
        layer_0,
        saved_0,
        place,
        mine_1,
        result_1_here,
        result_1_there,
        grad_input_1_here,
        grad_input_1_there,
    )
    vectors = jnp.concatenate(
        [
            vectors_0,
            jnp.sum(grad_rows_0.astype(F32), axis=0)[None],
            vectors_1,
            jnp.sum(grad_rows_1.astype(F32), axis=0)[None],
            jnp.zeros((2, 1024), F32),
        ]
    )
    total, *blocks, vectors = add(
        [grad_halves_0[0]],
        [send(grad_halves_0[1], SIBLING)],
        *quarters_1,
        vectors=(vectors, send(vectors, SIBLING)),
    )
    arrived = scatter(blocks)
    grad_input_0, unused_rounded = close_backward(total, arrived, 0, rows_0, grad_rows_0)
    mine_0, quarters_0 = quarters_over_dp(grads_0, send(grads_0, BACK_OVER), 0)
    flags = jnp.stack([flag, lax.axis_index("dp")]).astype(jnp.int32)
    grad_up, grad_qkv, grad_down, grad_out, grad_biases = finish(
        flags, [mine_0] + quarters_0 + [mine_1] + quarters_1
    )
    vectors = sum_vectors(vectors, arrived)
    vectors = ring_sum(vectors + send(vectors, table(step(0, 1))))
    vectors = jnp.where(on_first, vectors[:3], vectors[3:6])

    def output_of(value_0, there_0, here_1, there_1):
        here = jnp.where(on_first, value_0, here_1)
        there = jnp.where(on_first, there_0, there_1)
        return jnp.stack(
            [jnp.where(on_micro_0, here, there), jnp.where(on_micro_0, there, here)]
        )[None]

    return (
        output_of(result_0, result_0_there, result_1_here, result_1_there),
        output_of(
            grad_input_0,
            send(grad_input_0, BACK_OVER),
            grad_input_1_here,
            grad_input_1_there,
        ),
        vectors[0:1],
        vectors[1:2],
        grad_qkv.T.reshape(1, 1024, 1, QKV),
        grad_biases[0, FF_HERE:IN].reshape(1, 1, QKV),
        grad_out[None],
        vectors[2:3],
        grad_up[None],
        grad_biases[0:1, :FF_HERE],
        grad_down[None],
        vectors[2:3],
    )


def solution(mesh):
    rows = P("dp", ("z", "y"), None)
    layer_rows = P("pipe", "dp", ("z", "y"), None)
    heads = P("pipe", None, ("z", "y"), None)
    split = P("pipe", ("z", "y"), None)
    units = P("pipe", None, ("z", "y"))
    whole = P("pipe", None)
    unit_bias = P("pipe", ("z", "y"))
    return jax.shard_map(
        body,
        mesh=Mesh(mesh.devices.reshape(2, 4, 4, 4), ("pipe", "dp", "z", "y")),
        in_specs=(
            rows,
            P("dp", None),
            rows,
            whole,
            whole,
            heads,
            split,
            split,
            whole,
            units,
            unit_bias,
            split,
            whole,
        ),
        out_specs=(
            layer_rows,
            layer_rows,
            whole,
            whole,
            heads,
            split,
            split,
            whole,
            units,
            unit_bias,
            split,
            whole,
        ),
        check_vma=False,
    )
```

```python
import functools

import jax
import jax.numpy as jnp
from jax import lax
from jax.experimental import pallas as pl
from jax.experimental.pallas import tpu as pltpu
from jax.sharding import Mesh, PartitionSpec as P

HD = 64
ROT = 16
FF_HERE = 256
QKV = 3 * HD
IN = FF_HERE + QKV
OUT = FF_HERE + HD
PACKED = IN + 16 + OUT
SUMMED = 832
MIXED = 384
F_LIMIT = 14
B_LIMIT = 23
PACK_LIMIT = 56
ROWS = 2048
BLOCK = 128
SPAN = 512
SPANS = ROWS // SPAN
PER_SPAN = SPAN // BLOCK
EPSILON = 1e-05
NEGATIVE = -1e30
ROOT_HALF = 0.7071067811865476
INV_ROOT_TAU = 0.3989422804014327
DEVICES = ("pipe", "z", "y")
BF = jnp.bfloat16
F32 = jnp.float32


def table(rule):
    pairs = []
    for core in range(2):
        for z in range(4):
            for y in range(4):
                target = rule(core, z, y)
                if target is not None:
                    to_core, to_z, to_y = target
                    pairs.append((core * 16 + z * 4 + y, to_core * 16 + to_z % 4 * 4 + to_y))
    return pairs


def by_core(first, second):
    return table(lambda core, z, y: (first if core == 0 else second)(core, z, y))


def step(steps, flip=0):
    return lambda core, z, y: (core, z + steps, y ^ flip)


def nowhere(core, z, y):
    return None


PAIR = 3
SIBLING = table(lambda core, z, y: (1 - core, z, y))
OVER = by_core(nowhere, step(0, 1))
BACK_OVER = by_core(nowhere, lambda core, z, y: (0, z, y ^ 1))
SWAP = by_core(lambda core, z, y: (1, z, y ^ 1), lambda core, z, y: (0, z, y))
RING = (1, -1, 2)


def send(value, pairs):
    return lax.ppermute(value, DEVICES, pairs)


def gathered_blocks(core, z, y):
    def of(own):
        columns = (y ^ own, y ^ own ^ PAIR)
        steps = [0] + [-hops for hops in RING]
        return [(z + hops) % 4 * 4 + column for column in columns for hops in steps]

    first, second = jnp.stack(of(0)), jnp.stack(of(1))
    return jnp.where(
        core == 0, jnp.concatenate([first, second]), jnp.concatenate([second, first])
    ).astype(jnp.int32)


def with_sibling(blocks):
    return blocks + [send(block, SIBLING) for block in blocks]


def gather(rows):
    pair = send(rows, table(step(0, PAIR)))
    own = [send(rows, table(step(hops))) for hops in RING]
    far = [send(pair, table(step(hops))) for hops in RING]
    return with_sibling([rows] + own + [pair] + far)


def from_arguments(rows, on_first):
    near = send(rows, by_core(step(0, PAIR), step(0, 1)))
    beside = send(rows, by_core(nowhere, step(0, 2)))
    return jnp.concatenate([jnp.where(on_first, rows, near), jnp.where(on_first, near, beside)])


def gather_pieces(both):
    return with_sibling([both] + [send(both, table(step(hops))) for hops in RING])


def scatter(blocks):
    steps = [(-hops, 0) for hops in RING] + [(0, PAIR)] + [(-hops, PAIR) for hops in RING]
    return [send(block, table(step(hops, flip))) for block, (hops, flip) in zip(blocks, steps)]


def scatter_pieces(pieces):
    return [send(piece, table(step(-hops))) for piece, hops in zip(pieces, RING)]


def start_rows(lengths, total_rows):
    endings = jnp.cumsum(lengths)
    places = jnp.arange(total_rows, dtype=jnp.int32)
    passed = places[:, None] >= endings[None, :]
    return jnp.sum(jnp.where(passed, lengths[None, :], 0), axis=1)


def normalize(rows):
    average = jnp.mean(rows, axis=-1, keepdims=True)
    centred = rows - average
    inverse_std = lax.rsqrt(jnp.mean(centred * centred, axis=-1, keepdims=True) + EPSILON)
    return centred * inverse_std, inverse_std


def normalize_back(grad_rows, grad_scaled, rows):
    scaled, inverse_std = normalize(rows.astype(F32))
    return grad_rows.astype(F32) + inverse_std * (
        grad_scaled
        - jnp.mean(grad_scaled, axis=-1, keepdims=True)
        - scaled * jnp.mean(grad_scaled * scaled, axis=-1, keepdims=True)
    )


def block_of(index):
    return pl.ds(pl.multiple_of(index * BLOCK, BLOCK), BLOCK)


def dot(left, right, left_axis=1, right_axis=0):
    return lax.dot_general(
        left, right, (((left_axis,), (right_axis,)), ((), ())), preferred_element_type=F32
    )


def started(parts, sems, first):
    copies = [pltpu.make_async_copy(*part, sems.at[first + k]) for k, part in enumerate(parts)]
    for copy in copies:
        copy.start()
    return copies


def finished(copies):
    for copy in copies:
        copy.wait()


def stacked(refs, group, first):
    return jnp.concatenate(
        [refs[group * PER_SPAN + k][first : first + BLOCK] for k in range(PER_SPAN)]
    )


def chunk_of(refs, group):
    if len(refs) == 16:
        return stacked(refs, group, 0)
    pieces = refs[group // 2 * PER_SPAN : (group // 2 + 1) * PER_SPAN]
    return stacked(pieces, 0, group % 2 * BLOCK)


def half_of(refs, group):
    place = group % (SPANS // 2) * SPAN
    return refs[group // (SPANS // 2)].at[pl.ds(place, SPAN)]


def turned(pairs):
    lane = lax.broadcasted_iota(jnp.int32, pairs.shape, 1) % HD
    return jnp.where(
        lane < ROT // 2, -pltpu.roll(pairs, 2 * HD - ROT // 2, 1), pltpu.roll(pairs, ROT // 2, 1)
    )


def halves(pairs):
    lane = lax.broadcasted_iota(jnp.int32, pairs.shape, 1)
    queries = jnp.where(lane < HD, pairs * HD ** (-0.5), 0.0)
    return queries.astype(BF), pltpu.roll(pairs, HD, 1).astype(BF)


def penalty(scalars_ref, query_span, key_span):
    return jnp.where(key_span >= scalars_ref[16 + query_span], 0.0, -NEGATIVE).astype(F32)


def seen(scores):
    keys = lax.broadcasted_iota(jnp.int32, scores.shape, 0)
    queries = lax.broadcasted_iota(jnp.int32, scores.shape, 1)
    return jnp.where(keys <= queries, scores, NEGATIVE)


def store_parts(store_ref, saved_refs):
    lanes = (0, MIXED, MIXED + FF_HERE, MIXED + FF_HERE + 2 * HD)
    places = [
        store_ref.at[pl.ds(ROWS, ROWS), pl.ds(lane, ref.shape[1])]
        for lane, ref in zip(lanes, saved_refs)
    ]
    return places + [store_ref.at[pl.ds(0, ROWS)]]


def forward_kernel(n_chunks, stored, *refs):
    scalars_ref = refs[0]
    chunk_refs, refs = refs[1 : 1 + n_chunks], refs[1 + n_chunks :]
    w_in_ref, bias_ref, w_out_ref, cosine_ref, sine_ref = refs[:5]
    half_refs, log_sums_ref, refs = refs[5:7], refs[7], refs[8:]
    kept_hbm, kept_refs, refs = refs[:-9], refs[-9:-5], refs[-5:]
    mixed_ref, slope_ref, pairs_ref, values_ref = kept_refs
    queries_ref, keys_ref, turned_values_ref, ordered_ref, sems = refs
    copies = []
    if stored:
        kept_hbm = store_parts(kept_hbm[0], kept_refs)
        parts = []
        for k in range(16):
            source = chunk_refs[k // 8 * 4 + k % 4].at[pl.ds(k % 8 // 4 * BLOCK, BLOCK)]
            parts.append((source, kept_hbm[4].at[pl.ds(k * BLOCK, BLOCK)]))
        copies = started(parts, sems, 0)
    for group in range(SPANS):
        rows = slice(group * SPAN, (group + 1) * SPAN)
        projected = dot(chunk_of(chunk_refs, group), w_in_ref[...], 1, 1) + bias_ref[...]
        inner = projected[:, :FF_HERE]
        wave = 1.0 + lax.erf(inner * ROOT_HALF)
        mixed_ref[rows, :FF_HERE] = (0.5 * inner * wave).astype(BF)
        slope = 0.5 * wave + inner * jnp.exp(-0.5 * inner * inner) * INV_ROOT_TAU
        slope_ref[rows] = slope.astype(BF)
        for k in range(PER_SPAN):
            joined = projected[k * BLOCK : (k + 1) * BLOCK, FF_HERE:]
            place = block_of(scalars_ref[group * PER_SPAN + k])
            pairs = joined[:, : 2 * HD]
            pairs = pairs * cosine_ref[place] + turned(pairs) * sine_ref[place]
            pairs_ref[place] = pairs.astype(BF)
            queries_ref[place], keys_ref[place] = halves(pairs.astype(BF).astype(F32))
            values = joined[:, 2 * HD :]
            values_ref[place, :HD] = values.astype(BF)
            turned_values_ref[:, place] = values.T.astype(BF)
    for i in range(SPANS):
        span = slice(i * SPAN, (i + 1) * SPAN)
        queries = queries_ref[span]
        scores, offsets, highest = [], [], None
        for j in range(i + 1):
            block = dot(keys_ref[j * SPAN : (j + 1) * SPAN], queries, 1, 1)
            block = seen(block) if i == j else block
            offset = 0.0 if i == j else penalty(scalars_ref, i, j)
            top = jnp.max(block, axis=0, keepdims=True) - offset
            highest = top if highest is None else jnp.maximum(highest, top)
            scores.append(block)
            offsets.append(offset)
        total, summed = 0.0, 0.0
        for j in range(i + 1):
            exponent = jnp.exp(scores[j] - (highest + offsets[j]))
            total = total + jnp.sum(exponent, axis=0, keepdims=True)
            summed = summed + dot(
                turned_values_ref[:, j * SPAN : (j + 1) * SPAN], exponent.astype(BF)
            )
        log_sums_ref[:, span] = highest + jnp.log(total)
        ordered_ref[span] = (summed / total).T.astype(BF)
    for group in range(SPANS):
        for k in range(PER_SPAN):
            index = group * PER_SPAN + k
            here = slice(index * BLOCK, (index + 1) * BLOCK)
            mixed_ref[here, FF_HERE:OUT] = ordered_ref[block_of(scalars_ref[index])]
        rows = slice(group * SPAN, (group + 1) * SPAN)
        half_of(half_refs, group)[...] = dot(mixed_ref[rows, :OUT], w_out_ref[...]).astype(BF)
    copies += started(list(zip(kept_refs, kept_hbm)), sems, 16)
    finished(copies)


def backward_kernel(separate, n_earlier, *refs):
    scalars_ref = refs[0]
    count = 16 if separate else 8
    chunk_refs, refs = refs[1 : 1 + count], refs[1 + count :]
    feature_refs, given_ref = [], None
    if separate:
        given_ref, refs = refs[0], refs[1:]
    else:
        feature_refs, refs = refs[:16], refs[16:]

    w_in_ref, w_out_ref, kept_ref, norm_ref, log_sums_ref, cosine_ref, sine_ref = refs[:7]
    count = 5 if separate else 4
    n_saved = 1 if separate else 4
    saved_hbm, refs = refs[7 : 7 + n_saved], refs[7 + n_saved + n_earlier :]
    half_refs, quarter_refs, vectors_ref, refs = refs[:2], refs[2:6], refs[6], refs[7:]
    saved_refs, refs = refs[:count], refs[count:]
    mixed_ref, slope_ref, pairs_ref, values_ref = saved_refs[:4]
    features_ref = saved_refs[-1]
    grad_in_ref, queries_ref, keys_ref, turned_keys_ref, grad_heads_ref, products_ref = refs[:6]
    grad_queries_ref, grad_keys_ref, grad_values_ref, grads_ref, sems = refs[6:]
    if separate:
        saved_hbm = store_parts(saved_hbm[0], saved_refs[:4])
    copies = started(list(zip(saved_hbm, saved_refs)), sems, 0)
    finished(copies[:4])
    for group in range(SPANS):
        rows = slice(group * SPAN, (group + 1) * SPAN)
        grad_mixed = dot(chunk_of(chunk_refs, group), w_out_ref[...], 1, 1)
        grad_in_ref[rows, :FF_HERE] = (
            grad_mixed[:, :FF_HERE] * slope_ref[rows].astype(F32)
        ).astype(BF)
        for k in range(PER_SPAN):
            index = group * PER_SPAN + k
            here, place = slice(index * BLOCK, (index + 1) * BLOCK), block_of(scalars_ref[index])
            grad_heads = grad_mixed[k * BLOCK : (k + 1) * BLOCK, FF_HERE:].astype(BF)
            grad_heads_ref[place] = grad_heads
            product = grad_heads.astype(F32) * mixed_ref[here, FF_HERE:OUT].astype(F32)
            products_ref[:, place] = jnp.sum(product.T, axis=0, keepdims=True)
            queries_ref[here], keys = halves(pairs_ref[here].astype(F32))
            keys_ref[here] = keys
            turned_keys_ref[:, here] = keys[:, :HD].astype(F32).T.astype(BF)
    grad_queries_ref[...] = jnp.zeros_like(grad_queries_ref)
    for j in range(SPANS):
        key_span = slice(j * SPAN, (j + 1) * SPAN)
        keys, values = keys_ref[key_span], values_ref[key_span, :HD]
        grad_keys, grad_values = 0.0, 0.0
        for i in range(j, SPANS):
            span = slice(i * SPAN, (i + 1) * SPAN)
            queries, grad_heads = queries_ref[span], grad_heads_ref[span]
            scores = dot(keys, queries, 1, 1)
            scores = seen(scores) if i == j else scores
            offset = 0.0 if i == j else penalty(scalars_ref, i, j)
            probability = jnp.exp(scores - (log_sums_ref[:, span] + offset))
            grad_values += dot(probability.astype(BF), grad_heads)
            grad_probs = dot(values, grad_heads, 1, 1)
            grad_scores = (probability * (grad_probs - products_ref[:, span])).astype(BF)
            grad_keys += dot(grad_scores, queries)
            grad_queries_ref[:, span] += dot(turned_keys_ref[:, key_span], grad_scores)
        grad_keys_ref[key_span] = grad_keys
        grad_values_ref[key_span] = grad_values
    for group in range(SPANS):
        for k in range(PER_SPAN):
            index = group * PER_SPAN + k
            here, place = slice(index * BLOCK, (index + 1) * BLOCK), block_of(scalars_ref[index])
            grad_queries = (grad_queries_ref[:, place] * HD ** (-0.5)).T
            grad_pairs = jnp.concatenate([grad_queries, grad_keys_ref[place, :HD]], axis=1)
            grad_pairs = grad_pairs * cosine_ref[place] - turned(grad_pairs) * sine_ref[place]
            grad_in_ref[here, FF_HERE : FF_HERE + 2 * HD] = grad_pairs.astype(BF)
            grad_in_ref[here, FF_HERE + 2 * HD :] = grad_values_ref[place].astype(BF)
        rows = slice(group * SPAN, (group + 1) * SPAN)
        half_of(half_refs, group)[...] = dot(grad_in_ref[rows], w_in_ref[...]).astype(BF)
    finished(copies[4:])
    raw, after, columns = 0.0, 0.0, 0.0
    ones = jnp.ones((SPAN, BLOCK), BF)
    total = jnp.zeros((1, IN), F32)
    for group in range(SPANS):
        rows = slice(group * SPAN, (group + 1) * SPAN)
        grad_in = grad_in_ref[rows]
        features = features_ref[rows] if separate else stacked(feature_refs, group, 0)
        raw += dot(grad_in, features, 0, 0)
        columns += dot(grad_in, ones, 0, 0)
        total += jnp.sum(grad_in.astype(F32), axis=0, keepdims=True)
        after += dot(mixed_ref[rows, :OUT], chunk_of(chunk_refs, group), 0, 0)
    kept = kept_ref[...].astype(F32)
    gain, shift = norm_ref[0:1], norm_ref[1:2]
    column = columns[:, :1]
    grads_ref[:IN] = (raw * gain + column * shift).astype(BF)
    grads_ref[IN : IN + 16] = jnp.zeros((16, 1024), BF)
    grads_ref[IN : IN + 1, :IN] = total.astype(BF)
    grads_ref[IN + 16 : PACKED] = after.astype(BF)
    grads_ref[PACKED:] = jnp.zeros((SUMMED - PACKED, 1024), BF)
    n = SUMMED // 4
    for ref, steps in zip(quarter_refs, (0, 1, 3, 2)):
        ref[...] = grads_ref[pl.ds(pl.multiple_of(lax.rem(scalars_ref[20] + steps, 4) * n, 16), n)]
    grad_gain = jnp.sum(raw * kept, axis=0, keepdims=True)
    grad_shift = jnp.sum(column * kept, axis=0, keepdims=True)
    if not separate:
        vectors_ref[0:1] = grad_gain
        vectors_ref[1:2] = grad_shift
        return
    row = lax.broadcasted_iota(jnp.int32, (8, 1024), 0)
    vectors = jnp.where(row == 0, grad_gain, jnp.where(row == 1, grad_shift, given_ref[...]))
    high = vectors.astype(BF).astype(F32)
    vectors = jnp.concatenate([high, vectors - high]).astype(BF)
    for ref in half_refs:
        ref[ROWS // 2 :] = vectors


def pack_kernel(*refs):
    up_hbm, qkv_hbm, down_hbm, out_hbm, b_up_ref, b_qkv_ref, gain_ref, shift_ref = refs[:8]
    b_out_ref, b_down_ref, unused_ref, *packed_hbm, up_ref, packed_ref, sems = refs[8:]
    parts = [
        (up_hbm, up_ref),
        (qkv_hbm, packed_ref.at[pl.ds(FF_HERE, QKV)]),
        (down_hbm, packed_ref.at[pl.ds(IN + 16, FF_HERE)]),
        (out_hbm, packed_ref.at[pl.ds(IN + 16 + FF_HERE, HD)]),
    ]
    copies = started(parts, sems, 0)
    biases = jnp.concatenate(
        [b_up_ref[...], b_qkv_ref[...], jnp.zeros((1, 1024 - IN), F32)], axis=1
    )
    rows = lax.broadcasted_iota(jnp.int32, (16, 1024), 0)
    small = jnp.zeros((16, 1024), F32)
    for value, high_row, low_row in (
        (biases, 0, 1),
        (gain_ref[...], 2, 5),
        (shift_ref[...], 3, 6),
        (b_out_ref[...] + b_down_ref[...], 4, 7),
    ):
        high = value.astype(BF).astype(F32)
        small = jnp.where(rows == high_row, high, small)
        small = jnp.where(rows == low_row, value - high, small)
    packed_ref[IN : IN + 16] = small.astype(BF)
    copies[0].wait()
    packed_ref[:FF_HERE] = up_ref[...].T
    finished(copies[1:])
    finished(started([(packed_ref, target) for target in packed_hbm], sems, 0))


def unpack_kernel(
    flag_ref, first_hbm, second_hbm, w_in_ref, kept_ref, w_out_ref, bias_ref, norm_ref, packed_ref, sem
):
    @pl.when(flag_ref[0] == 1)
    def _():
        copy = pltpu.make_async_copy(first_hbm, packed_ref, sem)
        copy.start()
        copy.wait()

    @pl.when(flag_ref[0] != 1)
    def _():
        copy = pltpu.make_async_copy(second_hbm, packed_ref, sem)
        copy.start()
        copy.wait()

    w_in = packed_ref[:IN]
    small = packed_ref[IN : IN + 16]
    shifts = dot(small, w_in, 1, 1)
    small = small.astype(F32)
    norm_ref[0:3] = small[2:5] + small[5:8]
    bias_ref[...] = small[0:1, :IN] + small[1:2, :IN] + shifts[3:4] + shifts[6:7]
    kept_ref[...] = w_in
    w_in_ref[...] = (w_in.astype(F32) * norm_ref[0:1]).astype(BF)
    w_out_ref[...] = packed_ref[IN + 16 : PACKED]


def finish_kernel(scalars_ref, *refs):
    up_ref, qkv_ref, down_ref, out_ref, biases_ref, whole_ref = refs[-6:]
    n = SUMMED // 4
    for k in range(4):
        place = lax.rem(scalars_ref[20] + 4 - k, 4)
        whole_ref[pl.ds(pl.multiple_of(place * n, 16), n)] = refs[k][...]
    up_ref[...] = whole_ref[:FF_HERE].astype(F32).T
    qkv_ref[...] = whole_ref[FF_HERE:IN].astype(F32)
    biases_ref[...] = whole_ref[IN : IN + 16].astype(F32)[0:8]
    down_ref[...] = whole_ref[IN + 16 : IN + 16 + FF_HERE].astype(F32)
    out_ref[...] = whole_ref[IN + 16 + FF_HERE : PACKED].astype(F32)


def add_kernel(n_out, with_vectors, *refs):
    own_ref, other_ref = refs[:2]
    out_refs = refs[-n_out:]
    count = 8 // n_out
    for k, ref in enumerate(out_refs):
        for part in range(count):
            index = k + part * n_out
            rows = slice(index * BLOCK, (index + 1) * BLOCK)
            value = own_ref[rows].astype(F32) + other_ref[rows].astype(F32)
            ref[part * BLOCK : (part + 1) * BLOCK] = value.astype(ref.dtype)
    if with_vectors:
        rows = slice(ROWS // 2, ROWS // 2 + 16)
        both = own_ref[rows].astype(F32) + other_ref[rows].astype(F32)
        vectors = both[:8] + both[8:]
        high = vectors.astype(BF).astype(F32)
        below = jnp.concatenate([high, vectors - high])
        for ref in out_refs:
            ref[count * BLOCK :] = below.astype(ref.dtype)


def total_of(refs):
    total = refs[0][:BLOCK]
    for ref in refs[1:]:
        total += ref[:BLOCK].astype(F32)
    return total


def close_forward_kernel(*refs):
    rows_ref, norm_ref, result_ref, rounded_ref, scaled_ref = refs[-5:]
    total = total_of(refs[:-5])
    result = rows_ref[...].astype(F32) + total + norm_ref[2:3]
    result_ref[...] = result
    rounded = result.astype(BF)
    rounded_ref[...] = rounded
    scaled_ref[...] = normalize(rounded.astype(F32))[0].astype(BF)


def close_backward_kernel(*refs):
    rows_ref, grad_rows_ref, grad_ref, rounded_ref = refs[-4:]
    total = total_of(refs[:-4])
    grad = normalize_back(grad_rows_ref[...], total, rows_ref[...])
    grad_ref[...] = grad
    rounded_ref[...] = grad.astype(BF)


def fold_kernel(total_ref, *refs):
    mine_ref, pair_ref = refs[-2:]
    total = total_ref[...]
    for ref in refs[:3]:
        total += ref[...].astype(F32)
    size = mine_ref.shape[0]
    mine_ref[:BLOCK] = total[:BLOCK]
    pair_ref[:BLOCK] = total[BLOCK : 2 * BLOCK].astype(BF)
    if size > BLOCK:
        vectors = total[2 * BLOCK : 2 * BLOCK + 8] + total[2 * BLOCK + 8 :]
        high = vectors.astype(BF).astype(F32)
        mine_ref[BLOCK:] = jnp.concatenate([high, vectors - high])
        pair_ref[BLOCK:] = jnp.concatenate([high, vectors - high]).astype(BF)


def gate_kernel(*refs):
    pass


WHOLE = pl.BlockSpec(memory_space=pltpu.VMEM)
SCALARS = pl.BlockSpec(memory_space=pltpu.SMEM)
FAR = pl.BlockSpec(memory_space=pl.ANY)


def limit(size):
    return pltpu.CompilerParams(vmem_limit_bytes=size * 2**20)


SMALL = limit(12)
HALF = jax.ShapeDtypeStruct((ROWS // 2, 1024), BF)
SAVED = [
    jax.ShapeDtypeStruct((ROWS, width), BF) for width in (MIXED, FF_HERE, 2 * HD, 2 * HD, 1024)
]


STORE = jax.ShapeDtypeStruct((10 * ROWS, 1024), BF)


def like(shapes):
    return [pltpu.VMEM(shape.shape, shape.dtype) for shape in shapes]


def forward(chunks, layer, place, stored):
    saved = [STORE] if stored else SAVED[:4]
    outs = pl.pallas_call(
        functools.partial(forward_kernel, len(chunks), stored),
        out_shape=[HALF] * 2 + [jax.ShapeDtypeStruct((1, ROWS), F32)] + saved,
        in_specs=[SCALARS] + [WHOLE] * (len(chunks) + 5),
        out_specs=[WHOLE] * 3 + [FAR] * len(saved),
        scratch_shapes=like(SAVED[:4])
        + [
            pltpu.VMEM((ROWS, 2 * HD), BF),
            pltpu.VMEM((ROWS, 2 * HD), BF),
            pltpu.VMEM((HD, ROWS), BF),
            pltpu.VMEM((ROWS, HD), BF),
            pltpu.SemaphoreType.DMA((20,)),
        ],
        compiler_params=limit(F_LIMIT),
        cost_estimate=pl.CostEstimate(
            flops=12 * 10**9, bytes_accessed=2**24, transcendentals=ROWS * ROWS
        ),
        name="forward",
    )(
        place["scalars"],
        *chunks,
        layer["w_in"],
        layer["bias_in"],
        layer["w_out"],
        place["cosine"],
        place["sine"],
    )
    return outs[:2], outs[2:]


def backward(chunks, others, layer, saved, place, *earlier):
    separate = len(saved) == 2
    saved_shapes = SAVED if separate else SAVED[:4]
    half = (ROWS // 2 + 16 * separate, 1024)
    outs = pl.pallas_call(
        functools.partial(backward_kernel, separate, len(earlier)),
        out_shape=[jax.ShapeDtypeStruct(half, BF)] * 2
        + [jax.ShapeDtypeStruct((SUMMED // 4, 1024), BF)] * 4
        + [jax.ShapeDtypeStruct((2, 1024), F32)],
        in_specs=[SCALARS]
        + [WHOLE] * (len(chunks) + len(others) + 7)
        + [FAR] * (len(saved) - 1 + len(earlier)),
        out_specs=[WHOLE] * 7,
        scratch_shapes=like(saved_shapes)
        + [
            pltpu.VMEM((ROWS, IN), BF),
            pltpu.VMEM((ROWS, 2 * HD), BF),
            pltpu.VMEM((ROWS, 2 * HD), BF),
            pltpu.VMEM((HD, ROWS), BF),
            pltpu.VMEM((ROWS, HD), BF),
            pltpu.VMEM((1, ROWS), F32),
            pltpu.VMEM((HD, ROWS), F32),
            pltpu.VMEM((ROWS, 2 * HD), F32),
            pltpu.VMEM((ROWS, HD), F32),
            pltpu.VMEM((SUMMED, 1024), BF),
            pltpu.SemaphoreType.DMA((5,)),
        ],
        compiler_params=limit(B_LIMIT + 4 * separate),
        cost_estimate=pl.CostEstimate(
            flops=18 * 10**9, bytes_accessed=2**24, transcendentals=ROWS * ROWS
        ),
        name="backward",
    )(
        place["scalars"],
        *chunks,
        *others,
        layer["w_in"],
        layer["w_out"],
        layer["kept"],
        layer["norm"],
        saved[0],
        place["cosine"],
        place["sine"],
        *saved[1:],
        *earlier,
    )
    return outs[:2], outs[2:6], outs[6]


def pack(weights, vectors, earlier):
    return pl.pallas_call(
        pack_kernel,
        out_shape=[jax.ShapeDtypeStruct((PACKED, 1024), BF)] * 2,
        in_specs=[FAR] * 4 + [WHOLE] * 6 + [FAR],
        out_specs=[FAR] * 2,
        scratch_shapes=[
            pltpu.VMEM((1024, FF_HERE), BF),
            pltpu.VMEM((PACKED, 1024), BF),
            pltpu.SemaphoreType.DMA((4,)),
        ],
        compiler_params=limit(PACK_LIMIT),
        name="pack",
    )(*weights, *vectors, earlier)


def unpack(flag, first, second):
    w_in, kept, w_out, bias_in, norm = pl.pallas_call(
        unpack_kernel,
        out_shape=[
            jax.ShapeDtypeStruct((IN, 1024), BF),
            jax.ShapeDtypeStruct((IN, 1024), BF),
            jax.ShapeDtypeStruct((OUT, 1024), BF),
            jax.ShapeDtypeStruct((1, IN), F32),
            jax.ShapeDtypeStruct((3, 1024), F32),
        ],
        in_specs=[SCALARS] + [FAR] * 2,
        out_specs=[WHOLE] * 5,
        scratch_shapes=[pltpu.VMEM((PACKED, 1024), BF), pltpu.SemaphoreType.DMA],
        compiler_params=limit(16),
        name="unpack",
    )(flag, first, second)
    return {"w_in": w_in, "kept": kept, "w_out": w_out, "bias_in": bias_in, "norm": norm}


def finish(scalars, quarters, *earlier):
    return pl.pallas_call(
        finish_kernel,
        out_shape=[
            jax.ShapeDtypeStruct((1024, FF_HERE), F32),
            jax.ShapeDtypeStruct((QKV, 1024), F32),
            jax.ShapeDtypeStruct((FF_HERE, 1024), F32),
            jax.ShapeDtypeStruct((HD, 1024), F32),
            jax.ShapeDtypeStruct((8, 1024), F32),
        ],
        in_specs=[SCALARS] + [WHOLE] * 4 + [FAR] * len(earlier),
        out_specs=[WHOLE] * 5,
        scratch_shapes=[pltpu.VMEM((SUMMED, 1024), BF)],
        compiler_params=limit(16),
        name="finish",
    )(scalars, *quarters, *earlier)


def gate(values, *earlier):
    n = len(values)
    return pl.pallas_call(
        gate_kernel,
        out_shape=[jax.ShapeDtypeStruct(value.shape, value.dtype) for value in values],
        in_specs=[FAR] * (n + len(earlier)),
        out_specs=[FAR] * n,
        input_output_aliases={k: k for k in range(n)},
        compiler_params=limit(1),
        name="gate",
    )(*values, *earlier)


def add(own, other, n_out, *earlier):
    with_vectors = own.shape[0] > ROWS // 2
    size = ROWS // 2 // n_out + 16 * with_vectors
    return pl.pallas_call(
        functools.partial(add_kernel, n_out, with_vectors),
        out_shape=[
            jax.ShapeDtypeStruct((size, 1024), BF if k else F32) for k in range(n_out)
        ],
        in_specs=[WHOLE] * 2 + [FAR] * len(earlier),
        out_specs=[WHOLE] * n_out,
        compiler_params=SMALL,
        name="add",
    )(own, other, *earlier)


def fold(total, arrived, *earlier):
    size = (total.shape[0] - 16) // 2 + 16 if total.shape[0] > 2 * BLOCK else BLOCK
    return pl.pallas_call(
        fold_kernel,
        out_shape=[
            jax.ShapeDtypeStruct((size, 1024), F32),
            jax.ShapeDtypeStruct((size, 1024), BF),
        ],
        in_specs=[WHOLE] * 4 + [FAR] * len(earlier),
        out_specs=[WHOLE] * 2,
        compiler_params=SMALL,
        name="fold",
    )(total, *arrived, *earlier)


def close_forward(parts, rows, norm):
    shape = (BLOCK, 1024)
    return pl.pallas_call(
        close_forward_kernel,
        out_shape=[
            jax.ShapeDtypeStruct(shape, F32),
            jax.ShapeDtypeStruct(shape, BF),
            jax.ShapeDtypeStruct(shape, BF),
        ],
        in_specs=[WHOLE] * (len(parts) + 2),
        out_specs=[WHOLE] * 3,
        compiler_params=SMALL,
        name="close_forward",
    )(*parts, rows, norm)


def close_backward(parts, rows, grad_rows):
    shape = (BLOCK, 1024)
    return pl.pallas_call(
        close_backward_kernel,
        out_shape=[jax.ShapeDtypeStruct(shape, F32), jax.ShapeDtypeStruct(shape, BF)],
        in_specs=[WHOLE] * (len(parts) + 2),
        out_specs=[WHOLE] * 2,
        compiler_params=SMALL,
        name="close_backward",
    )(*parts, rows, grad_rows)


def rotary_lanes(starts):
    lane = jnp.arange(2 * HD, dtype=jnp.int32) % HD
    inverse = jnp.power(10000.0, -2.0 * (lane % (ROT // 2)).astype(F32) / ROT)
    inverse = jnp.where(lane < ROT, inverse, 0.0)[None, :]
    coarse = (jnp.arange(0, ROWS, 64, dtype=jnp.int32) - starts[::64]).astype(F32)[:, None] * inverse
    fine = jnp.arange(64, dtype=jnp.int32).astype(F32)[:, None] * inverse
    cos_a, sin_a = jnp.cos(coarse)[:, None, :], jnp.sin(coarse)[:, None, :]
    cos_b, sin_b = jnp.cos(fine)[None], jnp.sin(fine)[None]
    shape = (ROWS, 2 * HD)
    return (
        (cos_a * cos_b - sin_a * sin_b).reshape(shape),
        (sin_a * cos_b + cos_a * sin_b).reshape(shape),
    )


def ring_sum(value):
    pieces = [
        lax.ppermute(value, "dp", [(i, (i + steps) % 4) for i in range(4)]) for steps in (1, 3, 2)
    ]
    return value + pieces[0] + pieces[1] + pieces[2]


def over_dp(part, steps):
    return lax.ppermute(part, "dp", [(i, (i + steps) % 4) for i in range(4)])


def shares_from_dp(shares):
    return [shares[0]] + [over_dp(part, steps) for part, steps in zip(shares[1:], (1, 3, 2))]


def quarter_sum(shares):
    total = shares[0].astype(F32)
    for share in shares[1:]:
        total += share.astype(F32)
    return total.astype(BF)


def body(
    inputs,
    seq_lengths,
    cotangent,
    ln_gain,
    ln_bias,
    w_qkv,
    b_qkv,
    w_out,
    b_out,
    w_up,
    b_up,
    w_down,
    b_down,
):
    core, z, y = (lax.axis_index(name) for name in DEVICES)
    on_first = core == 0
    micro = jnp.where((y == 0) | (y == 3), 0, 1)
    on_micro_0 = micro == 0
    sent = jnp.where(on_first, micro, 1 - micro)

    def pick(value, index):
        return lax.dynamic_index_in_dim(value, index, 0, keepdims=False)

    sent_rows = pick(inputs, sent)
    scaled_rows = normalize(sent_rows.astype(F32))[0].astype(BF)
    scaled = from_arguments(scaled_rows, on_first)
    chunks_0 = gather_pieces(scaled)
    later_rows, later_grads = gate([sent_rows, pick(cotangent, sent)], scaled)
    rows_0 = jnp.where(on_first, later_rows, send(later_rows, OVER))
    both = from_arguments(later_grads, on_first)
    grad_rows_1 = both[:BLOCK]

    weights = (w_up[0], w_qkv.reshape(1024, QKV).T, w_down[0], w_out[0])
    small = (b_up, b_qkv[0], ln_gain, ln_bias, b_out, b_down)
    mine, again = pack(weights, small, scaled_rows)
    swapped = send(mine, SWAP)
    flag = jnp.where(on_first, 1, 0).astype(jnp.int32)
    layer_0 = unpack(flag[None], mine, swapped)

    starts = start_rows(pick(seq_lengths, micro), ROWS)
    cosine, sine = rotary_lanes(starts)
    scalars = [
        gathered_blocks(core, z, y),
        starts[::SPAN] // SPAN,
        lax.axis_index("dp")[None],
    ]
    place = {
        "scalars": jnp.concatenate([part.astype(jnp.int32) for part in scalars]),
        "cosine": cosine,
        "sine": sine,
    }

    (early,) = gate([both], chunks_0[3])
    pieces = [early] + [send(early, table(step(hops))) for hops in RING[:2]]
    halves_0, saved_0 = forward(chunks_0, layer_0, place, True)
    (other_0,) = gate([halves_0[1]], *pieces[1:])
    total, *blocks = add(halves_0[0], send(other_0, SIBLING), 8)
    arrived = scatter(blocks)
    result_0, rows_1, scaled_rows = close_forward([total] + arrived, rows_0, layer_0["norm"])
    (again,) = gate([again], rows_1)
    over = send(again, OVER)
    layer_1 = unpack(flag[None], swapped, over)
    chunks_1 = gather(scaled_rows)
    (late,) = gate([both], chunks_1[7])
    pieces.append(send(late, table(step(RING[2]))))
    halves_1, saved_1 = forward(chunks_1, layer_1, place, False)

    result_0_there = send(result_0, BACK_OVER)
    pieces[3:] = gate(pieces[3:], halves_1[0])
    grad_halves_1, shares_1, vectors_1 = backward(
        with_sibling(pieces), chunks_1, layer_1, saved_1, place, result_0_there
    )
    total, *blocks = add(grad_halves_1[0], send(grad_halves_1[1], SIBLING), 4)
    (other_1,) = gate([halves_1[1]], blocks[0])
    first, *pieces = add(halves_1[0], send(other_1, SIBLING), 4)
    shares_1 = shares_from_dp(shares_1)
    mine, pair = fold(total, scatter_pieces(blocks), *shares_1[1:])
    pair = send(pair, table(step(0, PAIR)))
    grad_input_1, grad_rows_0 = close_backward([mine, pair], rows_1, grad_rows_1)
    grad_chunks_0 = gather(grad_rows_0)
    share_1 = quarter_sum([*gate(shares_1[:1], mine), *shares_1[1:]])
    quarter_1 = (send(share_1, SIBLING).astype(F32) + send(share_1, OVER).astype(F32)).astype(BF)

    pieces = scatter_pieces(gate(pieces, grad_chunks_0[7]))
    grad_input_1_here = send(grad_input_1, SIBLING)
    grad_input_1_there = send(grad_input_1, OVER)

    vectors = jnp.concatenate(
        [
            jnp.zeros((2, 1024), F32),
            jnp.sum(grad_rows_0.astype(F32), axis=0)[None],
            vectors_1,
            jnp.sum(grad_rows_1.astype(F32), axis=0)[None],
            jnp.zeros((2, 1024), F32),
        ]
    )
    grad_halves_0, shares_0, unused_vectors = backward(
        grad_chunks_0,
        [vectors],
        layer_0,
        saved_0,
        place,
        quarter_1,
        grad_input_1_here,
        grad_input_1_there,
    )
    (other_0,) = gate([grad_halves_0[1]], *pieces)
    total, *blocks = add(grad_halves_0[0], send(other_0, SIBLING), 4)
    shares_0 = shares_from_dp(shares_0)
    mine, pair = fold(total, scatter_pieces(blocks), *shares_0[1:])
    mine_1, pair_1 = fold(first, pieces)
    result_1, unused_rounded, unused_rows = close_forward(
        [mine_1, send(pair_1, table(step(0, PAIR)))], rows_1, layer_1["norm"]
    )
    pair = send(pair, table(step(0, PAIR)))
    grad_input_0, unused_rounded = close_backward([mine, pair], rows_0, grad_rows_0)
    share_0 = quarter_sum([*gate(shares_0[:1], mine), *shares_0[1:]])
    mine_0 = (share_0.astype(F32) + send(share_0, BACK_OVER).astype(F32)).astype(BF)
    quarter = jnp.where(on_first, mine_0, quarter_1)
    quarters = [quarter] + [over_dp(quarter, steps) for steps in (1, 2, 3)]
    vectors = mine[BLOCK:] + pair[BLOCK:].astype(F32)
    vectors = vectors[:8] + vectors[8:]
    vectors = ring_sum(vectors + send(vectors, table(step(0, 1))))
    vectors = jnp.where(on_first, vectors[:3], vectors[3:6])
    grad_input_0_there = send(grad_input_0, BACK_OVER)
    grad_up, grad_qkv, grad_down, grad_out, grad_biases = finish(
        place["scalars"], quarters, grad_input_0_there, vectors
    )

    def output_of(value_0, there_0, here_1, there_1):
        here = jnp.where(on_first, value_0, here_1)
        there = jnp.where(on_first, there_0, there_1)
        return jnp.stack(
            [jnp.where(on_micro_0, here, there), jnp.where(on_micro_0, there, here)]
        )[None]

    return (
        output_of(
            result_0, result_0_there, send(result_1, SIBLING), send(result_1, OVER)
        ),
        output_of(
            grad_input_0,
            grad_input_0_there,
            grad_input_1_here,
            grad_input_1_there,
        ),
        vectors[0:1],
        vectors[1:2],
        grad_qkv.T.reshape(1, 1024, 1, QKV),
        grad_biases[0, FF_HERE:IN].reshape(1, 1, QKV),
        grad_out[None],
        vectors[2:3],
        grad_up[None],
        grad_biases[0:1, :FF_HERE],
        grad_down[None],
        vectors[2:3],
    )


def solution(mesh):
    rows = P("dp", ("z", "y"), None)
    layer_rows = P("pipe", "dp", ("z", "y"), None)
    heads = P("pipe", None, ("z", "y"), None)
    split = P("pipe", ("z", "y"), None)
    units = P("pipe", None, ("z", "y"))
    whole = P("pipe", None)
    unit_bias = P("pipe", ("z", "y"))
    return jax.shard_map(
        body,
        mesh=Mesh(mesh.devices.reshape(2, 4, 4, 4), ("pipe", "dp", "z", "y")),
        in_specs=(
            rows,
            P("dp", None),
            rows,
            whole,
            whole,
            heads,
            split,
            split,
            whole,
            units,
            unit_bias,
            split,
            whole,
        ),
        out_specs=(
            layer_rows,
            layer_rows,
            whole,
            whole,
            heads,
            split,
            split,
            whole,
            units,
            unit_bias,
            split,
            whole,
        ),
        check_vma=False,
    )
```

```python
import functools

import jax
import jax.numpy as jnp
from jax import lax
from jax.experimental import pallas as pl
from jax.experimental.pallas import tpu as pltpu
from jax.sharding import Mesh, PartitionSpec as P

HD = 64
ROT = 16
FF_HERE = 256
QKV = 3 * HD
IN = FF_HERE + QKV
OUT = FF_HERE + HD
PACKED = IN + 16 + OUT
SUMMED = 832
MIXED = 384
F_LIMIT = 14
B_LIMIT = 23
PACK_LIMIT = 56
ROWS = 2048
BLOCK = 128
SPAN = 512
SPANS = ROWS // SPAN
PER_SPAN = SPAN // BLOCK
EPSILON = 1e-05
NEGATIVE = -1e30
ROOT_HALF = 0.7071067811865476
INV_ROOT_TAU = 0.3989422804014327
DEVICES = ("pipe", "z", "y")
BF = jnp.bfloat16
F32 = jnp.float32


def table(rule):
    pairs = []
    for core in range(2):
        for z in range(4):
            for y in range(4):
                target = rule(core, z, y)
                if target is not None:
                    to_core, to_z, to_y = target
                    pairs.append((core * 16 + z * 4 + y, to_core * 16 + to_z % 4 * 4 + to_y))
    return pairs


def by_core(first, second):
    return table(lambda core, z, y: (first if core == 0 else second)(core, z, y))


def step(steps, flip=0):
    return lambda core, z, y: (core, z + steps, y ^ flip)


def nowhere(core, z, y):
    return None


PAIR = 3
SIBLING = table(lambda core, z, y: (1 - core, z, y))
OVER = by_core(nowhere, step(0, 1))
BACK_OVER = by_core(nowhere, lambda core, z, y: (0, z, y ^ 1))
SWAP = by_core(lambda core, z, y: (1, z, y ^ 1), lambda core, z, y: (0, z, y))
RING = (1, -1, 2)


def send(value, pairs):
    return lax.ppermute(value, DEVICES, pairs)


def gathered_blocks(core, z, y):
    def of(own):
        columns = (y ^ own, y ^ own ^ PAIR)
        steps = [0] + [-hops for hops in RING]
        return [(z + hops) % 4 * 4 + column for column in columns for hops in steps]

    first, second = jnp.stack(of(0)), jnp.stack(of(1))
    return jnp.where(
        core == 0, jnp.concatenate([first, second]), jnp.concatenate([second, first])
    ).astype(jnp.int32)


def with_sibling(blocks):
    return blocks + [send(block, SIBLING) for block in blocks]


def gather(rows):
    pair = send(rows, table(step(0, PAIR)))
    own = [send(rows, table(step(hops))) for hops in RING]
    far = [send(pair, table(step(hops))) for hops in RING]
    return with_sibling([rows] + own + [pair] + far)


def from_arguments(rows, on_first):
    near = send(rows, by_core(step(0, PAIR), step(0, 1)))
    beside = send(rows, by_core(nowhere, step(0, 2)))
    return jnp.concatenate([jnp.where(on_first, rows, near), jnp.where(on_first, near, beside)])


def gather_pieces(both):
    return with_sibling([both] + [send(both, table(step(hops))) for hops in RING])


def scatter(blocks):
    steps = [(-hops, 0) for hops in RING] + [(0, PAIR)] + [(-hops, PAIR) for hops in RING]
    return [send(block, table(step(hops, flip))) for block, (hops, flip) in zip(blocks, steps)]


def scatter_pieces(pieces):
    return [send(piece, table(step(-hops))) for piece, hops in zip(pieces, RING)]


def start_rows(lengths, total_rows):
    endings = jnp.cumsum(lengths)
    places = jnp.arange(total_rows, dtype=jnp.int32)
    passed = places[:, None] >= endings[None, :]
    return jnp.sum(jnp.where(passed, lengths[None, :], 0), axis=1)


def normalize(rows):
    average = jnp.mean(rows, axis=-1, keepdims=True)
    centred = rows - average
    inverse_std = lax.rsqrt(jnp.mean(centred * centred, axis=-1, keepdims=True) + EPSILON)
    return centred * inverse_std, inverse_std


def normalize_back(grad_rows, grad_scaled, rows):
    scaled, inverse_std = normalize(rows.astype(F32))
    return grad_rows.astype(F32) + inverse_std * (
        grad_scaled
        - jnp.mean(grad_scaled, axis=-1, keepdims=True)
        - scaled * jnp.mean(grad_scaled * scaled, axis=-1, keepdims=True)
    )


def block_of(index):
    return pl.ds(pl.multiple_of(index * BLOCK, BLOCK), BLOCK)


def dot(left, right, left_axis=1, right_axis=0):
    return lax.dot_general(
        left, right, (((left_axis,), (right_axis,)), ((), ())), preferred_element_type=F32
    )


def started(parts, sems, first):
    copies = [pltpu.make_async_copy(*part, sems.at[first + k]) for k, part in enumerate(parts)]
    for copy in copies:
        copy.start()
    return copies


def finished(copies):
    for copy in copies:
        copy.wait()


def stacked(refs, group, first):
    return jnp.concatenate(
        [refs[group * PER_SPAN + k][first : first + BLOCK] for k in range(PER_SPAN)]
    )


def chunk_of(refs, group):
    if len(refs) == 16:
        return stacked(refs, group, 0)
    pieces = refs[group // 2 * PER_SPAN : (group // 2 + 1) * PER_SPAN]
    return stacked(pieces, 0, group % 2 * BLOCK)


def half_of(refs, group):
    place = group % (SPANS // 2) * SPAN
    return refs[group // (SPANS // 2)].at[pl.ds(place, SPAN)]


def turned(pairs):
    lane = lax.broadcasted_iota(jnp.int32, pairs.shape, 1) % HD
    return jnp.where(
        lane < ROT // 2, -pltpu.roll(pairs, 2 * HD - ROT // 2, 1), pltpu.roll(pairs, ROT // 2, 1)
    )


def halves(pairs):
    lane = lax.broadcasted_iota(jnp.int32, pairs.shape, 1)
    queries = jnp.where(lane < HD, pairs * HD ** (-0.5), 0.0)
    return queries.astype(BF), pltpu.roll(pairs, HD, 1).astype(BF)


def penalty(scalars_ref, query_span, key_span):
    return jnp.where(key_span >= scalars_ref[16 + query_span], 0.0, -NEGATIVE).astype(F32)


def seen(scores):
    keys = lax.broadcasted_iota(jnp.int32, scores.shape, 0)
    queries = lax.broadcasted_iota(jnp.int32, scores.shape, 1)
    return jnp.where(keys <= queries, scores, NEGATIVE)


def store_parts(store_ref, saved_refs):
    lanes = (0, MIXED, MIXED + FF_HERE, MIXED + FF_HERE + 2 * HD)
    places = [
        store_ref.at[pl.ds(ROWS, ROWS), pl.ds(lane, ref.shape[1])]
        for lane, ref in zip(lanes, saved_refs)
    ]
    return places + [store_ref.at[pl.ds(0, ROWS)]]


def forward_kernel(n_chunks, stored, *refs):
    scalars_ref = refs[0]
    chunk_refs, refs = refs[1 : 1 + n_chunks], refs[1 + n_chunks :]
    w_in_ref, bias_ref, w_out_ref, cosine_ref, sine_ref = refs[:5]
    half_refs, log_sums_ref, refs = refs[5:7], refs[7], refs[8:]
    kept_hbm, kept_refs, refs = refs[:-9], refs[-9:-5], refs[-5:]
    mixed_ref, slope_ref, pairs_ref, values_ref = kept_refs
    queries_ref, keys_ref, turned_values_ref, ordered_ref, sems = refs
    copies = []
    if stored:
        kept_hbm = store_parts(kept_hbm[0], kept_refs)
        parts = []
        for k in range(16):
            source = chunk_refs[k // 8 * 4 + k % 4].at[pl.ds(k % 8 // 4 * BLOCK, BLOCK)]
            parts.append((source, kept_hbm[4].at[pl.ds(k * BLOCK, BLOCK)]))
        copies = started(parts, sems, 0)
    for group in range(SPANS):
        rows = slice(group * SPAN, (group + 1) * SPAN)
        projected = dot(chunk_of(chunk_refs, group), w_in_ref[...], 1, 1) + bias_ref[...]
        inner = projected[:, :FF_HERE]
        wave = 1.0 + lax.erf(inner * ROOT_HALF)
        mixed_ref[rows, :FF_HERE] = (0.5 * inner * wave).astype(BF)
        slope = 0.5 * wave + inner * jnp.exp(-0.5 * inner * inner) * INV_ROOT_TAU
        slope_ref[rows] = slope.astype(BF)
        for k in range(PER_SPAN):
            joined = projected[k * BLOCK : (k + 1) * BLOCK, FF_HERE:]
            place = block_of(scalars_ref[group * PER_SPAN + k])
            pairs = joined[:, : 2 * HD]
            pairs = pairs * cosine_ref[place] + turned(pairs) * sine_ref[place]
            pairs_ref[place] = pairs.astype(BF)
            queries_ref[place], keys_ref[place] = halves(pairs.astype(BF).astype(F32))
            values = joined[:, 2 * HD :]
            values_ref[place, :HD] = values.astype(BF)
            turned_values_ref[:, place] = values.T.astype(BF)
    for i in range(SPANS):
        span = slice(i * SPAN, (i + 1) * SPAN)
        queries = queries_ref[span]
        scores, offsets, highest = [], [], None
        for j in range(i + 1):
            block = dot(keys_ref[j * SPAN : (j + 1) * SPAN], queries, 1, 1)
            block = seen(block) if i == j else block
            offset = 0.0 if i == j else penalty(scalars_ref, i, j)
            top = jnp.max(block, axis=0, keepdims=True) - offset
            highest = top if highest is None else jnp.maximum(highest, top)
            scores.append(block)
            offsets.append(offset)
        total, summed = 0.0, 0.0
        for j in range(i + 1):
            exponent = jnp.exp(scores[j] - (highest + offsets[j]))
            total = total + jnp.sum(exponent, axis=0, keepdims=True)
            summed = summed + dot(
                turned_values_ref[:, j * SPAN : (j + 1) * SPAN], exponent.astype(BF)
            )
        log_sums_ref[:, span] = highest + jnp.log(total)
        ordered_ref[span] = (summed / total).T.astype(BF)
    for group in range(SPANS):
        for k in range(PER_SPAN):
            index = group * PER_SPAN + k
            here = slice(index * BLOCK, (index + 1) * BLOCK)
            mixed_ref[here, FF_HERE:OUT] = ordered_ref[block_of(scalars_ref[index])]
        rows = slice(group * SPAN, (group + 1) * SPAN)
        half_of(half_refs, group)[...] = dot(mixed_ref[rows, :OUT], w_out_ref[...]).astype(BF)
    copies += started(list(zip(kept_refs, kept_hbm)), sems, 16)
    finished(copies)


def backward_kernel(separate, n_earlier, *refs):
    scalars_ref = refs[0]
    count = 16 if separate else 8
    chunk_refs, refs = refs[1 : 1 + count], refs[1 + count :]
    feature_refs, given_refs = [], None
    if separate:
        given_refs, refs = refs[:3], refs[3:]
    else:
        feature_refs, refs = refs[:16], refs[16:]

    w_in_ref, w_out_ref, kept_ref, norm_ref, log_sums_ref, cosine_ref, sine_ref = refs[:7]
    count = 5 if separate else 4
    n_saved = 1 if separate else 4
    saved_hbm, refs = refs[7 : 7 + n_saved], refs[7 + n_saved + n_earlier :]
    n_parts = 4 if separate else 2
    half_refs, quarter_refs, refs = refs[:2], refs[2 : 2 + n_parts], refs[2 + n_parts :]
    vectors_ref, refs = refs[0], refs[1:]
    saved_refs, refs = refs[:count], refs[count:]
    mixed_ref, slope_ref, pairs_ref, values_ref = saved_refs[:4]
    features_ref = saved_refs[-1]
    grad_in_ref, queries_ref, keys_ref, turned_keys_ref, grad_heads_ref, products_ref = refs[:6]
    grad_queries_ref, grad_keys_ref, grad_values_ref, grads_ref, sems = refs[6:]
    if separate:
        saved_hbm = store_parts(saved_hbm[0], saved_refs[:4])
    copies = started(list(zip(saved_hbm, saved_refs)), sems, 0)
    finished(copies[:4])
    for group in range(SPANS):
        rows = slice(group * SPAN, (group + 1) * SPAN)
        grad_mixed = dot(chunk_of(chunk_refs, group), w_out_ref[...], 1, 1)
        grad_in_ref[rows, :FF_HERE] = (
            grad_mixed[:, :FF_HERE] * slope_ref[rows].astype(F32)
        ).astype(BF)
        for k in range(PER_SPAN):
            index = group * PER_SPAN + k
            here, place = slice(index * BLOCK, (index + 1) * BLOCK), block_of(scalars_ref[index])
            grad_heads = grad_mixed[k * BLOCK : (k + 1) * BLOCK, FF_HERE:].astype(BF)
            grad_heads_ref[place] = grad_heads
            product = grad_heads.astype(F32) * mixed_ref[here, FF_HERE:OUT].astype(F32)
            products_ref[:, place] = jnp.sum(product.T, axis=0, keepdims=True)
            queries_ref[here], keys = halves(pairs_ref[here].astype(F32))
            keys_ref[here] = keys
            turned_keys_ref[:, here] = keys[:, :HD].astype(F32).T.astype(BF)
    grad_queries_ref[...] = jnp.zeros_like(grad_queries_ref)
    for j in range(SPANS):
        key_span = slice(j * SPAN, (j + 1) * SPAN)
        keys, values = keys_ref[key_span], values_ref[key_span, :HD]
        grad_keys, grad_values = 0.0, 0.0
        for i in range(j, SPANS):
            span = slice(i * SPAN, (i + 1) * SPAN)
            queries, grad_heads = queries_ref[span], grad_heads_ref[span]
            scores = dot(keys, queries, 1, 1)
            scores = seen(scores) if i == j else scores
            offset = 0.0 if i == j else penalty(scalars_ref, i, j)
            probability = jnp.exp(scores - (log_sums_ref[:, span] + offset))
            grad_values += dot(probability.astype(BF), grad_heads)
            grad_probs = dot(values, grad_heads, 1, 1)
            grad_scores = (probability * (grad_probs - products_ref[:, span])).astype(BF)
            grad_keys += dot(grad_scores, queries)
            grad_queries_ref[:, span] += dot(turned_keys_ref[:, key_span], grad_scores)
        grad_keys_ref[key_span] = grad_keys
        grad_values_ref[key_span] = grad_values
    for group in range(SPANS):
        for k in range(PER_SPAN):
            index = group * PER_SPAN + k
            here, place = slice(index * BLOCK, (index + 1) * BLOCK), block_of(scalars_ref[index])
            grad_queries = (grad_queries_ref[:, place] * HD ** (-0.5)).T
            grad_pairs = jnp.concatenate([grad_queries, grad_keys_ref[place, :HD]], axis=1)
            grad_pairs = grad_pairs * cosine_ref[place] - turned(grad_pairs) * sine_ref[place]
            grad_in_ref[here, FF_HERE : FF_HERE + 2 * HD] = grad_pairs.astype(BF)
            grad_in_ref[here, FF_HERE + 2 * HD :] = grad_values_ref[place].astype(BF)
        rows = slice(group * SPAN, (group + 1) * SPAN)
        half_of(half_refs, group)[...] = dot(grad_in_ref[rows], w_in_ref[...]).astype(BF)
    finished(copies[4:])
    raw, after, columns = 0.0, 0.0, 0.0
    ones = jnp.ones((SPAN, BLOCK), BF)
    total = jnp.zeros((1, IN), F32)
    for group in range(SPANS):
        rows = slice(group * SPAN, (group + 1) * SPAN)
        grad_in = grad_in_ref[rows]
        features = features_ref[rows] if separate else stacked(feature_refs, group, 0)
        raw += dot(grad_in, features, 0, 0)
        columns += dot(grad_in, ones, 0, 0)
        total += jnp.sum(grad_in.astype(F32), axis=0, keepdims=True)
        after += dot(mixed_ref[rows, :OUT], chunk_of(chunk_refs, group), 0, 0)
    kept = kept_ref[...].astype(F32)
    gain, shift = norm_ref[0:1], norm_ref[1:2]
    column = columns[:, :1]
    grads_ref[:IN] = (raw * gain + column * shift).astype(BF)
    grads_ref[IN : IN + 16] = jnp.zeros((16, 1024), BF)
    grads_ref[IN : IN + 1, :IN] = total.astype(BF)
    grads_ref[IN + 16 : PACKED] = after.astype(BF)
    grads_ref[PACKED:] = jnp.zeros((SUMMED - PACKED, 1024), BF)
    n = SUMMED // 4

    def quarter(index):
        return grads_ref[pl.ds(pl.multiple_of(index * n, 16), n)]

    here = scalars_ref[20]
    if separate:
        for ref, steps in zip(quarter_refs, (0, 1, 3, 2)):
            ref[...] = quarter(lax.rem(here + steps, 4))
    else:
        for ref, first in zip(quarter_refs, (here, here ^ 1)):
            ref[:n] = quarter(first)
            ref[n:] = quarter(first ^ 2)
    grad_gain = jnp.sum(raw * kept, axis=0, keepdims=True)
    grad_shift = jnp.sum(column * kept, axis=0, keepdims=True)
    if not separate:
        vectors_ref[0:1] = grad_gain
        vectors_ref[1:2] = grad_shift
        return
    row = lax.broadcasted_iota(jnp.int32, (8, 1024), 0)
    rows_ref, norm_1_ref, rows_1_ref = given_refs
    parts = (grad_gain, grad_shift, rows_ref[...], norm_1_ref[0:1], norm_1_ref[1:2], rows_1_ref[...])
    vectors = jnp.zeros((8, 1024), F32)
    for k, part in enumerate(parts):
        vectors = jnp.where(row == k, part, vectors)
    high = vectors.astype(BF).astype(F32)
    vectors = jnp.concatenate([high, vectors - high]).astype(BF)
    for ref in half_refs:
        ref[ROWS // 2 :] = vectors


def pack_kernel(*refs):
    up_hbm, qkv_hbm, down_hbm, out_hbm, b_up_ref, b_qkv_ref, gain_ref, shift_ref = refs[:8]
    b_out_ref, b_down_ref, unused_ref, *packed_hbm, up_ref, packed_ref, sems = refs[8:]
    parts = [
        (up_hbm, up_ref),
        (qkv_hbm, packed_ref.at[pl.ds(FF_HERE, QKV)]),
        (down_hbm, packed_ref.at[pl.ds(IN + 16, FF_HERE)]),
        (out_hbm, packed_ref.at[pl.ds(IN + 16 + FF_HERE, HD)]),
    ]
    copies = started(parts, sems, 0)
    biases = jnp.concatenate(
        [b_up_ref[...], b_qkv_ref[...], jnp.zeros((1, 1024 - IN), F32)], axis=1
    )
    rows = lax.broadcasted_iota(jnp.int32, (16, 1024), 0)
    small = jnp.zeros((16, 1024), F32)
    for value, high_row, low_row in (
        (biases, 0, 1),
        (gain_ref[...], 2, 5),
        (shift_ref[...], 3, 6),
        (b_out_ref[...] + b_down_ref[...], 4, 7),
    ):
        high = value.astype(BF).astype(F32)
        small = jnp.where(rows == high_row, high, small)
        small = jnp.where(rows == low_row, value - high, small)
    packed_ref[IN : IN + 16] = small.astype(BF)
    copies[0].wait()
    packed_ref[:FF_HERE] = up_ref[...].T
    finished(copies[1:])
    finished(started([(packed_ref, target) for target in packed_hbm], sems, 0))


def unpack_kernel(
    flag_ref, first_hbm, second_hbm, w_in_ref, kept_ref, w_out_ref, bias_ref, norm_ref, packed_ref, sem
):
    @pl.when(flag_ref[0] == 1)
    def _():
        copy = pltpu.make_async_copy(first_hbm, packed_ref, sem)
        copy.start()
        copy.wait()

    @pl.when(flag_ref[0] != 1)
    def _():
        copy = pltpu.make_async_copy(second_hbm, packed_ref, sem)
        copy.start()
        copy.wait()

    w_in = packed_ref[:IN]
    small = packed_ref[IN : IN + 16]
    shifts = dot(small, w_in, 1, 1)
    small = small.astype(F32)
    norm_ref[0:3] = small[2:5] + small[5:8]
    bias_ref[...] = small[0:1, :IN] + small[1:2, :IN] + shifts[3:4] + shifts[6:7]
    kept_ref[...] = w_in
    w_in_ref[...] = (w_in.astype(F32) * norm_ref[0:1]).astype(BF)
    w_out_ref[...] = packed_ref[IN + 16 : PACKED]


def finish_kernel(scalars_ref, *refs):
    up_ref, qkv_ref, down_ref, out_ref, biases_ref, vectors_ref, whole_ref = refs[4:]
    n = SUMMED // 4
    vectors = 0.0
    for k in range(4):
        place = lax.rem(scalars_ref[20] + 4 - k, 4)
        whole_ref[pl.ds(pl.multiple_of(place * n, 16), n)] = refs[k][:n]
        vectors += refs[k][n : n + 8].astype(F32) + refs[k][n + 8 :].astype(F32)
    vectors_ref[...] = vectors
    up_ref[...] = whole_ref[:FF_HERE].astype(F32).T
    qkv_ref[...] = whole_ref[FF_HERE:IN].astype(F32)
    biases_ref[...] = whole_ref[IN : IN + 16].astype(F32)[0:8]
    down_ref[...] = whole_ref[IN + 16 : IN + 16 + FF_HERE].astype(F32)
    out_ref[...] = whole_ref[IN + 16 + FF_HERE : PACKED].astype(F32)


def add_kernel(n_out, with_vectors, *refs):
    own_ref, other_ref = refs[:2]
    out_refs = refs[-n_out:]
    count = 8 // n_out
    for k, ref in enumerate(out_refs):
        for part in range(count):
            index = k + part * n_out
            rows = slice(index * BLOCK, (index + 1) * BLOCK)
            value = own_ref[rows].astype(F32) + other_ref[rows].astype(F32)
            ref[part * BLOCK : (part + 1) * BLOCK] = value.astype(ref.dtype)
    if with_vectors:
        rows = slice(ROWS // 2, ROWS // 2 + 16)
        both = own_ref[rows].astype(F32) + other_ref[rows].astype(F32)
        vectors = both[:8] + both[8:]
        high = vectors.astype(BF).astype(F32)
        below = jnp.concatenate([high, vectors - high])
        for ref in out_refs:
            ref[count * BLOCK :] = below.astype(ref.dtype)


def total_of(refs):
    total = refs[0][:BLOCK]
    for ref in refs[1:]:
        total += ref[:BLOCK].astype(F32)
    return total


def close_forward_kernel(*refs):
    rows_ref, norm_ref, result_ref, rounded_ref, scaled_ref = refs[-5:]
    total = total_of(refs[:-5])
    result = rows_ref[...].astype(F32) + total + norm_ref[2:3]
    result_ref[...] = result
    rounded = result.astype(BF)
    rounded_ref[...] = rounded
    scaled_ref[...] = normalize(rounded.astype(F32))[0].astype(BF)


def close_backward_kernel(n_parts, *refs):
    rows_ref, grad_rows_ref = refs[n_parts : n_parts + 2]
    grad_ref, rounded_ref = refs[-2:]
    total = total_of(refs[:n_parts])
    grad = normalize_back(grad_rows_ref[...], total, rows_ref[...])
    grad_ref[...] = grad
    rounded_ref[...] = grad.astype(BF)


def fold_kernel(total_ref, *refs):
    mine_ref, pair_ref = refs[-2:]
    total = total_ref[...]
    for ref in refs[:3]:
        total += ref[...].astype(F32)
    size = mine_ref.shape[0]
    mine_ref[:BLOCK] = total[:BLOCK]
    pair_ref[:BLOCK] = total[BLOCK : 2 * BLOCK].astype(BF)
    if size > BLOCK:
        vectors = total[2 * BLOCK : 2 * BLOCK + 8] + total[2 * BLOCK + 8 :]
        high = vectors.astype(BF).astype(F32)
        mine_ref[BLOCK:] = jnp.concatenate([high, vectors - high])
        pair_ref[BLOCK:] = jnp.concatenate([high, vectors - high]).astype(BF)


def join_kernel(quarter_ref, mine_ref, pair_ref, joined_ref):
    n = SUMMED // 4
    joined_ref[:n] = quarter_ref[...]
    both = mine_ref[BLOCK:] + pair_ref[BLOCK:].astype(F32)
    vectors = both[:8] + both[8:]
    high = vectors.astype(BF).astype(F32)
    joined_ref[n:] = jnp.concatenate([high, vectors - high]).astype(BF)


def gate_kernel(*refs):
    pass


WHOLE = pl.BlockSpec(memory_space=pltpu.VMEM)
SCALARS = pl.BlockSpec(memory_space=pltpu.SMEM)
FAR = pl.BlockSpec(memory_space=pl.ANY)


def limit(size):
    return pltpu.CompilerParams(vmem_limit_bytes=size * 2**20)


SMALL = limit(12)
HALF = jax.ShapeDtypeStruct((ROWS // 2, 1024), BF)
SAVED = [
    jax.ShapeDtypeStruct((ROWS, width), BF) for width in (MIXED, FF_HERE, 2 * HD, 2 * HD, 1024)
]


STORE = jax.ShapeDtypeStruct((10 * ROWS, 1024), BF)


def like(shapes):
    return [pltpu.VMEM(shape.shape, shape.dtype) for shape in shapes]


def forward(chunks, layer, place, stored):
    saved = [STORE] if stored else SAVED[:4]
    outs = pl.pallas_call(
        functools.partial(forward_kernel, len(chunks), stored),
        out_shape=[HALF] * 2 + [jax.ShapeDtypeStruct((1, ROWS), F32)] + saved,
        in_specs=[SCALARS] + [WHOLE] * (len(chunks) + 5),
        out_specs=[WHOLE] * 3 + [FAR] * len(saved),
        scratch_shapes=like(SAVED[:4])
        + [
            pltpu.VMEM((ROWS, 2 * HD), BF),
            pltpu.VMEM((ROWS, 2 * HD), BF),
            pltpu.VMEM((HD, ROWS), BF),
            pltpu.VMEM((ROWS, HD), BF),
            pltpu.SemaphoreType.DMA((20,)),
        ],
        compiler_params=limit(F_LIMIT),
        cost_estimate=pl.CostEstimate(
            flops=12 * 10**9, bytes_accessed=2**24, transcendentals=ROWS * ROWS
        ),
        name="forward",
    )(
        place["scalars"],
        *chunks,
        layer["w_in"],
        layer["bias_in"],
        layer["w_out"],
        place["cosine"],
        place["sine"],
    )
    return outs[:2], outs[2:]


def backward(chunks, others, layer, saved, place, *earlier):
    separate = len(saved) == 2
    saved_shapes = SAVED if separate else SAVED[:4]
    half = (ROWS // 2 + 16 * separate, 1024)
    parts = 4 if separate else 2
    outs = pl.pallas_call(
        functools.partial(backward_kernel, separate, len(earlier)),
        out_shape=[jax.ShapeDtypeStruct(half, BF)] * 2
        + [jax.ShapeDtypeStruct((SUMMED // parts, 1024), BF)] * parts
        + [jax.ShapeDtypeStruct((2, 1024), F32)],
        in_specs=[SCALARS]
        + [WHOLE] * (len(chunks) + len(others) + 7)
        + [FAR] * (len(saved) - 1 + len(earlier)),
        out_specs=[WHOLE] * (3 + parts),
        scratch_shapes=like(saved_shapes)
        + [
            pltpu.VMEM((ROWS, IN), BF),
            pltpu.VMEM((ROWS, 2 * HD), BF),
            pltpu.VMEM((ROWS, 2 * HD), BF),
            pltpu.VMEM((HD, ROWS), BF),
            pltpu.VMEM((ROWS, HD), BF),
            pltpu.VMEM((1, ROWS), F32),
            pltpu.VMEM((HD, ROWS), F32),
            pltpu.VMEM((ROWS, 2 * HD), F32),
            pltpu.VMEM((ROWS, HD), F32),
            pltpu.VMEM((SUMMED, 1024), BF),
            pltpu.SemaphoreType.DMA((5,)),
        ],
        compiler_params=limit(B_LIMIT + 4 * separate),
        cost_estimate=pl.CostEstimate(
            flops=18 * 10**9, bytes_accessed=2**24, transcendentals=ROWS * ROWS
        ),
        name="backward",
    )(
        place["scalars"],
        *chunks,
        *others,
        layer["w_in"],
        layer["w_out"],
        layer["kept"],
        layer["norm"],
        saved[0],
        place["cosine"],
        place["sine"],
        *saved[1:],
        *earlier,
    )
    return outs[:2], outs[2:-1], outs[-1]


def pack(weights, vectors, earlier):
    return pl.pallas_call(
        pack_kernel,
        out_shape=[jax.ShapeDtypeStruct((PACKED, 1024), BF)] * 2,
        in_specs=[FAR] * 4 + [WHOLE] * 6 + [FAR],
        out_specs=[FAR] * 2,
        scratch_shapes=[
            pltpu.VMEM((1024, FF_HERE), BF),
            pltpu.VMEM((PACKED, 1024), BF),
            pltpu.SemaphoreType.DMA((4,)),
        ],
        compiler_params=limit(PACK_LIMIT),
        name="pack",
    )(*weights, *vectors, earlier)


def unpack(flag, first, second):
    w_in, kept, w_out, bias_in, norm = pl.pallas_call(
        unpack_kernel,
        out_shape=[
            jax.ShapeDtypeStruct((IN, 1024), BF),
            jax.ShapeDtypeStruct((IN, 1024), BF),
            jax.ShapeDtypeStruct((OUT, 1024), BF),
            jax.ShapeDtypeStruct((1, IN), F32),
            jax.ShapeDtypeStruct((3, 1024), F32),
        ],
        in_specs=[SCALARS] + [FAR] * 2,
        out_specs=[WHOLE] * 5,
        scratch_shapes=[pltpu.VMEM((PACKED, 1024), BF), pltpu.SemaphoreType.DMA],
        compiler_params=limit(16),
        name="unpack",
    )(flag, first, second)
    return {"w_in": w_in, "kept": kept, "w_out": w_out, "bias_in": bias_in, "norm": norm}


def finish(scalars, quarters):
    return pl.pallas_call(
        finish_kernel,
        out_shape=[
            jax.ShapeDtypeStruct((1024, FF_HERE), F32),
            jax.ShapeDtypeStruct((QKV, 1024), F32),
            jax.ShapeDtypeStruct((FF_HERE, 1024), F32),
            jax.ShapeDtypeStruct((HD, 1024), F32),
            jax.ShapeDtypeStruct((8, 1024), F32),
            jax.ShapeDtypeStruct((8, 1024), F32),
        ],
        in_specs=[SCALARS] + [WHOLE] * 4,
        out_specs=[WHOLE] * 6,
        scratch_shapes=[pltpu.VMEM((SUMMED, 1024), BF)],
        compiler_params=limit(16),
        name="finish",
    )(scalars, *quarters)


def gate(values, *earlier):
    n = len(values)
    return pl.pallas_call(
        gate_kernel,
        out_shape=[jax.ShapeDtypeStruct(value.shape, value.dtype) for value in values],
        in_specs=[FAR] * (n + len(earlier)),
        out_specs=[FAR] * n,
        input_output_aliases={k: k for k in range(n)},
        compiler_params=limit(1),
        name="gate",
    )(*values, *earlier)


def add(own, other, n_out, *earlier):
    with_vectors = own.shape[0] > ROWS // 2
    size = ROWS // 2 // n_out + 16 * with_vectors
    return pl.pallas_call(
        functools.partial(add_kernel, n_out, with_vectors),
        out_shape=[
            jax.ShapeDtypeStruct((size, 1024), BF if k else F32) for k in range(n_out)
        ],
        in_specs=[WHOLE] * 2 + [FAR] * len(earlier),
        out_specs=[WHOLE] * n_out,
        compiler_params=SMALL,
        name="add",
    )(own, other, *earlier)


def fold(total, arrived, *earlier):
    size = (total.shape[0] - 16) // 2 + 16 if total.shape[0] > 2 * BLOCK else BLOCK
    return pl.pallas_call(
        fold_kernel,
        out_shape=[
            jax.ShapeDtypeStruct((size, 1024), F32),
            jax.ShapeDtypeStruct((size, 1024), BF),
        ],
        in_specs=[WHOLE] * 4 + [FAR] * len(earlier),
        out_specs=[WHOLE] * 2,
        compiler_params=SMALL,
        name="fold",
    )(total, *arrived, *earlier)


def join(quarter, mine, pair):
    return pl.pallas_call(
        join_kernel,
        out_shape=jax.ShapeDtypeStruct((SUMMED // 4 + 16, 1024), BF),
        in_specs=[WHOLE] * 3,
        out_specs=WHOLE,
        compiler_params=SMALL,
        name="join",
    )(quarter, mine, pair)


def close_forward(parts, rows, norm):
    shape = (BLOCK, 1024)
    return pl.pallas_call(
        close_forward_kernel,
        out_shape=[
            jax.ShapeDtypeStruct(shape, F32),
            jax.ShapeDtypeStruct(shape, BF),
            jax.ShapeDtypeStruct(shape, BF),
        ],
        in_specs=[WHOLE] * (len(parts) + 2),
        out_specs=[WHOLE] * 3,
        compiler_params=SMALL,
        name="close_forward",
    )(*parts, rows, norm)


def close_backward(parts, rows, grad_rows, *earlier):
    shape = (BLOCK, 1024)
    return pl.pallas_call(
        functools.partial(close_backward_kernel, len(parts)),
        out_shape=[jax.ShapeDtypeStruct(shape, F32), jax.ShapeDtypeStruct(shape, BF)],
        in_specs=[WHOLE] * (len(parts) + 2) + [FAR] * len(earlier),
        out_specs=[WHOLE] * 2,
        compiler_params=SMALL,
        name="close_backward",
    )(*parts, rows, grad_rows, *earlier)


def rotary_lanes(starts):
    lane = jnp.arange(2 * HD, dtype=jnp.int32) % HD
    inverse = jnp.power(10000.0, -2.0 * (lane % (ROT // 2)).astype(F32) / ROT)
    inverse = jnp.where(lane < ROT, inverse, 0.0)[None, :]
    coarse = (jnp.arange(0, ROWS, 64, dtype=jnp.int32) - starts[::64]).astype(F32)[:, None] * inverse
    fine = jnp.arange(64, dtype=jnp.int32).astype(F32)[:, None] * inverse
    cos_a, sin_a = jnp.cos(coarse)[:, None, :], jnp.sin(coarse)[:, None, :]
    cos_b, sin_b = jnp.cos(fine)[None], jnp.sin(fine)[None]
    shape = (ROWS, 2 * HD)
    return (
        (cos_a * cos_b - sin_a * sin_b).reshape(shape),
        (sin_a * cos_b + cos_a * sin_b).reshape(shape),
    )


def over_dp(part, steps):
    return lax.ppermute(part, "dp", [(i, (i + steps) % 4) for i in range(4)])


def shares_from_dp(shares):
    return [shares[0]] + [over_dp(part, steps) for part, steps in zip(shares[1:], (1, 3, 2))]


def exchanged(kept, given, flip):
    arrived = lax.ppermute(given, "dp", [(i, i ^ flip) for i in range(4)])
    return (kept.astype(F32) + arrived.astype(F32)).astype(BF)


def quarter_sum(shares):
    total = shares[0].astype(F32)
    for share in shares[1:]:
        total += share.astype(F32)
    return total.astype(BF)


def body(
    inputs,
    seq_lengths,
    cotangent,
    ln_gain,
    ln_bias,
    w_qkv,
    b_qkv,
    w_out,
    b_out,
    w_up,
    b_up,
    w_down,
    b_down,
):
    core, z, y = (lax.axis_index(name) for name in DEVICES)
    on_first = core == 0
    micro = jnp.where((y == 0) | (y == 3), 0, 1)
    on_micro_0 = micro == 0
    sent = jnp.where(on_first, micro, 1 - micro)

    def pick(value, index):
        return lax.dynamic_index_in_dim(value, index, 0, keepdims=False)

    sent_rows = pick(inputs, sent)
    scaled_rows = normalize(sent_rows.astype(F32))[0].astype(BF)
    scaled = from_arguments(scaled_rows, on_first)
    chunks_0 = gather_pieces(scaled)
    later_rows, later_grads = gate([sent_rows, pick(cotangent, sent)], scaled)
    rows_0 = jnp.where(on_first, later_rows, send(later_rows, OVER))
    both = from_arguments(later_grads, on_first)
    grad_rows_1 = both[:BLOCK]

    weights = (w_up[0], w_qkv.reshape(1024, QKV).T, w_down[0], w_out[0])
    small = (b_up, b_qkv[0], ln_gain, ln_bias, b_out, b_down)
    mine, again = pack(weights, small, scaled_rows)
    swapped = send(mine, SWAP)
    flag = jnp.where(on_first, 1, 0).astype(jnp.int32)
    layer_0 = unpack(flag[None], mine, swapped)

    starts = start_rows(pick(seq_lengths, micro), ROWS)
    cosine, sine = rotary_lanes(starts)
    scalars = [
        gathered_blocks(core, z, y),
        starts[::SPAN] // SPAN,
        lax.axis_index("dp")[None],
    ]
    place = {
        "scalars": jnp.concatenate([part.astype(jnp.int32) for part in scalars]),
        "cosine": cosine,
        "sine": sine,
    }

    (early,) = gate([both], chunks_0[3])
    pieces = [early] + [send(early, table(step(hops))) for hops in RING[:2]]
    halves_0, saved_0 = forward(chunks_0, layer_0, place, True)
    (other_0,) = gate([halves_0[1]], *pieces[1:])
    total, *blocks = add(halves_0[0], send(other_0, SIBLING), 8)
    arrived = scatter(blocks)
    result_0, rows_1, scaled_rows = close_forward([total] + arrived, rows_0, layer_0["norm"])
    (again,) = gate([again], rows_1)
    over = send(again, OVER)
    layer_1 = unpack(flag[None], swapped, over)
    chunks_1 = gather(scaled_rows)
    (late,) = gate([both], chunks_1[5])
    pieces.append(send(late, table(step(RING[2]))))
    halves_1, saved_1 = forward(chunks_1, layer_1, place, False)

    result_0_there = send(result_0, BACK_OVER)
    pieces[3:] = gate(pieces[3:], halves_1[0])
    grad_halves_1, halves_of_1, vectors_1 = backward(
        with_sibling(pieces), chunks_1, layer_1, saved_1, place, result_0_there
    )
    total, *blocks = add(grad_halves_1[0], send(grad_halves_1[1], SIBLING), 4)
    (other_1,) = gate([halves_1[1]], blocks[0])
    first, *pieces = add(halves_1[0], send(other_1, SIBLING), 4)
    (given,) = gate([halves_of_1[1]], blocks[0])
    half_1 = exchanged(halves_of_1[0], given, 1)
    mine, pair = fold(total, scatter_pieces(blocks))
    pair = send(pair, table(step(0, PAIR)))
    grad_input_1, grad_rows_0 = close_backward([mine, pair], rows_1, grad_rows_1)
    grad_chunks_0 = gather(grad_rows_0)
    n = SUMMED // 4
    share_1 = exchanged(half_1[:n], half_1[n:], 2)
    quarter_1 = (send(share_1, SIBLING).astype(F32) + send(share_1, OVER).astype(F32)).astype(BF)

    pieces = scatter_pieces(gate(pieces, grad_chunks_0[5]))
    grad_input_1_here = send(grad_input_1, SIBLING)
    grad_input_1_there = send(grad_input_1, OVER)

    rows_sums = [
        jnp.sum(rows.astype(F32), axis=0, keepdims=True) for rows in (grad_rows_0, grad_rows_1)
    ]
    grad_halves_0, shares_0, unused_vectors = backward(
        grad_chunks_0,
        [rows_sums[0], vectors_1, rows_sums[1]],
        layer_0,
        saved_0,
        place,
        quarter_1,
        grad_input_1_here,
        grad_input_1_there,
    )
    (other_0,) = gate([grad_halves_0[1]], *pieces)
    total, *blocks = add(grad_halves_0[0], send(other_0, SIBLING), 4)
    shares_0 = shares_from_dp(shares_0)
    share_0 = quarter_sum(shares_0)
    mine_0 = (share_0.astype(F32) + send(share_0, BACK_OVER).astype(F32)).astype(BF)
    quarter = jnp.where(on_first, mine_0, quarter_1)
    mine, pair = fold(total, scatter_pieces(blocks), *shares_0[1:])
    mine_1, pair_1 = fold(first, pieces)
    result_1, unused_rounded, unused_rows = close_forward(
        [mine_1, send(pair_1, table(step(0, PAIR)))], rows_1, layer_1["norm"]
    )
    pair = send(pair, table(step(0, PAIR)))
    grad_input_0, unused_rounded = close_backward([mine, pair], rows_0, grad_rows_0)
    quarter = join(quarter, mine, pair)
    quarters = [quarter] + [over_dp(quarter, steps) for steps in (1, 2, 3)]
    grad_input_0_there = send(grad_input_0, BACK_OVER)
    grad_up, grad_qkv, grad_down, grad_out, grad_biases, vectors = finish(
        place["scalars"], quarters
    )
    vectors = vectors + send(vectors, table(step(0, 1)))
    vectors = jnp.where(on_first, vectors[:3], vectors[3:6])

    def output_of(value_0, there_0, here_1, there_1):
        here = jnp.where(on_first, value_0, here_1)
        there = jnp.where(on_first, there_0, there_1)
        return jnp.stack(
            [jnp.where(on_micro_0, here, there), jnp.where(on_micro_0, there, here)]
        )[None]

    return (
        output_of(
            result_0, result_0_there, send(result_1, SIBLING), send(result_1, OVER)
        ),
        output_of(
            grad_input_0,
            grad_input_0_there,
            grad_input_1_here,
            grad_input_1_there,
        ),
        vectors[0:1],
        vectors[1:2],
        grad_qkv.T.reshape(1, 1024, 1, QKV),
        grad_biases[0, FF_HERE:IN].reshape(1, 1, QKV),
        grad_out[None],
        vectors[2:3],
        grad_up[None],
        grad_biases[0:1, :FF_HERE],
        grad_down[None],
        vectors[2:3],
    )


def solution(mesh):
    rows = P("dp", ("z", "y"), None)
    layer_rows = P("pipe", "dp", ("z", "y"), None)
    heads = P("pipe", None, ("z", "y"), None)
    split = P("pipe", ("z", "y"), None)
    units = P("pipe", None, ("z", "y"))
    whole = P("pipe", None)
    unit_bias = P("pipe", ("z", "y"))
    return jax.shard_map(
        body,
        mesh=Mesh(mesh.devices.reshape(2, 4, 4, 4), ("pipe", "dp", "z", "y")),
        in_specs=(
            rows,
            P("dp", None),
            rows,
            whole,
            whole,
            heads,
            split,
            split,
            whole,
            units,
            unit_bias,
            split,
            whole,
        ),
        out_specs=(
            layer_rows,
            layer_rows,
            whole,
            whole,
            heads,
            split,
            split,
            whole,
            units,
            unit_bias,
            split,
            whole,
        ),
        check_vma=False,
    )
```

```python
import functools

import jax
import jax.numpy as jnp
from jax import lax
from jax.experimental import pallas as pl
from jax.experimental.pallas import tpu as pltpu
from jax.sharding import Mesh, PartitionSpec as P

HD = 64
ROT = 16
FF_HERE = 256
QKV = 3 * HD
IN = FF_HERE + QKV
OUT = FF_HERE + HD
PACKED = IN + 16 + OUT
SUMMED = 832
MIXED = 384
F_LIMIT = 14
B_LIMIT = 23
PACK_LIMIT = 56
FOLD_COST = 30 * 10**9
ROWS = 2048
BLOCK = 128
SPAN = 512
SPANS = ROWS // SPAN
PER_SPAN = SPAN // BLOCK
EPSILON = 1e-05
NEGATIVE = -1e30
ROOT_HALF = 0.7071067811865476
INV_ROOT_TAU = 0.3989422804014327
DEVICES = ("pipe", "z", "y")
BF = jnp.bfloat16
F32 = jnp.float32


def table(rule):
    pairs = []
    for core in range(2):
        for z in range(4):
            for y in range(4):
                target = rule(core, z, y)
                if target is not None:
                    to_core, to_z, to_y = target
                    pairs.append((core * 16 + z * 4 + y, to_core * 16 + to_z % 4 * 4 + to_y))
    return pairs


def by_core(first, second):
    return table(lambda core, z, y: (first if core == 0 else second)(core, z, y))


def step(steps, flip=0):
    return lambda core, z, y: (core, z + steps, y ^ flip)


def nowhere(core, z, y):
    return None


PAIR = 3
SIBLING = table(lambda core, z, y: (1 - core, z, y))
OVER = by_core(nowhere, step(0, 1))
BACK_OVER = by_core(nowhere, lambda core, z, y: (0, z, y ^ 1))
SWAP = by_core(lambda core, z, y: (1, z, y ^ 1), lambda core, z, y: (0, z, y))
RING = (1, -1, 2)


def send(value, pairs):
    return lax.ppermute(value, DEVICES, pairs)


def gathered_blocks(core, z, y):
    def of(own):
        columns = (y ^ own, y ^ own ^ PAIR)
        steps = [0] + [-hops for hops in RING]
        return [(z + hops) % 4 * 4 + column for column in columns for hops in steps]

    first, second = jnp.stack(of(0)), jnp.stack(of(1))
    return jnp.where(
        core == 0, jnp.concatenate([first, second]), jnp.concatenate([second, first])
    ).astype(jnp.int32)


def with_sibling(blocks):
    return blocks + [send(block, SIBLING) for block in blocks]


def gather(rows):
    pair = send(rows, table(step(0, PAIR)))
    own = [send(rows, table(step(hops))) for hops in RING]
    far = [send(pair, table(step(hops))) for hops in RING]
    return with_sibling([rows] + own + [pair] + far)


def from_arguments(rows, on_first):
    near = send(rows, by_core(step(0, PAIR), step(0, 1)))
    beside = send(rows, by_core(nowhere, step(0, 2)))
    return jnp.concatenate([jnp.where(on_first, rows, near), jnp.where(on_first, near, beside)])


def gather_pieces(both):
    return with_sibling([both] + [send(both, table(step(hops))) for hops in RING])


def scatter(blocks):
    steps = [(-hops, 0) for hops in RING] + [(0, PAIR)] + [(-hops, PAIR) for hops in RING]
    return [send(block, table(step(hops, flip))) for block, (hops, flip) in zip(blocks, steps)]


def scatter_pieces(pieces):
    return [send(piece, table(step(-hops))) for piece, hops in zip(pieces, RING)]


def start_rows(lengths, total_rows):
    endings = jnp.cumsum(lengths)
    places = jnp.arange(total_rows, dtype=jnp.int32)
    passed = places[:, None] >= endings[None, :]
    return jnp.sum(jnp.where(passed, lengths[None, :], 0), axis=1)


def normalize(rows):
    average = jnp.mean(rows, axis=-1, keepdims=True)
    centred = rows - average
    inverse_std = lax.rsqrt(jnp.mean(centred * centred, axis=-1, keepdims=True) + EPSILON)
    return centred * inverse_std, inverse_std


def normalize_back(grad_rows, grad_scaled, rows):
    scaled, inverse_std = normalize(rows.astype(F32))
    return grad_rows.astype(F32) + inverse_std * (
        grad_scaled
        - jnp.mean(grad_scaled, axis=-1, keepdims=True)
        - scaled * jnp.mean(grad_scaled * scaled, axis=-1, keepdims=True)
    )


def block_of(index):
    return pl.ds(pl.multiple_of(index * BLOCK, BLOCK), BLOCK)


def dot(left, right, left_axis=1, right_axis=0):
    return lax.dot_general(
        left, right, (((left_axis,), (right_axis,)), ((), ())), preferred_element_type=F32
    )


def started(parts, sems, first):
    copies = [pltpu.make_async_copy(*part, sems.at[first + k]) for k, part in enumerate(parts)]
    for copy in copies:
        copy.start()
    return copies


def finished(copies):
    for copy in copies:
        copy.wait()


def stacked(refs, group, first):
    return jnp.concatenate(
        [refs[group * PER_SPAN + k][first : first + BLOCK] for k in range(PER_SPAN)]
    )


def chunk_of(refs, group):
    if len(refs) == 16:
        return stacked(refs, group, 0)
    pieces = refs[group // 2 * PER_SPAN : (group // 2 + 1) * PER_SPAN]
    return stacked(pieces, 0, group % 2 * BLOCK)


def half_of(refs, group):
    place = group % (SPANS // 2) * SPAN
    return refs[group // (SPANS // 2)].at[pl.ds(place, SPAN)]


def turned(pairs):
    lane = lax.broadcasted_iota(jnp.int32, pairs.shape, 1) % HD
    return jnp.where(
        lane < ROT // 2, -pltpu.roll(pairs, 2 * HD - ROT // 2, 1), pltpu.roll(pairs, ROT // 2, 1)
    )


def halves(pairs):
    lane = lax.broadcasted_iota(jnp.int32, pairs.shape, 1)
    queries = jnp.where(lane < HD, pairs * HD ** (-0.5), 0.0)
    return queries.astype(BF), pltpu.roll(pairs, HD, 1).astype(BF)


def penalty(scalars_ref, query_span, key_span):
    return jnp.where(key_span >= scalars_ref[16 + query_span], 0.0, -NEGATIVE).astype(F32)


def seen(scores):
    keys = lax.broadcasted_iota(jnp.int32, scores.shape, 0)
    queries = lax.broadcasted_iota(jnp.int32, scores.shape, 1)
    return jnp.where(keys <= queries, scores, NEGATIVE)


def store_parts(store_ref, saved_refs):
    lanes = (0, MIXED, MIXED + FF_HERE, MIXED + FF_HERE + 2 * HD)
    places = [
        store_ref.at[pl.ds(ROWS, ROWS), pl.ds(lane, ref.shape[1])]
        for lane, ref in zip(lanes, saved_refs)
    ]
    return places + [store_ref.at[pl.ds(0, ROWS)]]


def forward_kernel(n_chunks, stored, *refs):
    scalars_ref = refs[0]
    chunk_refs, refs = refs[1 : 1 + n_chunks], refs[1 + n_chunks :]
    w_in_ref, bias_ref, w_out_ref, cosine_ref, sine_ref = refs[:5]
    half_refs, log_sums_ref, refs = refs[5:7], refs[7], refs[8:]
    kept_hbm, kept_refs, refs = refs[:-9], refs[-9:-5], refs[-5:]
    mixed_ref, slope_ref, pairs_ref, values_ref = kept_refs
    queries_ref, keys_ref, turned_values_ref, ordered_ref, sems = refs
    copies = []
    if stored:
        kept_hbm = store_parts(kept_hbm[0], kept_refs)
        parts = []
        for k in range(16):
            source = chunk_refs[k // 8 * 4 + k % 4].at[pl.ds(k % 8 // 4 * BLOCK, BLOCK)]
            parts.append((source, kept_hbm[4].at[pl.ds(k * BLOCK, BLOCK)]))
        copies = started(parts, sems, 0)
    for group in range(SPANS):
        rows = slice(group * SPAN, (group + 1) * SPAN)
        projected = dot(chunk_of(chunk_refs, group), w_in_ref[...], 1, 1) + bias_ref[...]
        inner = projected[:, :FF_HERE]
        wave = 1.0 + lax.erf(inner * ROOT_HALF)
        mixed_ref[rows, :FF_HERE] = (0.5 * inner * wave).astype(BF)
        slope = 0.5 * wave + inner * jnp.exp(-0.5 * inner * inner) * INV_ROOT_TAU
        slope_ref[rows] = slope.astype(BF)
        for k in range(PER_SPAN):
            joined = projected[k * BLOCK : (k + 1) * BLOCK, FF_HERE:]
            place = block_of(scalars_ref[group * PER_SPAN + k])
            pairs = joined[:, : 2 * HD]
            pairs = pairs * cosine_ref[place] + turned(pairs) * sine_ref[place]
            pairs_ref[place] = pairs.astype(BF)
            queries_ref[place], keys_ref[place] = halves(pairs.astype(BF).astype(F32))
            values = joined[:, 2 * HD :]
            values_ref[place, :HD] = values.astype(BF)
            turned_values_ref[:, place] = values.T.astype(BF)
    for i in range(SPANS):
        span = slice(i * SPAN, (i + 1) * SPAN)
        queries = queries_ref[span]
        scores, offsets, highest = [], [], None
        for j in range(i + 1):
            block = dot(keys_ref[j * SPAN : (j + 1) * SPAN], queries, 1, 1)
            block = seen(block) if i == j else block
            offset = 0.0 if i == j else penalty(scalars_ref, i, j)
            top = jnp.max(block, axis=0, keepdims=True) - offset
            highest = top if highest is None else jnp.maximum(highest, top)
            scores.append(block)
            offsets.append(offset)
        total, summed = 0.0, 0.0
        for j in range(i + 1):
            exponent = jnp.exp(scores[j] - (highest + offsets[j]))
            total = total + jnp.sum(exponent, axis=0, keepdims=True)
            summed = summed + dot(
                turned_values_ref[:, j * SPAN : (j + 1) * SPAN], exponent.astype(BF)
            )
        log_sums_ref[:, span] = highest + jnp.log(total)
        ordered_ref[span] = (summed / total).T.astype(BF)
    for group in range(SPANS):
        for k in range(PER_SPAN):
            index = group * PER_SPAN + k
            here = slice(index * BLOCK, (index + 1) * BLOCK)
            mixed_ref[here, FF_HERE:OUT] = ordered_ref[block_of(scalars_ref[index])]
        rows = slice(group * SPAN, (group + 1) * SPAN)
        half_of(half_refs, group)[...] = dot(mixed_ref[rows, :OUT], w_out_ref[...]).astype(BF)
    copies += started(list(zip(kept_refs, kept_hbm)), sems, 16)
    finished(copies)


def backward_kernel(separate, n_earlier, *refs):
    scalars_ref = refs[0]
    count = 16 if separate else 8
    chunk_refs, refs = refs[1 : 1 + count], refs[1 + count :]
    feature_refs, given_refs = [], None
    if separate:
        given_refs, refs = refs[:3], refs[3:]
    else:
        feature_refs, refs = refs[:16], refs[16:]

    w_in_ref, w_out_ref, kept_ref, norm_ref, log_sums_ref, cosine_ref, sine_ref = refs[:7]
    count = 5 if separate else 4
    n_saved = 1 if separate else 4
    saved_hbm, refs = refs[7 : 7 + n_saved], refs[7 + n_saved + n_earlier :]
    n_parts = 4 if separate else 2
    half_refs, quarter_refs, refs = refs[:2], refs[2 : 2 + n_parts], refs[2 + n_parts :]
    vectors_ref, refs = refs[0], refs[1:]
    saved_refs, refs = refs[:count], refs[count:]
    mixed_ref, slope_ref, pairs_ref, values_ref = saved_refs[:4]
    features_ref = saved_refs[-1]
    grad_in_ref, queries_ref, keys_ref, turned_keys_ref, grad_heads_ref, products_ref = refs[:6]
    grad_queries_ref, grad_keys_ref, grad_values_ref, grads_ref, sems = refs[6:]
    if separate:
        saved_hbm = store_parts(saved_hbm[0], saved_refs[:4])
    copies = started(list(zip(saved_hbm, saved_refs)), sems, 0)
    finished(copies[:4])
    for group in range(SPANS):
        rows = slice(group * SPAN, (group + 1) * SPAN)
        grad_mixed = dot(chunk_of(chunk_refs, group), w_out_ref[...], 1, 1)
        grad_in_ref[rows, :FF_HERE] = (
            grad_mixed[:, :FF_HERE] * slope_ref[rows].astype(F32)
        ).astype(BF)
        for k in range(PER_SPAN):
            index = group * PER_SPAN + k
            here, place = slice(index * BLOCK, (index + 1) * BLOCK), block_of(scalars_ref[index])
            grad_heads = grad_mixed[k * BLOCK : (k + 1) * BLOCK, FF_HERE:].astype(BF)
            grad_heads_ref[place] = grad_heads
            product = grad_heads.astype(F32) * mixed_ref[here, FF_HERE:OUT].astype(F32)
            products_ref[:, place] = jnp.sum(product.T, axis=0, keepdims=True)
            queries_ref[here], keys = halves(pairs_ref[here].astype(F32))
            keys_ref[here] = keys
            turned_keys_ref[:, here] = keys[:, :HD].astype(F32).T.astype(BF)
    grad_queries_ref[...] = jnp.zeros_like(grad_queries_ref)
    for j in range(SPANS):
        key_span = slice(j * SPAN, (j + 1) * SPAN)
        keys, values = keys_ref[key_span], values_ref[key_span, :HD]
        grad_keys, grad_values = 0.0, 0.0
        for i in range(j, SPANS):
            span = slice(i * SPAN, (i + 1) * SPAN)
            queries, grad_heads = queries_ref[span], grad_heads_ref[span]
            scores = dot(keys, queries, 1, 1)
            scores = seen(scores) if i == j else scores
            offset = 0.0 if i == j else penalty(scalars_ref, i, j)
            probability = jnp.exp(scores - (log_sums_ref[:, span] + offset))
            grad_values += dot(probability.astype(BF), grad_heads)
            grad_probs = dot(values, grad_heads, 1, 1)
            grad_scores = (probability * (grad_probs - products_ref[:, span])).astype(BF)
            grad_keys += dot(grad_scores, queries)
            grad_queries_ref[:, span] += dot(turned_keys_ref[:, key_span], grad_scores)
        grad_keys_ref[key_span] = grad_keys
        grad_values_ref[key_span] = grad_values
    for group in range(SPANS):
        for k in range(PER_SPAN):
            index = group * PER_SPAN + k
            here, place = slice(index * BLOCK, (index + 1) * BLOCK), block_of(scalars_ref[index])
            grad_queries = (grad_queries_ref[:, place] * HD ** (-0.5)).T
            grad_pairs = jnp.concatenate([grad_queries, grad_keys_ref[place, :HD]], axis=1)
            grad_pairs = grad_pairs * cosine_ref[place] - turned(grad_pairs) * sine_ref[place]
            grad_in_ref[here, FF_HERE : FF_HERE + 2 * HD] = grad_pairs.astype(BF)
            grad_in_ref[here, FF_HERE + 2 * HD :] = grad_values_ref[place].astype(BF)
        rows = slice(group * SPAN, (group + 1) * SPAN)
        half_of(half_refs, group)[...] = dot(grad_in_ref[rows], w_in_ref[...]).astype(BF)
    finished(copies[4:])
    raw, after, columns = 0.0, 0.0, 0.0
    ones = jnp.ones((SPAN, BLOCK), BF)
    total = jnp.zeros((1, IN), F32)
    for group in range(SPANS):
        rows = slice(group * SPAN, (group + 1) * SPAN)
        grad_in = grad_in_ref[rows]
        features = features_ref[rows] if separate else stacked(feature_refs, group, 0)
        raw += dot(grad_in, features, 0, 0)
        columns += dot(grad_in, ones, 0, 0)
        total += jnp.sum(grad_in.astype(F32), axis=0, keepdims=True)
        after += dot(mixed_ref[rows, :OUT], chunk_of(chunk_refs, group), 0, 0)
    kept = kept_ref[...].astype(F32)
    gain, shift = norm_ref[0:1], norm_ref[1:2]
    column = columns[:, :1]
    grads_ref[:IN] = (raw * gain + column * shift).astype(BF)
    grads_ref[IN : IN + 16] = jnp.zeros((16, 1024), BF)
    grads_ref[IN : IN + 1, :IN] = total.astype(BF)
    grads_ref[IN + 16 : PACKED] = after.astype(BF)
    grads_ref[PACKED:] = jnp.zeros((SUMMED - PACKED, 1024), BF)
    n = SUMMED // 4

    def quarter(index):
        return grads_ref[pl.ds(pl.multiple_of(index * n, 16), n)]

    here = scalars_ref[20]
    if separate:
        for ref, steps in zip(quarter_refs, (0, 1, 3, 2)):
            ref[...] = quarter(lax.rem(here + steps, 4))
    else:
        for ref, first in zip(quarter_refs, (here, here ^ 1)):
            ref[:n] = quarter(first)
            ref[n:] = quarter(first ^ 2)
    grad_gain = jnp.sum(raw * kept, axis=0, keepdims=True)
    grad_shift = jnp.sum(column * kept, axis=0, keepdims=True)
    if not separate:
        vectors_ref[0:1] = grad_gain
        vectors_ref[1:2] = grad_shift
        return
    row = lax.broadcasted_iota(jnp.int32, (8, 1024), 0)
    rows_ref, norm_1_ref, rows_1_ref = given_refs
    parts = (grad_gain, grad_shift, rows_ref[...], norm_1_ref[0:1], norm_1_ref[1:2], rows_1_ref[...])
    vectors = jnp.zeros((8, 1024), F32)
    for k, part in enumerate(parts):
        vectors = jnp.where(row == k, part, vectors)
    high = vectors.astype(BF).astype(F32)
    vectors = jnp.concatenate([high, vectors - high]).astype(BF)
    for ref in half_refs:
        ref[ROWS // 2 :] = vectors


def pack_kernel(*refs):
    up_hbm, qkv_hbm, down_hbm, out_hbm, b_up_ref, b_qkv_ref, gain_ref, shift_ref = refs[:8]
    b_out_ref, b_down_ref, unused_ref, *packed_hbm, up_ref, packed_ref, sems = refs[8:]
    parts = [
        (up_hbm, up_ref),
        (qkv_hbm, packed_ref.at[pl.ds(FF_HERE, QKV)]),
        (down_hbm, packed_ref.at[pl.ds(IN + 16, FF_HERE)]),
        (out_hbm, packed_ref.at[pl.ds(IN + 16 + FF_HERE, HD)]),
    ]
    copies = started(parts, sems, 0)
    biases = jnp.concatenate(
        [b_up_ref[...], b_qkv_ref[...], jnp.zeros((1, 1024 - IN), F32)], axis=1
    )
    rows = lax.broadcasted_iota(jnp.int32, (16, 1024), 0)
    small = jnp.zeros((16, 1024), F32)
    for value, high_row, low_row in (
        (biases, 0, 1),
        (gain_ref[...], 2, 5),
        (shift_ref[...], 3, 6),
        (b_out_ref[...] + b_down_ref[...], 4, 7),
    ):
        high = value.astype(BF).astype(F32)
        small = jnp.where(rows == high_row, high, small)
        small = jnp.where(rows == low_row, value - high, small)
    packed_ref[IN : IN + 16] = small.astype(BF)
    copies[0].wait()
    packed_ref[:FF_HERE] = up_ref[...].T
    finished(copies[1:])
    finished(started([(packed_ref, target) for target in packed_hbm], sems, 0))


def unpack_kernel(
    flag_ref, first_hbm, second_hbm, w_in_ref, kept_ref, w_out_ref, bias_ref, norm_ref, packed_ref, sem
):
    @pl.when(flag_ref[0] == 1)
    def _():
        copy = pltpu.make_async_copy(first_hbm, packed_ref, sem)
        copy.start()
        copy.wait()

    @pl.when(flag_ref[0] != 1)
    def _():
        copy = pltpu.make_async_copy(second_hbm, packed_ref, sem)
        copy.start()
        copy.wait()

    w_in = packed_ref[:IN]
    small = packed_ref[IN : IN + 16]
    shifts = dot(small, w_in, 1, 1)
    small = small.astype(F32)
    norm_ref[0:3] = small[2:5] + small[5:8]
    bias_ref[...] = small[0:1, :IN] + small[1:2, :IN] + shifts[3:4] + shifts[6:7]
    kept_ref[...] = w_in
    w_in_ref[...] = (w_in.astype(F32) * norm_ref[0:1]).astype(BF)
    w_out_ref[...] = packed_ref[IN + 16 : PACKED]


def finish_kernel(scalars_ref, *refs):
    up_ref, qkv_ref, down_ref, out_ref, b_up_ref, b_qkv_ref, whole_ref = refs[4:]
    n = SUMMED // 4
    for k in range(4):
        place = lax.rem(scalars_ref[20] + 4 - k, 4)
        whole_ref[pl.ds(pl.multiple_of(place * n, 16), n)] = refs[k][:n]
    up_ref[...] = whole_ref[:FF_HERE].astype(F32).T
    qkv_ref[...] = whole_ref[FF_HERE:IN].astype(F32)
    biases = whole_ref[IN : IN + 16].astype(F32)[0:1]
    b_up_ref[...] = biases[:, :FF_HERE]
    b_qkv_ref[...] = biases[:, FF_HERE:IN]
    down_ref[...] = whole_ref[IN + 16 : IN + 16 + FF_HERE].astype(F32)
    out_ref[...] = whole_ref[IN + 16 + FF_HERE : PACKED].astype(F32)


def vectors_kernel(*refs):
    n = SUMMED // 4
    total = 0.0
    for ref in refs[:4]:
        total += ref[n : n + 8].astype(F32) + ref[n + 8 :].astype(F32)
    refs[4][...] = total


def norms_kernel(flag_ref, mine_ref, there_ref, gain_ref, shift_ref, b_out_ref, b_down_ref):
    total = mine_ref[...] + there_ref[...]
    mine = jnp.where(flag_ref[0] == 1, total[0:3], total[3:6])
    gain_ref[...] = mine[0:1]
    shift_ref[...] = mine[1:2]
    b_out_ref[...] = mine[2:3]
    b_down_ref[...] = mine[2:3]


def add_kernel(n_out, with_vectors, *refs):
    own_ref, other_ref = refs[:2]
    out_refs = refs[-n_out:]
    count = 8 // n_out
    for k, ref in enumerate(out_refs):
        for part in range(count):
            index = k + part * n_out
            rows = slice(index * BLOCK, (index + 1) * BLOCK)
            value = own_ref[rows].astype(F32) + other_ref[rows].astype(F32)
            ref[part * BLOCK : (part + 1) * BLOCK] = value.astype(ref.dtype)
    if with_vectors:
        rows = slice(ROWS // 2, ROWS // 2 + 16)
        both = own_ref[rows].astype(F32) + other_ref[rows].astype(F32)
        vectors = both[:8] + both[8:]
        high = vectors.astype(BF).astype(F32)
        below = jnp.concatenate([high, vectors - high])
        for ref in out_refs:
            ref[count * BLOCK :] = below.astype(ref.dtype)


def total_of(refs):
    total = refs[0][:BLOCK]
    for ref in refs[1:]:
        total += ref[:BLOCK].astype(F32)
    return total


def close_forward_kernel(*refs):
    rows_ref, norm_ref, result_ref, rounded_ref, scaled_ref = refs[-5:]
    total = total_of(refs[:-5])
    result = rows_ref[...].astype(F32) + total + norm_ref[2:3]
    result_ref[...] = result
    rounded = result.astype(BF)
    rounded_ref[...] = rounded
    scaled_ref[...] = normalize(rounded.astype(F32))[0].astype(BF)


def close_backward_kernel(n_parts, *refs):
    rows_ref, grad_rows_ref = refs[n_parts : n_parts + 2]
    grad_ref, rounded_ref = refs[-2:]
    total = total_of(refs[:n_parts])
    grad = normalize_back(grad_rows_ref[...], total, rows_ref[...])
    grad_ref[...] = grad
    rounded_ref[...] = grad.astype(BF)


def fold_kernel(total_ref, *refs):
    mine_ref, pair_ref = refs[-2:]
    total = total_ref[...]
    for ref in refs[:3]:
        total += ref[...].astype(F32)
    size = mine_ref.shape[0]
    mine_ref[:BLOCK] = total[:BLOCK]
    pair_ref[:BLOCK] = total[BLOCK : 2 * BLOCK].astype(BF)
    if size > BLOCK:
        vectors = total[2 * BLOCK : 2 * BLOCK + 8] + total[2 * BLOCK + 8 :]
        high = vectors.astype(BF).astype(F32)
        mine_ref[BLOCK:] = jnp.concatenate([high, vectors - high])
        pair_ref[BLOCK:] = jnp.concatenate([high, vectors - high]).astype(BF)


def join_kernel(quarter_ref, mine_ref, pair_ref, joined_ref):
    n = SUMMED // 4
    joined_ref[:n] = quarter_ref[...]
    both = mine_ref[BLOCK:] + pair_ref[BLOCK:].astype(F32)
    vectors = both[:8] + both[8:]
    high = vectors.astype(BF).astype(F32)
    joined_ref[n:] = jnp.concatenate([high, vectors - high]).astype(BF)


def gate_kernel(*refs):
    pass


WHOLE = pl.BlockSpec(memory_space=pltpu.VMEM)
SCALARS = pl.BlockSpec(memory_space=pltpu.SMEM)
FAR = pl.BlockSpec(memory_space=pl.ANY)


def limit(size):
    return pltpu.CompilerParams(vmem_limit_bytes=size * 2**20)


SMALL = limit(12)
HALF = jax.ShapeDtypeStruct((ROWS // 2, 1024), BF)
SAVED = [
    jax.ShapeDtypeStruct((ROWS, width), BF) for width in (MIXED, FF_HERE, 2 * HD, 2 * HD, 1024)
]


STORE = jax.ShapeDtypeStruct((10 * ROWS, 1024), BF)


def like(shapes):
    return [pltpu.VMEM(shape.shape, shape.dtype) for shape in shapes]


def forward(chunks, layer, place, stored):
    saved = [STORE] if stored else SAVED[:4]
    outs = pl.pallas_call(
        functools.partial(forward_kernel, len(chunks), stored),
        out_shape=[HALF] * 2 + [jax.ShapeDtypeStruct((1, ROWS), F32)] + saved,
        in_specs=[SCALARS] + [WHOLE] * (len(chunks) + 5),
        out_specs=[WHOLE] * 3 + [FAR] * len(saved),
        scratch_shapes=like(SAVED[:4])
        + [
            pltpu.VMEM((ROWS, 2 * HD), BF),
            pltpu.VMEM((ROWS, 2 * HD), BF),
            pltpu.VMEM((HD, ROWS), BF),
            pltpu.VMEM((ROWS, HD), BF),
            pltpu.SemaphoreType.DMA((20,)),
        ],
        compiler_params=limit(F_LIMIT),
        cost_estimate=pl.CostEstimate(
            flops=12 * 10**9, bytes_accessed=2**24, transcendentals=ROWS * ROWS
        ),
        name="forward",
    )(
        place["scalars"],
        *chunks,
        layer["w_in"],
        layer["bias_in"],
        layer["w_out"],
        place["cosine"],
        place["sine"],
    )
    return outs[:2], outs[2:]


def backward(chunks, others, layer, saved, place, *earlier):
    separate = len(saved) == 2
    saved_shapes = SAVED if separate else SAVED[:4]
    half = (ROWS // 2 + 16 * separate, 1024)
    parts = 4 if separate else 2
    outs = pl.pallas_call(
        functools.partial(backward_kernel, separate, len(earlier)),
        out_shape=[jax.ShapeDtypeStruct(half, BF)] * 2
        + [jax.ShapeDtypeStruct((SUMMED // parts, 1024), BF)] * parts
        + [jax.ShapeDtypeStruct((2, 1024), F32)],
        in_specs=[SCALARS]
        + [WHOLE] * (len(chunks) + len(others) + 7)
        + [FAR] * (len(saved) - 1 + len(earlier)),
        out_specs=[WHOLE] * (3 + parts),
        scratch_shapes=like(saved_shapes)
        + [
            pltpu.VMEM((ROWS, IN), BF),
            pltpu.VMEM((ROWS, 2 * HD), BF),
            pltpu.VMEM((ROWS, 2 * HD), BF),
            pltpu.VMEM((HD, ROWS), BF),
            pltpu.VMEM((ROWS, HD), BF),
            pltpu.VMEM((1, ROWS), F32),
            pltpu.VMEM((HD, ROWS), F32),
            pltpu.VMEM((ROWS, 2 * HD), F32),
            pltpu.VMEM((ROWS, HD), F32),
            pltpu.VMEM((SUMMED, 1024), BF),
            pltpu.SemaphoreType.DMA((5,)),
        ],
        compiler_params=limit(B_LIMIT + 4 * separate),
        cost_estimate=pl.CostEstimate(
            flops=18 * 10**9, bytes_accessed=2**24, transcendentals=ROWS * ROWS
        ),
        name="backward",
    )(
        place["scalars"],
        *chunks,
        *others,
        layer["w_in"],
        layer["w_out"],
        layer["kept"],
        layer["norm"],
        saved[0],
        place["cosine"],
        place["sine"],
        *saved[1:],
        *earlier,
    )
    return outs[:2], outs[2:-1], outs[-1]


def pack(weights, vectors, earlier):
    return pl.pallas_call(
        pack_kernel,
        out_shape=[jax.ShapeDtypeStruct((PACKED, 1024), BF)] * 2,
        in_specs=[FAR] * 4 + [WHOLE] * 6 + [FAR],
        out_specs=[FAR] * 2,
        scratch_shapes=[
            pltpu.VMEM((1024, FF_HERE), BF),
            pltpu.VMEM((PACKED, 1024), BF),
            pltpu.SemaphoreType.DMA((4,)),
        ],
        compiler_params=limit(PACK_LIMIT),
        name="pack",
    )(*weights, *vectors, earlier)


def unpack(flag, first, second):
    w_in, kept, w_out, bias_in, norm = pl.pallas_call(
        unpack_kernel,
        out_shape=[
            jax.ShapeDtypeStruct((IN, 1024), BF),
            jax.ShapeDtypeStruct((IN, 1024), BF),
            jax.ShapeDtypeStruct((OUT, 1024), BF),
            jax.ShapeDtypeStruct((1, IN), F32),
            jax.ShapeDtypeStruct((3, 1024), F32),
        ],
        in_specs=[SCALARS] + [FAR] * 2,
        out_specs=[WHOLE] * 5,
        scratch_shapes=[pltpu.VMEM((PACKED, 1024), BF), pltpu.SemaphoreType.DMA],
        compiler_params=limit(16),
        name="unpack",
    )(flag, first, second)
    return {"w_in": w_in, "kept": kept, "w_out": w_out, "bias_in": bias_in, "norm": norm}


def finish(scalars, quarters):
    return pl.pallas_call(
        finish_kernel,
        out_shape=[
            jax.ShapeDtypeStruct((1024, FF_HERE), F32),
            jax.ShapeDtypeStruct((QKV, 1024), F32),
            jax.ShapeDtypeStruct((FF_HERE, 1024), F32),
            jax.ShapeDtypeStruct((HD, 1024), F32),
            jax.ShapeDtypeStruct((1, FF_HERE), F32),
            jax.ShapeDtypeStruct((1, QKV), F32),
        ],
        in_specs=[SCALARS] + [WHOLE] * 4,
        out_specs=[WHOLE] * 6,
        scratch_shapes=[pltpu.VMEM((SUMMED, 1024), BF)],
        compiler_params=limit(16),
        name="finish",
    )(scalars, *quarters)


def sum_vectors(quarters):
    return pl.pallas_call(
        vectors_kernel,
        out_shape=jax.ShapeDtypeStruct((8, 1024), F32),
        in_specs=[WHOLE] * 4,
        out_specs=WHOLE,
        compiler_params=SMALL,
        name="sum_vectors",
    )(*quarters)


def norm_grads(flag, mine, there):
    return pl.pallas_call(
        norms_kernel,
        out_shape=[jax.ShapeDtypeStruct((1, 1024), F32)] * 4,
        in_specs=[SCALARS] + [WHOLE] * 2,
        out_specs=[WHOLE] * 4,
        compiler_params=SMALL,
        name="norm_grads",
    )(flag, mine, there)


def gate(values, *earlier):
    n = len(values)
    return pl.pallas_call(
        gate_kernel,
        out_shape=[jax.ShapeDtypeStruct(value.shape, value.dtype) for value in values],
        in_specs=[FAR] * (n + len(earlier)),
        out_specs=[FAR] * n,
        input_output_aliases={k: k for k in range(n)},
        compiler_params=limit(1),
        name="gate",
    )(*values, *earlier)


def add(own, other, n_out, *earlier):
    with_vectors = own.shape[0] > ROWS // 2
    size = ROWS // 2 // n_out + 16 * with_vectors
    return pl.pallas_call(
        functools.partial(add_kernel, n_out, with_vectors),
        out_shape=[
            jax.ShapeDtypeStruct((size, 1024), BF if k else F32) for k in range(n_out)
        ],
        in_specs=[WHOLE] * 2 + [FAR] * len(earlier),
        out_specs=[WHOLE] * n_out,
        compiler_params=SMALL,
        name="add",
    )(own, other, *earlier)


def fold(total, arrived, *earlier):
    size = (total.shape[0] - 16) // 2 + 16 if total.shape[0] > 2 * BLOCK else BLOCK
    return pl.pallas_call(
        fold_kernel,
        out_shape=[
            jax.ShapeDtypeStruct((size, 1024), F32),
            jax.ShapeDtypeStruct((size, 1024), BF),
        ],
        in_specs=[WHOLE] * 4 + [FAR] * len(earlier),
        out_specs=[WHOLE] * 2,
        compiler_params=SMALL,
        cost_estimate=pl.CostEstimate(
            flops=FOLD_COST, bytes_accessed=2**20, transcendentals=0
        ),
        name="fold",
    )(total, *arrived, *earlier)


def join(quarter, mine, pair):
    return pl.pallas_call(
        join_kernel,
        out_shape=jax.ShapeDtypeStruct((SUMMED // 4 + 16, 1024), BF),
        in_specs=[WHOLE] * 3,
        out_specs=WHOLE,
        compiler_params=SMALL,
        name="join",
    )(quarter, mine, pair)


def close_forward(parts, rows, norm):
    shape = (BLOCK, 1024)
    return pl.pallas_call(
        close_forward_kernel,
        out_shape=[
            jax.ShapeDtypeStruct(shape, F32),
            jax.ShapeDtypeStruct(shape, BF),
            jax.ShapeDtypeStruct(shape, BF),
        ],
        in_specs=[WHOLE] * (len(parts) + 2),
        out_specs=[WHOLE] * 3,
        compiler_params=SMALL,
        name="close_forward",
    )(*parts, rows, norm)


def close_backward(parts, rows, grad_rows, *earlier):
    shape = (BLOCK, 1024)
    return pl.pallas_call(
        functools.partial(close_backward_kernel, len(parts)),
        out_shape=[jax.ShapeDtypeStruct(shape, F32), jax.ShapeDtypeStruct(shape, BF)],
        in_specs=[WHOLE] * (len(parts) + 2) + [FAR] * len(earlier),
        out_specs=[WHOLE] * 2,
        compiler_params=SMALL,
        name="close_backward",
    )(*parts, rows, grad_rows, *earlier)


def rotary_lanes(starts):
    lane = jnp.arange(2 * HD, dtype=jnp.int32) % HD
    inverse = jnp.power(10000.0, -2.0 * (lane % (ROT // 2)).astype(F32) / ROT)
    inverse = jnp.where(lane < ROT, inverse, 0.0)[None, :]
    coarse = (jnp.arange(0, ROWS, 64, dtype=jnp.int32) - starts[::64]).astype(F32)[:, None] * inverse
    fine = jnp.arange(64, dtype=jnp.int32).astype(F32)[:, None] * inverse
    cos_a, sin_a = jnp.cos(coarse)[:, None, :], jnp.sin(coarse)[:, None, :]
    cos_b, sin_b = jnp.cos(fine)[None], jnp.sin(fine)[None]
    shape = (ROWS, 2 * HD)
    return (
        (cos_a * cos_b - sin_a * sin_b).reshape(shape),
        (sin_a * cos_b + cos_a * sin_b).reshape(shape),
    )


def over_dp(part, steps):
    return lax.ppermute(part, "dp", [(i, (i + steps) % 4) for i in range(4)])


def shares_from_dp(shares):
    return [shares[0]] + [over_dp(part, steps) for part, steps in zip(shares[1:], (1, 3, 2))]


def exchanged(kept, given, flip):
    arrived = lax.ppermute(given, "dp", [(i, i ^ flip) for i in range(4)])
    return (kept.astype(F32) + arrived.astype(F32)).astype(BF)


def quarter_sum(shares):
    total = shares[0].astype(F32)
    for share in shares[1:]:
        total += share.astype(F32)
    return total.astype(BF)


def body(
    inputs,
    seq_lengths,
    cotangent,
    ln_gain,
    ln_bias,
    w_qkv,
    b_qkv,
    w_out,
    b_out,
    w_up,
    b_up,
    w_down,
    b_down,
):
    core, z, y = (lax.axis_index(name) for name in DEVICES)
    on_first = core == 0
    micro = jnp.where((y == 0) | (y == 3), 0, 1)
    on_micro_0 = micro == 0
    sent = jnp.where(on_first, micro, 1 - micro)

    def pick(value, index):
        return lax.dynamic_index_in_dim(value, index, 0, keepdims=False)

    sent_rows = pick(inputs, sent)
    scaled_rows = normalize(sent_rows.astype(F32))[0].astype(BF)
    scaled = from_arguments(scaled_rows, on_first)
    chunks_0 = gather_pieces(scaled)
    later_rows, later_grads = gate([sent_rows, pick(cotangent, sent)], scaled)
    rows_0 = jnp.where(on_first, later_rows, send(later_rows, OVER))
    both = from_arguments(later_grads, on_first)
    grad_rows_1 = both[:BLOCK]

    weights = (w_up[0], w_qkv.reshape(1024, QKV).T, w_down[0], w_out[0])
    small = (b_up, b_qkv[0], ln_gain, ln_bias, b_out, b_down)
    mine, again = pack(weights, small, scaled_rows)
    swapped = send(mine, SWAP)
    flag = jnp.where(on_first, 1, 0).astype(jnp.int32)
    layer_0 = unpack(flag[None], mine, swapped)

    starts = start_rows(pick(seq_lengths, micro), ROWS)
    cosine, sine = rotary_lanes(starts)
    scalars = [
        gathered_blocks(core, z, y),
        starts[::SPAN] // SPAN,
        lax.axis_index("dp")[None],
    ]
    place = {
        "scalars": jnp.concatenate([part.astype(jnp.int32) for part in scalars]),
        "cosine": cosine,
        "sine": sine,
    }

    (early,) = gate([both], chunks_0[2])
    pieces = [early] + [send(early, table(step(hops))) for hops in RING[:2]]
    halves_0, saved_0 = forward(chunks_0, layer_0, place, True)
    (other_0,) = gate([halves_0[1]], *pieces[1:])
    total, *blocks = add(halves_0[0], send(other_0, SIBLING), 8)
    arrived = scatter(blocks)
    result_0, rows_1, scaled_rows = close_forward([total] + arrived, rows_0, layer_0["norm"])
    (again,) = gate([again], rows_1)
    over = send(again, OVER)
    layer_1 = unpack(flag[None], swapped, over)
    chunks_1 = gather(scaled_rows)
    (late,) = gate([both], chunks_1[5])
    pieces.append(send(late, table(step(RING[2]))))
    halves_1, saved_1 = forward(chunks_1, layer_1, place, False)

    result_0_there = send(result_0, BACK_OVER)
    pieces[3:] = gate(pieces[3:], halves_1[0])
    grad_halves_1, halves_of_1, vectors_1 = backward(
        with_sibling(pieces), chunks_1, layer_1, saved_1, place, result_0_there
    )
    total, *blocks = add(grad_halves_1[0], send(grad_halves_1[1], SIBLING), 4)
    (other_1,) = gate([halves_1[1]], blocks[0])
    first, *pieces = add(halves_1[0], send(other_1, SIBLING), 4)
    (given,) = gate([halves_of_1[1]], blocks[0])
    half_1 = exchanged(halves_of_1[0], given, 1)
    mine, pair = fold(total, scatter_pieces(blocks))
    pair = send(pair, table(step(0, PAIR)))
    grad_input_1, grad_rows_0 = close_backward([mine, pair], rows_1, grad_rows_1)
    grad_chunks_0 = gather(grad_rows_0)
    n = SUMMED // 4
    share_1 = exchanged(half_1[:n], half_1[n:], 2)
    quarter_1 = (send(share_1, SIBLING).astype(F32) + send(share_1, OVER).astype(F32)).astype(BF)

    pieces = scatter_pieces(gate(pieces, grad_chunks_0[5]))
    grad_input_1_here = send(grad_input_1, SIBLING)
    grad_input_1_there = send(grad_input_1, OVER)

    rows_sums = [
        jnp.sum(rows.astype(F32), axis=0, keepdims=True) for rows in (grad_rows_0, grad_rows_1)
    ]
    grad_halves_0, shares_0, unused_vectors = backward(
        grad_chunks_0,
        [rows_sums[0], vectors_1, rows_sums[1]],
        layer_0,
        saved_0,
        place,
        quarter_1,
        grad_input_1_here,
        grad_input_1_there,
    )
    (other_0,) = gate([grad_halves_0[1]], *pieces)
    total, *blocks = add(grad_halves_0[0], send(other_0, SIBLING), 4)
    shares_0 = shares_from_dp(shares_0)
    share_0 = quarter_sum(shares_0)
    mine_0 = (share_0.astype(F32) + send(share_0, BACK_OVER).astype(F32)).astype(BF)
    quarter = jnp.where(on_first, mine_0, quarter_1)
    mine, pair = fold(total, scatter_pieces(blocks), *shares_0[1:])
    mine_1, pair_1 = fold(first, pieces)
    result_1, unused_rounded, unused_rows = close_forward(
        [mine_1, send(pair_1, table(step(0, PAIR)))], rows_1, layer_1["norm"]
    )
    pair = send(pair, table(step(0, PAIR)))
    grad_input_0, unused_rounded = close_backward([mine, pair], rows_0, grad_rows_0)
    quarter = join(quarter, mine, pair)
    quarters = [quarter] + [over_dp(quarter, steps) for steps in (1, 2, 3)]
    grad_input_0_there = send(grad_input_0, BACK_OVER)
    vectors = sum_vectors(quarters)
    grad_gain, grad_shift, grad_b_out, grad_b_down = norm_grads(
        flag[None], vectors, send(vectors, table(step(0, 1)))
    )
    grad_up, grad_qkv, grad_down, grad_out, grad_b_up, grad_b_qkv = finish(
        place["scalars"], quarters
    )

    def output_of(value_0, there_0, here_1, there_1):
        here = jnp.where(on_first, value_0, here_1)
        there = jnp.where(on_first, there_0, there_1)
        return jnp.stack(
            [jnp.where(on_micro_0, here, there), jnp.where(on_micro_0, there, here)]
        )[None]

    return (
        output_of(
            result_0, result_0_there, send(result_1, SIBLING), send(result_1, OVER)
        ),
        output_of(
            grad_input_0,
            grad_input_0_there,
            grad_input_1_here,
            grad_input_1_there,
        ),
        grad_gain,
        grad_shift,
        grad_qkv.T.reshape(1, 1024, 1, QKV),
        grad_b_qkv[None],
        grad_out[None],
        grad_b_out,
        grad_up[None],
        grad_b_up,
        grad_down[None],
        grad_b_down,
    )


def solution(mesh):
    rows = P("dp", ("z", "y"), None)
    layer_rows = P("pipe", "dp", ("z", "y"), None)
    heads = P("pipe", None, ("z", "y"), None)
    split = P("pipe", ("z", "y"), None)
    units = P("pipe", None, ("z", "y"))
    whole = P("pipe", None)
    unit_bias = P("pipe", ("z", "y"))
    return jax.shard_map(
        body,
        mesh=Mesh(mesh.devices.reshape(2, 4, 4, 4), ("pipe", "dp", "z", "y")),
        in_specs=(
            rows,
            P("dp", None),
            rows,
            whole,
            whole,
            heads,
            split,
            split,
            whole,
            units,
            unit_bias,
            split,
            whole,
        ),
        out_specs=(
            layer_rows,
            layer_rows,
            whole,
            whole,
            heads,
            split,
            split,
            whole,
            units,
            unit_bias,
            split,
            whole,
        ),
        check_vma=False,
    )
```

```python
import functools

import jax
import jax.numpy as jnp
from jax import lax
from jax.experimental import pallas as pl
from jax.experimental.pallas import tpu as pltpu
from jax.sharding import Mesh, PartitionSpec as P

HD = 64
ROT = 16
FF_HERE = 256
QKV = 3 * HD
IN = FF_HERE + QKV
OUT = FF_HERE + HD
PACKED = IN + 16 + OUT
SUMMED = 832
MIXED = 384
F_LIMIT = 14
B_LIMIT = 23
PACK_LIMIT = 56
FOLD_COST = 30 * 10**9
ADD_COST = 30 * 10**9
ROWS = 2048
BLOCK = 128
SPAN = 512
SPANS = ROWS // SPAN
PER_SPAN = SPAN // BLOCK
EPSILON = 1e-05
NEGATIVE = -1e30
ROOT_HALF = 0.7071067811865476
INV_ROOT_TAU = 0.3989422804014327
DEVICES = ("pipe", "z", "y")
BF = jnp.bfloat16
F32 = jnp.float32


def table(rule):
    pairs = []
    for core in range(2):
        for z in range(4):
            for y in range(4):
                target = rule(core, z, y)
                if target is not None:
                    to_core, to_z, to_y = target
                    pairs.append((core * 16 + z * 4 + y, to_core * 16 + to_z % 4 * 4 + to_y))
    return pairs


def by_core(first, second):
    return table(lambda core, z, y: (first if core == 0 else second)(core, z, y))


def step(steps, flip=0):
    return lambda core, z, y: (core, z + steps, y ^ flip)


def nowhere(core, z, y):
    return None


PAIR = 3
SIBLING = table(lambda core, z, y: (1 - core, z, y))
OVER = by_core(nowhere, step(0, 1))
BACK_OVER = by_core(nowhere, lambda core, z, y: (0, z, y ^ 1))
SWAP = by_core(lambda core, z, y: (1, z, y ^ 1), lambda core, z, y: (0, z, y))
RING = (1, -1, 2)


def send(value, pairs):
    return lax.ppermute(value, DEVICES, pairs)


def gathered_blocks(core, z, y):
    def of(own):
        columns = (y ^ own, y ^ own ^ PAIR)
        steps = [0] + [-hops for hops in RING]
        return [(z + hops) % 4 * 4 + column for column in columns for hops in steps]

    first, second = jnp.stack(of(0)), jnp.stack(of(1))
    return jnp.where(
        core == 0, jnp.concatenate([first, second]), jnp.concatenate([second, first])
    ).astype(jnp.int32)


def with_sibling(blocks):
    return blocks + [send(block, SIBLING) for block in blocks]


def gather(rows):
    pair = send(rows, table(step(0, PAIR)))
    own = [send(rows, table(step(hops))) for hops in RING]
    far = [send(pair, table(step(hops))) for hops in RING]
    return with_sibling([rows] + own + [pair] + far)


def from_arguments(rows, on_first):
    near = send(rows, by_core(step(0, PAIR), step(0, 1)))
    beside = send(rows, by_core(nowhere, step(0, 2)))
    return jnp.concatenate([jnp.where(on_first, rows, near), jnp.where(on_first, near, beside)])


def gather_pieces(both):
    return with_sibling([both] + [send(both, table(step(hops))) for hops in RING])


def scatter(blocks):
    steps = [(-hops, 0) for hops in RING] + [(0, PAIR)] + [(-hops, PAIR) for hops in RING]
    return [send(block, table(step(hops, flip))) for block, (hops, flip) in zip(blocks, steps)]


def scatter_pieces(pieces):
    return [send(piece, table(step(-hops))) for piece, hops in zip(pieces, RING)]


def start_rows(lengths, total_rows):
    endings = jnp.cumsum(lengths)
    places = jnp.arange(total_rows, dtype=jnp.int32)
    passed = places[:, None] >= endings[None, :]
    return jnp.sum(jnp.where(passed, lengths[None, :], 0), axis=1)


def normalize(rows):
    average = jnp.mean(rows, axis=-1, keepdims=True)
    centred = rows - average
    inverse_std = lax.rsqrt(jnp.mean(centred * centred, axis=-1, keepdims=True) + EPSILON)
    return centred * inverse_std, inverse_std


def normalize_back(grad_rows, grad_scaled, rows):
    scaled, inverse_std = normalize(rows.astype(F32))
    return grad_rows.astype(F32) + inverse_std * (
        grad_scaled
        - jnp.mean(grad_scaled, axis=-1, keepdims=True)
        - scaled * jnp.mean(grad_scaled * scaled, axis=-1, keepdims=True)
    )


def block_of(index):
    return pl.ds(pl.multiple_of(index * BLOCK, BLOCK), BLOCK)


def dot(left, right, left_axis=1, right_axis=0):
    return lax.dot_general(
        left, right, (((left_axis,), (right_axis,)), ((), ())), preferred_element_type=F32
    )


def started(parts, sems, first):
    copies = [pltpu.make_async_copy(*part, sems.at[first + k]) for k, part in enumerate(parts)]
    for copy in copies:
        copy.start()
    return copies


def finished(copies):
    for copy in copies:
        copy.wait()


def stacked(refs, group, first):
    return jnp.concatenate(
        [refs[group * PER_SPAN + k][first : first + BLOCK] for k in range(PER_SPAN)]
    )


def chunk_of(refs, group):
    if len(refs) == 16:
        return stacked(refs, group, 0)
    pieces = refs[group // 2 * PER_SPAN : (group // 2 + 1) * PER_SPAN]
    return stacked(pieces, 0, group % 2 * BLOCK)


def half_of(refs, group):
    place = group % (SPANS // 2) * SPAN
    return refs[group // (SPANS // 2)].at[pl.ds(place, SPAN)]


def turned(pairs):
    lane = lax.broadcasted_iota(jnp.int32, pairs.shape, 1) % HD
    return jnp.where(
        lane < ROT // 2, -pltpu.roll(pairs, 2 * HD - ROT // 2, 1), pltpu.roll(pairs, ROT // 2, 1)
    )


def halves(pairs):
    lane = lax.broadcasted_iota(jnp.int32, pairs.shape, 1)
    queries = jnp.where(lane < HD, pairs * HD ** (-0.5), 0.0)
    return queries.astype(BF), pltpu.roll(pairs, HD, 1).astype(BF)


def penalty(scalars_ref, query_span, key_span):
    return jnp.where(key_span >= scalars_ref[16 + query_span], 0.0, -NEGATIVE).astype(F32)


def seen(scores):
    keys = lax.broadcasted_iota(jnp.int32, scores.shape, 0)
    queries = lax.broadcasted_iota(jnp.int32, scores.shape, 1)
    return jnp.where(keys <= queries, scores, NEGATIVE)


def store_parts(store_ref, saved_refs):
    lanes = (0, MIXED, MIXED + FF_HERE, MIXED + FF_HERE + 2 * HD)
    places = [
        store_ref.at[pl.ds(ROWS, ROWS), pl.ds(lane, ref.shape[1])]
        for lane, ref in zip(lanes, saved_refs)
    ]
    return places + [store_ref.at[pl.ds(0, ROWS)]]


def forward_kernel(n_chunks, stored, *refs):
    scalars_ref = refs[0]
    chunk_refs, refs = refs[1 : 1 + n_chunks], refs[1 + n_chunks :]
    w_in_ref, bias_ref, w_out_ref, cosine_ref, sine_ref = refs[:5]
    half_refs, log_sums_ref, refs = refs[5:7], refs[7], refs[8:]
    kept_hbm, kept_refs, refs = refs[:-9], refs[-9:-5], refs[-5:]
    mixed_ref, slope_ref, pairs_ref, values_ref = kept_refs
    queries_ref, keys_ref, turned_values_ref, ordered_ref, sems = refs
    copies = []
    if stored:
        kept_hbm = store_parts(kept_hbm[0], kept_refs)
        parts = []
        for k in range(16):
            source = chunk_refs[k // 8 * 4 + k % 4].at[pl.ds(k % 8 // 4 * BLOCK, BLOCK)]
            parts.append((source, kept_hbm[4].at[pl.ds(k * BLOCK, BLOCK)]))
        copies = started(parts, sems, 0)
    for group in range(SPANS):
        rows = slice(group * SPAN, (group + 1) * SPAN)
        projected = dot(chunk_of(chunk_refs, group), w_in_ref[...], 1, 1) + bias_ref[...]
        inner = projected[:, :FF_HERE]
        wave = 1.0 + lax.erf(inner * ROOT_HALF)
        mixed_ref[rows, :FF_HERE] = (0.5 * inner * wave).astype(BF)
        slope = 0.5 * wave + inner * jnp.exp(-0.5 * inner * inner) * INV_ROOT_TAU
        slope_ref[rows] = slope.astype(BF)
        for k in range(PER_SPAN):
            joined = projected[k * BLOCK : (k + 1) * BLOCK, FF_HERE:]
            place = block_of(scalars_ref[group * PER_SPAN + k])
            pairs = joined[:, : 2 * HD]
            pairs = pairs * cosine_ref[place] + turned(pairs) * sine_ref[place]
            pairs_ref[place] = pairs.astype(BF)
            queries_ref[place], keys_ref[place] = halves(pairs.astype(BF).astype(F32))
            values = joined[:, 2 * HD :]
            values_ref[place, :HD] = values.astype(BF)
            turned_values_ref[:, place] = values.T.astype(BF)
    for i in range(SPANS):
        span = slice(i * SPAN, (i + 1) * SPAN)
        queries = queries_ref[span]
        scores, offsets, highest = [], [], None
        for j in range(i + 1):
            block = dot(keys_ref[j * SPAN : (j + 1) * SPAN], queries, 1, 1)
            block = seen(block) if i == j else block
            offset = 0.0 if i == j else penalty(scalars_ref, i, j)
            top = jnp.max(block, axis=0, keepdims=True) - offset
            highest = top if highest is None else jnp.maximum(highest, top)
            scores.append(block)
            offsets.append(offset)
        total, summed = 0.0, 0.0
        for j in range(i + 1):
            exponent = jnp.exp(scores[j] - (highest + offsets[j]))
            total = total + jnp.sum(exponent, axis=0, keepdims=True)
            summed = summed + dot(
                turned_values_ref[:, j * SPAN : (j + 1) * SPAN], exponent.astype(BF)
            )
        log_sums_ref[:, span] = highest + jnp.log(total)
        ordered_ref[span] = (summed / total).T.astype(BF)
    for group in range(SPANS):
        for k in range(PER_SPAN):
            index = group * PER_SPAN + k
            here = slice(index * BLOCK, (index + 1) * BLOCK)
            mixed_ref[here, FF_HERE:OUT] = ordered_ref[block_of(scalars_ref[index])]
        rows = slice(group * SPAN, (group + 1) * SPAN)
        half_of(half_refs, group)[...] = dot(mixed_ref[rows, :OUT], w_out_ref[...]).astype(BF)
    copies += started(list(zip(kept_refs, kept_hbm)), sems, 16)
    finished(copies)


def backward_kernel(separate, n_earlier, *refs):
    scalars_ref = refs[0]
    count = 16 if separate else 8
    chunk_refs, refs = refs[1 : 1 + count], refs[1 + count :]
    feature_refs, given_refs = [], None
    if separate:
        given_refs, refs = refs[:3], refs[3:]
    else:
        feature_refs, refs = refs[:16], refs[16:]

    w_in_ref, w_out_ref, kept_ref, norm_ref, log_sums_ref, cosine_ref, sine_ref = refs[:7]
    count = 5 if separate else 4
    n_saved = 1 if separate else 4
    saved_hbm, refs = refs[7 : 7 + n_saved], refs[7 + n_saved + n_earlier :]
    n_parts = 4 if separate else 2
    half_refs, quarter_refs, refs = refs[:2], refs[2 : 2 + n_parts], refs[2 + n_parts :]
    vectors_ref, refs = refs[0], refs[1:]
    saved_refs, refs = refs[:count], refs[count:]
    mixed_ref, slope_ref, pairs_ref, values_ref = saved_refs[:4]
    features_ref = saved_refs[-1]
    grad_in_ref, queries_ref, keys_ref, turned_keys_ref, grad_heads_ref, products_ref = refs[:6]
    grad_queries_ref, grad_keys_ref, grad_values_ref, grads_ref, sems = refs[6:]
    if separate:
        saved_hbm = store_parts(saved_hbm[0], saved_refs[:4])
    copies = started(list(zip(saved_hbm, saved_refs)), sems, 0)
    finished(copies[:4])
    for group in range(SPANS):
        rows = slice(group * SPAN, (group + 1) * SPAN)
        grad_mixed = dot(chunk_of(chunk_refs, group), w_out_ref[...], 1, 1)
        grad_in_ref[rows, :FF_HERE] = (
            grad_mixed[:, :FF_HERE] * slope_ref[rows].astype(F32)
        ).astype(BF)
        for k in range(PER_SPAN):
            index = group * PER_SPAN + k
            here, place = slice(index * BLOCK, (index + 1) * BLOCK), block_of(scalars_ref[index])
            grad_heads = grad_mixed[k * BLOCK : (k + 1) * BLOCK, FF_HERE:].astype(BF)
            grad_heads_ref[place] = grad_heads
            product = grad_heads.astype(F32) * mixed_ref[here, FF_HERE:OUT].astype(F32)
            products_ref[:, place] = jnp.sum(product.T, axis=0, keepdims=True)
            queries_ref[here], keys = halves(pairs_ref[here].astype(F32))
            keys_ref[here] = keys
            turned_keys_ref[:, here] = keys[:, :HD].astype(F32).T.astype(BF)
    grad_queries_ref[...] = jnp.zeros_like(grad_queries_ref)
    for j in range(SPANS):
        key_span = slice(j * SPAN, (j + 1) * SPAN)
        keys, values = keys_ref[key_span], values_ref[key_span, :HD]
        grad_keys, grad_values = 0.0, 0.0
        for i in range(j, SPANS):
            span = slice(i * SPAN, (i + 1) * SPAN)
            queries, grad_heads = queries_ref[span], grad_heads_ref[span]
            scores = dot(keys, queries, 1, 1)
            scores = seen(scores) if i == j else scores
            offset = 0.0 if i == j else penalty(scalars_ref, i, j)
            probability = jnp.exp(scores - (log_sums_ref[:, span] + offset))
            grad_values += dot(probability.astype(BF), grad_heads)
            grad_probs = dot(values, grad_heads, 1, 1)
            grad_scores = (probability * (grad_probs - products_ref[:, span])).astype(BF)
            grad_keys += dot(grad_scores, queries)
            grad_queries_ref[:, span] += dot(turned_keys_ref[:, key_span], grad_scores)
        grad_keys_ref[key_span] = grad_keys
        grad_values_ref[key_span] = grad_values
    for group in range(SPANS):
        for k in range(PER_SPAN):
            index = group * PER_SPAN + k
            here, place = slice(index * BLOCK, (index + 1) * BLOCK), block_of(scalars_ref[index])
            grad_queries = (grad_queries_ref[:, place] * HD ** (-0.5)).T
            grad_pairs = jnp.concatenate([grad_queries, grad_keys_ref[place, :HD]], axis=1)
            grad_pairs = grad_pairs * cosine_ref[place] - turned(grad_pairs) * sine_ref[place]
            grad_in_ref[here, FF_HERE : FF_HERE + 2 * HD] = grad_pairs.astype(BF)
            grad_in_ref[here, FF_HERE + 2 * HD :] = grad_values_ref[place].astype(BF)
        rows = slice(group * SPAN, (group + 1) * SPAN)
        half_of(half_refs, group)[...] = dot(grad_in_ref[rows], w_in_ref[...]).astype(BF)
    finished(copies[4:])
    raw, after, columns = 0.0, 0.0, 0.0
    ones = jnp.ones((SPAN, BLOCK), BF)
    total = jnp.zeros((1, IN), F32)
    for group in range(SPANS):
        rows = slice(group * SPAN, (group + 1) * SPAN)
        grad_in = grad_in_ref[rows]
        features = features_ref[rows] if separate else stacked(feature_refs, group, 0)
        raw += dot(grad_in, features, 0, 0)
        columns += dot(grad_in, ones, 0, 0)
        total += jnp.sum(grad_in.astype(F32), axis=0, keepdims=True)
        after += dot(mixed_ref[rows, :OUT], chunk_of(chunk_refs, group), 0, 0)
    kept = kept_ref[...].astype(F32)
    gain, shift = norm_ref[0:1], norm_ref[1:2]
    column = columns[:, :1]
    grads_ref[:IN] = (raw * gain + column * shift).astype(BF)
    grads_ref[IN : IN + 16] = jnp.zeros((16, 1024), BF)
    grads_ref[IN : IN + 1, :IN] = total.astype(BF)
    grads_ref[IN + 16 : PACKED] = after.astype(BF)
    grads_ref[PACKED:] = jnp.zeros((SUMMED - PACKED, 1024), BF)
    n = SUMMED // 4

    def quarter(index):
        return grads_ref[pl.ds(pl.multiple_of(index * n, 16), n)]

    here = scalars_ref[20]
    if separate:
        for ref, steps in zip(quarter_refs, (0, 1, 3, 2)):
            ref[...] = quarter(lax.rem(here + steps, 4))
    else:
        for ref, first in zip(quarter_refs, (here, here ^ 1)):
            ref[:n] = quarter(first)
            ref[n:] = quarter(first ^ 2)
    grad_gain = jnp.sum(raw * kept, axis=0, keepdims=True)
    grad_shift = jnp.sum(column * kept, axis=0, keepdims=True)
    if not separate:
        vectors_ref[0:1] = grad_gain
        vectors_ref[1:2] = grad_shift
        return
    row = lax.broadcasted_iota(jnp.int32, (8, 1024), 0)
    rows_ref, norm_1_ref, rows_1_ref = given_refs
    parts = (grad_gain, grad_shift, rows_ref[...], norm_1_ref[0:1], norm_1_ref[1:2], rows_1_ref[...])
    vectors = jnp.zeros((8, 1024), F32)
    for k, part in enumerate(parts):
        vectors = jnp.where(row == k, part, vectors)
    high = vectors.astype(BF).astype(F32)
    vectors = jnp.concatenate([high, vectors - high]).astype(BF)
    for ref in half_refs:
        ref[ROWS // 2 :] = vectors


def pack_kernel(*refs):
    up_hbm, qkv_hbm, down_hbm, out_hbm, b_up_ref, b_qkv_ref, gain_ref, shift_ref = refs[:8]
    b_out_ref, b_down_ref, unused_ref, *packed_hbm, up_ref, packed_ref, sems = refs[8:]
    parts = [
        (up_hbm, up_ref),
        (qkv_hbm, packed_ref.at[pl.ds(FF_HERE, QKV)]),
        (down_hbm, packed_ref.at[pl.ds(IN + 16, FF_HERE)]),
        (out_hbm, packed_ref.at[pl.ds(IN + 16 + FF_HERE, HD)]),
    ]
    copies = started(parts, sems, 0)
    biases = jnp.concatenate(
        [b_up_ref[...], b_qkv_ref[...], jnp.zeros((1, 1024 - IN), F32)], axis=1
    )
    rows = lax.broadcasted_iota(jnp.int32, (16, 1024), 0)
    small = jnp.zeros((16, 1024), F32)
    for value, high_row, low_row in (
        (biases, 0, 1),
        (gain_ref[...], 2, 5),
        (shift_ref[...], 3, 6),
        (b_out_ref[...] + b_down_ref[...], 4, 7),
    ):
        high = value.astype(BF).astype(F32)
        small = jnp.where(rows == high_row, high, small)
        small = jnp.where(rows == low_row, value - high, small)
    packed_ref[IN : IN + 16] = small.astype(BF)
    copies[0].wait()
    packed_ref[:FF_HERE] = up_ref[...].T
    finished(copies[1:])
    finished(started([(packed_ref, target) for target in packed_hbm], sems, 0))


def unpack_kernel(
    flag_ref, first_hbm, second_hbm, w_in_ref, kept_ref, w_out_ref, bias_ref, norm_ref, packed_ref, sem
):
    @pl.when(flag_ref[0] == 1)
    def _():
        copy = pltpu.make_async_copy(first_hbm, packed_ref, sem)
        copy.start()
        copy.wait()

    @pl.when(flag_ref[0] != 1)
    def _():
        copy = pltpu.make_async_copy(second_hbm, packed_ref, sem)
        copy.start()
        copy.wait()

    w_in = packed_ref[:IN]
    small = packed_ref[IN : IN + 16]
    shifts = dot(small, w_in, 1, 1)
    small = small.astype(F32)
    norm_ref[0:3] = small[2:5] + small[5:8]
    bias_ref[...] = small[0:1, :IN] + small[1:2, :IN] + shifts[3:4] + shifts[6:7]
    kept_ref[...] = w_in
    w_in_ref[...] = (w_in.astype(F32) * norm_ref[0:1]).astype(BF)
    w_out_ref[...] = packed_ref[IN + 16 : PACKED]


def finish_kernel(scalars_ref, *refs):
    up_ref, qkv_ref, down_ref, out_ref, b_up_ref, b_qkv_ref, whole_ref = refs[4:]
    n = SUMMED // 4
    for k in range(4):
        place = lax.rem(scalars_ref[20] + 4 - k, 4)
        whole_ref[pl.ds(pl.multiple_of(place * n, 16), n)] = refs[k][:n]
    up_ref[...] = whole_ref[:FF_HERE].astype(F32).T
    qkv_ref[...] = whole_ref[FF_HERE:IN].astype(F32)
    biases = whole_ref[IN : IN + 16].astype(F32)[0:1]
    b_up_ref[...] = biases[:, :FF_HERE]
    b_qkv_ref[...] = biases[:, FF_HERE:IN]
    down_ref[...] = whole_ref[IN + 16 : IN + 16 + FF_HERE].astype(F32)
    out_ref[...] = whole_ref[IN + 16 + FF_HERE : PACKED].astype(F32)


def vectors_kernel(*refs):
    n = SUMMED // 4
    total = 0.0
    for ref in refs[:4]:
        total += ref[n : n + 8].astype(F32) + ref[n + 8 :].astype(F32)
    refs[4][...] = total


def norms_kernel(flag_ref, mine_ref, there_ref, gain_ref, shift_ref, b_out_ref, b_down_ref):
    total = mine_ref[...] + there_ref[...]
    mine = jnp.where(flag_ref[0] == 1, total[0:3], total[3:6])
    gain_ref[...] = mine[0:1]
    shift_ref[...] = mine[1:2]
    b_out_ref[...] = mine[2:3]
    b_down_ref[...] = mine[2:3]


def add_kernel(n_out, with_vectors, *refs):
    own_ref, other_ref = refs[:2]
    out_refs = refs[-n_out:]
    count = 8 // n_out
    for k, ref in enumerate(out_refs):
        for part in range(count):
            index = k + part * n_out
            rows = slice(index * BLOCK, (index + 1) * BLOCK)
            value = own_ref[rows].astype(F32) + other_ref[rows].astype(F32)
            ref[part * BLOCK : (part + 1) * BLOCK] = value.astype(ref.dtype)
    if with_vectors:
        rows = slice(ROWS // 2, ROWS // 2 + 16)
        both = own_ref[rows].astype(F32) + other_ref[rows].astype(F32)
        vectors = both[:8] + both[8:]
        high = vectors.astype(BF).astype(F32)
        below = jnp.concatenate([high, vectors - high])
        for ref in out_refs:
            ref[count * BLOCK :] = below.astype(ref.dtype)


def total_of(refs):
    total = refs[0][:BLOCK]
    for ref in refs[1:]:
        total += ref[:BLOCK].astype(F32)
    return total


def close_forward_kernel(*refs):
    rows_ref, norm_ref, result_ref, rounded_ref, scaled_ref = refs[-5:]
    total = total_of(refs[:-5])
    result = rows_ref[...].astype(F32) + total + norm_ref[2:3]
    result_ref[...] = result
    rounded = result.astype(BF)
    rounded_ref[...] = rounded
    scaled_ref[...] = normalize(rounded.astype(F32))[0].astype(BF)


def close_backward_kernel(n_parts, *refs):
    rows_ref, grad_rows_ref = refs[n_parts : n_parts + 2]
    grad_ref, rounded_ref = refs[-2:]
    total = total_of(refs[:n_parts])
    grad = normalize_back(grad_rows_ref[...], total, rows_ref[...])
    grad_ref[...] = grad
    rounded_ref[...] = grad.astype(BF)


def fold_kernel(total_ref, *refs):
    mine_ref, pair_ref = refs[-2:]
    total = total_ref[...]
    for ref in refs[:3]:
        total += ref[...].astype(F32)
    size = mine_ref.shape[0]
    mine_ref[:BLOCK] = total[:BLOCK]
    pair_ref[:BLOCK] = total[BLOCK : 2 * BLOCK].astype(BF)
    if size > BLOCK:
        vectors = total[2 * BLOCK : 2 * BLOCK + 8] + total[2 * BLOCK + 8 :]
        high = vectors.astype(BF).astype(F32)
        mine_ref[BLOCK:] = jnp.concatenate([high, vectors - high])
        pair_ref[BLOCK:] = jnp.concatenate([high, vectors - high]).astype(BF)


def join_kernel(quarter_ref, mine_ref, pair_ref, joined_ref):
    n = SUMMED // 4
    joined_ref[:n] = quarter_ref[...]
    both = mine_ref[BLOCK:] + pair_ref[BLOCK:].astype(F32)
    vectors = both[:8] + both[8:]
    high = vectors.astype(BF).astype(F32)
    joined_ref[n:] = jnp.concatenate([high, vectors - high]).astype(BF)


def gate_kernel(*refs):
    pass


WHOLE = pl.BlockSpec(memory_space=pltpu.VMEM)
SCALARS = pl.BlockSpec(memory_space=pltpu.SMEM)
FAR = pl.BlockSpec(memory_space=pl.ANY)


def limit(size):
    return pltpu.CompilerParams(vmem_limit_bytes=size * 2**20)


SMALL = limit(12)
HALF = jax.ShapeDtypeStruct((ROWS // 2, 1024), BF)
SAVED = [
    jax.ShapeDtypeStruct((ROWS, width), BF) for width in (MIXED, FF_HERE, 2 * HD, 2 * HD, 1024)
]


STORE = jax.ShapeDtypeStruct((10 * ROWS, 1024), BF)


def like(shapes):
    return [pltpu.VMEM(shape.shape, shape.dtype) for shape in shapes]


def forward(chunks, layer, place, stored):
    saved = [STORE] if stored else SAVED[:4]
    outs = pl.pallas_call(
        functools.partial(forward_kernel, len(chunks), stored),
        out_shape=[HALF] * 2 + [jax.ShapeDtypeStruct((1, ROWS), F32)] + saved,
        in_specs=[SCALARS] + [WHOLE] * (len(chunks) + 5),
        out_specs=[WHOLE] * 3 + [FAR] * len(saved),
        scratch_shapes=like(SAVED[:4])
        + [
            pltpu.VMEM((ROWS, 2 * HD), BF),
            pltpu.VMEM((ROWS, 2 * HD), BF),
            pltpu.VMEM((HD, ROWS), BF),
            pltpu.VMEM((ROWS, HD), BF),
            pltpu.SemaphoreType.DMA((20,)),
        ],
        compiler_params=limit(F_LIMIT),
        cost_estimate=pl.CostEstimate(
            flops=12 * 10**9, bytes_accessed=2**24, transcendentals=ROWS * ROWS
        ),
        name="forward",
    )(
        place["scalars"],
        *chunks,
        layer["w_in"],
        layer["bias_in"],
        layer["w_out"],
        place["cosine"],
        place["sine"],
    )
    return outs[:2], outs[2:]


def backward(chunks, others, layer, saved, place, *earlier):
    separate = len(saved) == 2
    saved_shapes = SAVED if separate else SAVED[:4]
    half = (ROWS // 2 + 16 * separate, 1024)
    parts = 4 if separate else 2
    outs = pl.pallas_call(
        functools.partial(backward_kernel, separate, len(earlier)),
        out_shape=[jax.ShapeDtypeStruct(half, BF)] * 2
        + [jax.ShapeDtypeStruct((SUMMED // parts, 1024), BF)] * parts
        + [jax.ShapeDtypeStruct((2, 1024), F32)],
        in_specs=[SCALARS]
        + [WHOLE] * (len(chunks) + len(others) + 7)
        + [FAR] * (len(saved) - 1 + len(earlier)),
        out_specs=[WHOLE] * (3 + parts),
        scratch_shapes=like(saved_shapes)
        + [
            pltpu.VMEM((ROWS, IN), BF),
            pltpu.VMEM((ROWS, 2 * HD), BF),
            pltpu.VMEM((ROWS, 2 * HD), BF),
            pltpu.VMEM((HD, ROWS), BF),
            pltpu.VMEM((ROWS, HD), BF),
            pltpu.VMEM((1, ROWS), F32),
            pltpu.VMEM((HD, ROWS), F32),
            pltpu.VMEM((ROWS, 2 * HD), F32),
            pltpu.VMEM((ROWS, HD), F32),
            pltpu.VMEM((SUMMED, 1024), BF),
            pltpu.SemaphoreType.DMA((5,)),
        ],
        compiler_params=limit(B_LIMIT + 4 * separate),
        cost_estimate=pl.CostEstimate(
            flops=18 * 10**9, bytes_accessed=2**24, transcendentals=ROWS * ROWS
        ),
        name="backward",
    )(
        place["scalars"],
        *chunks,
        *others,
        layer["w_in"],
        layer["w_out"],
        layer["kept"],
        layer["norm"],
        saved[0],
        place["cosine"],
        place["sine"],
        *saved[1:],
        *earlier,
    )
    return outs[:2], outs[2:-1], outs[-1]


def pack(weights, vectors, earlier):
    return pl.pallas_call(
        pack_kernel,
        out_shape=[jax.ShapeDtypeStruct((PACKED, 1024), BF)] * 2,
        in_specs=[FAR] * 4 + [WHOLE] * 6 + [FAR],
        out_specs=[FAR] * 2,
        scratch_shapes=[
            pltpu.VMEM((1024, FF_HERE), BF),
            pltpu.VMEM((PACKED, 1024), BF),
            pltpu.SemaphoreType.DMA((4,)),
        ],
        compiler_params=limit(PACK_LIMIT),
        name="pack",
    )(*weights, *vectors, earlier)


def unpack(flag, first, second):
    w_in, kept, w_out, bias_in, norm = pl.pallas_call(
        unpack_kernel,
        out_shape=[
            jax.ShapeDtypeStruct((IN, 1024), BF),
            jax.ShapeDtypeStruct((IN, 1024), BF),
            jax.ShapeDtypeStruct((OUT, 1024), BF),
            jax.ShapeDtypeStruct((1, IN), F32),
            jax.ShapeDtypeStruct((3, 1024), F32),
        ],
        in_specs=[SCALARS] + [FAR] * 2,
        out_specs=[WHOLE] * 5,
        scratch_shapes=[pltpu.VMEM((PACKED, 1024), BF), pltpu.SemaphoreType.DMA],
        compiler_params=limit(16),
        name="unpack",
    )(flag, first, second)
    return {"w_in": w_in, "kept": kept, "w_out": w_out, "bias_in": bias_in, "norm": norm}


def finish(scalars, quarters):
    return pl.pallas_call(
        finish_kernel,
        out_shape=[
            jax.ShapeDtypeStruct((1024, FF_HERE), F32),
            jax.ShapeDtypeStruct((QKV, 1024), F32),
            jax.ShapeDtypeStruct((FF_HERE, 1024), F32),
            jax.ShapeDtypeStruct((HD, 1024), F32),
            jax.ShapeDtypeStruct((1, FF_HERE), F32),
            jax.ShapeDtypeStruct((1, QKV), F32),
        ],
        in_specs=[SCALARS] + [WHOLE] * 4,
        out_specs=[WHOLE] * 6,
        scratch_shapes=[pltpu.VMEM((SUMMED, 1024), BF)],
        compiler_params=limit(16),
        name="finish",
    )(scalars, *quarters)


def sum_vectors(quarters):
    return pl.pallas_call(
        vectors_kernel,
        out_shape=jax.ShapeDtypeStruct((8, 1024), F32),
        in_specs=[WHOLE] * 4,
        out_specs=WHOLE,
        compiler_params=SMALL,
        name="sum_vectors",
    )(*quarters)


def norm_grads(flag, mine, there):
    return pl.pallas_call(
        norms_kernel,
        out_shape=[jax.ShapeDtypeStruct((1, 1024), F32)] * 4,
        in_specs=[SCALARS] + [WHOLE] * 2,
        out_specs=[WHOLE] * 4,
        compiler_params=SMALL,
        name="norm_grads",
    )(flag, mine, there)


def gate(values, *earlier):
    n = len(values)
    return pl.pallas_call(
        gate_kernel,
        out_shape=[jax.ShapeDtypeStruct(value.shape, value.dtype) for value in values],
        in_specs=[FAR] * (n + len(earlier)),
        out_specs=[FAR] * n,
        input_output_aliases={k: k for k in range(n)},
        compiler_params=limit(1),
        name="gate",
    )(*values, *earlier)


def add(own, other, n_out, *earlier):
    with_vectors = own.shape[0] > ROWS // 2
    size = ROWS // 2 // n_out + 16 * with_vectors
    return pl.pallas_call(
        functools.partial(add_kernel, n_out, with_vectors),
        out_shape=[
            jax.ShapeDtypeStruct((size, 1024), BF if k else F32) for k in range(n_out)
        ],
        in_specs=[WHOLE] * 2 + [FAR] * len(earlier),
        out_specs=[WHOLE] * n_out,
        compiler_params=SMALL,
        cost_estimate=pl.CostEstimate(
            flops=ADD_COST, bytes_accessed=2**20, transcendentals=0
        ),
        name="add",
    )(own, other, *earlier)


def fold(total, arrived, *earlier):
    size = (total.shape[0] - 16) // 2 + 16 if total.shape[0] > 2 * BLOCK else BLOCK
    return pl.pallas_call(
        fold_kernel,
        out_shape=[
            jax.ShapeDtypeStruct((size, 1024), F32),
            jax.ShapeDtypeStruct((size, 1024), BF),
        ],
        in_specs=[WHOLE] * 4 + [FAR] * len(earlier),
        out_specs=[WHOLE] * 2,
        compiler_params=SMALL,
        cost_estimate=pl.CostEstimate(
            flops=FOLD_COST, bytes_accessed=2**20, transcendentals=0
        ),
        name="fold",
    )(total, *arrived, *earlier)


def join(quarter, mine, pair):
    return pl.pallas_call(
        join_kernel,
        out_shape=jax.ShapeDtypeStruct((SUMMED // 4 + 16, 1024), BF),
        in_specs=[WHOLE] * 3,
        out_specs=WHOLE,
        compiler_params=SMALL,
        name="join",
    )(quarter, mine, pair)


def close_forward(parts, rows, norm):
    shape = (BLOCK, 1024)
    return pl.pallas_call(
        close_forward_kernel,
        out_shape=[
            jax.ShapeDtypeStruct(shape, F32),
            jax.ShapeDtypeStruct(shape, BF),
            jax.ShapeDtypeStruct(shape, BF),
        ],
        in_specs=[WHOLE] * (len(parts) + 2),
        out_specs=[WHOLE] * 3,
        compiler_params=SMALL,
        name="close_forward",
    )(*parts, rows, norm)


def close_backward(parts, rows, grad_rows, *earlier):
    shape = (BLOCK, 1024)
    return pl.pallas_call(
        functools.partial(close_backward_kernel, len(parts)),
        out_shape=[jax.ShapeDtypeStruct(shape, F32), jax.ShapeDtypeStruct(shape, BF)],
        in_specs=[WHOLE] * (len(parts) + 2) + [FAR] * len(earlier),
        out_specs=[WHOLE] * 2,
        compiler_params=SMALL,
        name="close_backward",
    )(*parts, rows, grad_rows, *earlier)


def rotary_lanes(starts):
    lane = jnp.arange(2 * HD, dtype=jnp.int32) % HD
    inverse = jnp.power(10000.0, -2.0 * (lane % (ROT // 2)).astype(F32) / ROT)
    inverse = jnp.where(lane < ROT, inverse, 0.0)[None, :]
    coarse = (jnp.arange(0, ROWS, 64, dtype=jnp.int32) - starts[::64]).astype(F32)[:, None] * inverse
    fine = jnp.arange(64, dtype=jnp.int32).astype(F32)[:, None] * inverse
    cos_a, sin_a = jnp.cos(coarse)[:, None, :], jnp.sin(coarse)[:, None, :]
    cos_b, sin_b = jnp.cos(fine)[None], jnp.sin(fine)[None]
    shape = (ROWS, 2 * HD)
    return (
        (cos_a * cos_b - sin_a * sin_b).reshape(shape),
        (sin_a * cos_b + cos_a * sin_b).reshape(shape),
    )


def over_dp(part, steps):
    return lax.ppermute(part, "dp", [(i, (i + steps) % 4) for i in range(4)])


def shares_from_dp(shares):
    return [shares[0]] + [over_dp(part, steps) for part, steps in zip(shares[1:], (1, 3, 2))]


def exchanged(kept, given, flip):
    arrived = lax.ppermute(given, "dp", [(i, i ^ flip) for i in range(4)])
    return (kept.astype(F32) + arrived.astype(F32)).astype(BF)


def quarter_sum(shares):
    total = shares[0].astype(F32)
    for share in shares[1:]:
        total += share.astype(F32)
    return total.astype(BF)


def body(
    inputs,
    seq_lengths,
    cotangent,
    ln_gain,
    ln_bias,
    w_qkv,
    b_qkv,
    w_out,
    b_out,
    w_up,
    b_up,
    w_down,
    b_down,
):
    core, z, y = (lax.axis_index(name) for name in DEVICES)
    on_first = core == 0
    micro = jnp.where((y == 0) | (y == 3), 0, 1)
    on_micro_0 = micro == 0
    sent = jnp.where(on_first, micro, 1 - micro)

    def pick(value, index):
        return lax.dynamic_index_in_dim(value, index, 0, keepdims=False)

    sent_rows = pick(inputs, sent)
    scaled_rows = normalize(sent_rows.astype(F32))[0].astype(BF)
    scaled = from_arguments(scaled_rows, on_first)
    chunks_0 = gather_pieces(scaled)
    later_rows, later_grads = gate([sent_rows, pick(cotangent, sent)], scaled)
    rows_0 = jnp.where(on_first, later_rows, send(later_rows, OVER))
    both = from_arguments(later_grads, on_first)
    grad_rows_1 = both[:BLOCK]

    weights = (w_up[0], w_qkv.reshape(1024, QKV).T, w_down[0], w_out[0])
    small = (b_up, b_qkv[0], ln_gain, ln_bias, b_out, b_down)
    mine, again = pack(weights, small, scaled_rows)
    swapped = send(mine, SWAP)
    flag = jnp.where(on_first, 1, 0).astype(jnp.int32)
    layer_0 = unpack(flag[None], mine, swapped)

    starts = start_rows(pick(seq_lengths, micro), ROWS)
    cosine, sine = rotary_lanes(starts)
    scalars = [
        gathered_blocks(core, z, y),
        starts[::SPAN] // SPAN,
        lax.axis_index("dp")[None],
    ]
    place = {
        "scalars": jnp.concatenate([part.astype(jnp.int32) for part in scalars]),
        "cosine": cosine,
        "sine": sine,
    }

    (early,) = gate([both], chunks_0[2])
    pieces = [early] + [send(early, table(step(hops))) for hops in RING[:2]]
    halves_0, saved_0 = forward(chunks_0, layer_0, place, True)
    (other_0,) = gate([halves_0[1]], *pieces[1:])
    total, *blocks = add(halves_0[0], send(other_0, SIBLING), 8)
    arrived = scatter(blocks)
    result_0, rows_1, scaled_rows = close_forward([total] + arrived, rows_0, layer_0["norm"])
    (again,) = gate([again], rows_1)
    over = send(again, OVER)
    layer_1 = unpack(flag[None], swapped, over)
    chunks_1 = gather(scaled_rows)
    (late,) = gate([both], chunks_1[5])
    pieces.append(send(late, table(step(RING[2]))))
    halves_1, saved_1 = forward(chunks_1, layer_1, place, False)

    result_0_there = send(result_0, BACK_OVER)
    pieces[3:] = gate(pieces[3:], halves_1[0])
    grad_halves_1, halves_of_1, vectors_1 = backward(
        with_sibling(pieces), chunks_1, layer_1, saved_1, place, result_0_there
    )
    total, *blocks = add(grad_halves_1[0], send(grad_halves_1[1], SIBLING), 4)
    (other_1,) = gate([halves_1[1]], blocks[0])
    first, *pieces = add(halves_1[0], send(other_1, SIBLING), 4)
    (given,) = gate([halves_of_1[1]], blocks[0])
    half_1 = exchanged(halves_of_1[0], given, 1)
    mine, pair = fold(total, scatter_pieces(blocks))
    pair = send(pair, table(step(0, PAIR)))
    grad_input_1, grad_rows_0 = close_backward([mine, pair], rows_1, grad_rows_1)
    grad_chunks_0 = gather(grad_rows_0)
    n = SUMMED // 4
    share_1 = exchanged(half_1[:n], half_1[n:], 2)
    quarter_1 = (send(share_1, SIBLING).astype(F32) + send(share_1, OVER).astype(F32)).astype(BF)

    pieces = scatter_pieces(gate(pieces, grad_chunks_0[5]))
    grad_input_1_here = send(grad_input_1, SIBLING)
    grad_input_1_there = send(grad_input_1, OVER)

    rows_sums = [
        jnp.sum(rows.astype(F32), axis=0, keepdims=True) for rows in (grad_rows_0, grad_rows_1)
    ]
    grad_halves_0, shares_0, unused_vectors = backward(
        grad_chunks_0,
        [rows_sums[0], vectors_1, rows_sums[1]],
        layer_0,
        saved_0,
        place,
        quarter_1,
        grad_input_1_here,
        grad_input_1_there,
    )
    (other_0,) = gate([grad_halves_0[1]], *pieces)
    total, *blocks = add(grad_halves_0[0], send(other_0, SIBLING), 4)
    shares_0 = shares_from_dp(shares_0)
    share_0 = quarter_sum(shares_0)
    mine_0 = (share_0.astype(F32) + send(share_0, BACK_OVER).astype(F32)).astype(BF)
    quarter = jnp.where(on_first, mine_0, quarter_1)
    mine, pair = fold(total, scatter_pieces(blocks), *shares_0[1:])
    mine_1, pair_1 = fold(first, pieces)
    result_1, unused_rounded, unused_rows = close_forward(
        [mine_1, send(pair_1, table(step(0, PAIR)))], rows_1, layer_1["norm"]
    )
    pair = send(pair, table(step(0, PAIR)))
    grad_input_0, unused_rounded = close_backward([mine, pair], rows_0, grad_rows_0)
    quarter = join(quarter, mine, pair)
    quarters = [quarter] + [over_dp(quarter, steps) for steps in (1, 2, 3)]
    grad_input_0_there = send(grad_input_0, BACK_OVER)
    vectors = sum_vectors(quarters)
    grad_gain, grad_shift, grad_b_out, grad_b_down = norm_grads(
        flag[None], vectors, send(vectors, table(step(0, 1)))
    )
    grad_up, grad_qkv, grad_down, grad_out, grad_b_up, grad_b_qkv = finish(
        place["scalars"], quarters
    )

    def output_of(value_0, there_0, here_1, there_1):
        here = jnp.where(on_first, value_0, here_1)
        there = jnp.where(on_first, there_0, there_1)
        return jnp.stack(
            [jnp.where(on_micro_0, here, there), jnp.where(on_micro_0, there, here)]
        )[None]

    return (
        output_of(
            result_0, result_0_there, send(result_1, SIBLING), send(result_1, OVER)
        ),
        output_of(
            grad_input_0,
            grad_input_0_there,
            grad_input_1_here,
            grad_input_1_there,
        ),
        grad_gain,
        grad_shift,
        grad_qkv.T.reshape(1, 1024, 1, QKV),
        grad_b_qkv[None],
        grad_out[None],
        grad_b_out,
        grad_up[None],
        grad_b_up,
        grad_down[None],
        grad_b_down,
    )


def solution(mesh):
    rows = P("dp", ("z", "y"), None)
    layer_rows = P("pipe", "dp", ("z", "y"), None)
    heads = P("pipe", None, ("z", "y"), None)
    split = P("pipe", ("z", "y"), None)
    units = P("pipe", None, ("z", "y"))
    whole = P("pipe", None)
    unit_bias = P("pipe", ("z", "y"))
    return jax.shard_map(
        body,
        mesh=Mesh(mesh.devices.reshape(2, 4, 4, 4), ("pipe", "dp", "z", "y")),
        in_specs=(
            rows,
            P("dp", None),
            rows,
            whole,
            whole,
            heads,
            split,
            split,
            whole,
            units,
            unit_bias,
            split,
            whole,
        ),
        out_specs=(
            layer_rows,
            layer_rows,
            whole,
            whole,
            heads,
            split,
            split,
            whole,
            units,
            unit_bias,
            split,
            whole,
        ),
        check_vma=False,
    )
```

```python
import functools

import jax
import jax.numpy as jnp
from jax import lax
from jax.experimental import pallas as pl
from jax.experimental.pallas import tpu as pltpu
from jax.sharding import Mesh, PartitionSpec as P

HD = 64
ROT = 16
FF_HERE = 256
QKV = 3 * HD
IN = FF_HERE + QKV
OUT = FF_HERE + HD
PACKED = IN + 16 + OUT
SUMMED = 832
MIXED = 384
F_LIMIT = 14
B_LIMIT = 23
PACK_LIMIT = 56
FOLD_COST = 30 * 10**9
ADD_COST = 30 * 10**9
ROWS = 2048
BLOCK = 128
SPAN = 512
SPANS = ROWS // SPAN
PER_SPAN = SPAN // BLOCK
EPSILON = 1e-05
NEGATIVE = -1e30
ROOT_HALF = 0.7071067811865476
INV_ROOT_TAU = 0.3989422804014327
DEVICES = ("pipe", "z", "y")
BF = jnp.bfloat16
F32 = jnp.float32


def table(rule):
    pairs = []
    for core in range(2):
        for z in range(4):
            for y in range(4):
                target = rule(core, z, y)
                if target is not None:
                    to_core, to_z, to_y = target
                    pairs.append((core * 16 + z * 4 + y, to_core * 16 + to_z % 4 * 4 + to_y))
    return pairs


def by_core(first, second):
    return table(lambda core, z, y: (first if core == 0 else second)(core, z, y))


def step(steps, flip=0):
    return lambda core, z, y: (core, z + steps, y ^ flip)


def nowhere(core, z, y):
    return None


PAIR = 3
SIBLING = table(lambda core, z, y: (1 - core, z, y))
OVER = by_core(nowhere, step(0, 1))
BACK_OVER = by_core(nowhere, lambda core, z, y: (0, z, y ^ 1))
SWAP = by_core(lambda core, z, y: (1, z, y ^ 1), lambda core, z, y: (0, z, y))
RING = (1, -1, 2)


def send(value, pairs):
    return lax.ppermute(value, DEVICES, pairs)


def gathered_blocks(core, z, y):
    def of(own):
        columns = (y ^ own, y ^ own ^ PAIR)
        steps = [0] + [-hops for hops in RING]
        return [(z + hops) % 4 * 4 + column for column in columns for hops in steps]

    first, second = jnp.stack(of(0)), jnp.stack(of(1))
    return jnp.where(
        core == 0, jnp.concatenate([first, second]), jnp.concatenate([second, first])
    ).astype(jnp.int32)


def with_sibling(blocks):
    return blocks + [send(block, SIBLING) for block in blocks]


def gather(rows):
    pair = send(rows, table(step(0, PAIR)))
    own = [send(rows, table(step(hops))) for hops in RING]
    far = [send(pair, table(step(hops))) for hops in RING]
    return with_sibling([rows] + own + [pair] + far)


def from_arguments(rows, on_first):
    near = send(rows, by_core(step(0, PAIR), step(0, 1)))
    beside = send(rows, by_core(nowhere, step(0, 2)))
    return jnp.concatenate([jnp.where(on_first, rows, near), jnp.where(on_first, near, beside)])


def gather_pieces(both):
    return with_sibling([both] + [send(both, table(step(hops))) for hops in RING])


def scatter(blocks):
    steps = [(-hops, 0) for hops in RING] + [(0, PAIR)] + [(-hops, PAIR) for hops in RING]
    return [send(block, table(step(hops, flip))) for block, (hops, flip) in zip(blocks, steps)]


def scatter_pieces(pieces):
    return [send(piece, table(step(-hops))) for piece, hops in zip(pieces, RING)]


def start_rows(lengths, total_rows):
    endings = jnp.cumsum(lengths)
    places = jnp.arange(total_rows, dtype=jnp.int32)
    passed = places[:, None] >= endings[None, :]
    return jnp.sum(jnp.where(passed, lengths[None, :], 0), axis=1)


def normalize(rows):
    average = jnp.mean(rows, axis=-1, keepdims=True)
    centred = rows - average
    inverse_std = lax.rsqrt(jnp.mean(centred * centred, axis=-1, keepdims=True) + EPSILON)
    return centred * inverse_std, inverse_std


def normalize_back(grad_rows, grad_scaled, rows):
    scaled, inverse_std = normalize(rows.astype(F32))
    return grad_rows.astype(F32) + inverse_std * (
        grad_scaled
        - jnp.mean(grad_scaled, axis=-1, keepdims=True)
        - scaled * jnp.mean(grad_scaled * scaled, axis=-1, keepdims=True)
    )


def block_of(index):
    return pl.ds(pl.multiple_of(index * BLOCK, BLOCK), BLOCK)


def dot(left, right, left_axis=1, right_axis=0):
    return lax.dot_general(
        left, right, (((left_axis,), (right_axis,)), ((), ())), preferred_element_type=F32
    )


def started(parts, sems, first):
    copies = [pltpu.make_async_copy(*part, sems.at[first + k]) for k, part in enumerate(parts)]
    for copy in copies:
        copy.start()
    return copies


def finished(copies):
    for copy in copies:
        copy.wait()


def stacked(refs, group, first):
    return jnp.concatenate(
        [refs[group * PER_SPAN + k][first : first + BLOCK] for k in range(PER_SPAN)]
    )


def chunk_of(refs, group):
    if len(refs) == 16:
        return stacked(refs, group, 0)
    pieces = refs[group // 2 * PER_SPAN : (group // 2 + 1) * PER_SPAN]
    return stacked(pieces, 0, group % 2 * BLOCK)


def half_of(refs, group):
    place = group % (SPANS // 2) * SPAN
    return refs[group // (SPANS // 2)].at[pl.ds(place, SPAN)]


def turned(pairs):
    lane = lax.broadcasted_iota(jnp.int32, pairs.shape, 1) % HD
    return jnp.where(
        lane < ROT // 2, -pltpu.roll(pairs, 2 * HD - ROT // 2, 1), pltpu.roll(pairs, ROT // 2, 1)
    )


def halves(pairs):
    lane = lax.broadcasted_iota(jnp.int32, pairs.shape, 1)
    queries = jnp.where(lane < HD, pairs * HD ** (-0.5), 0.0)
    return queries.astype(BF), pltpu.roll(pairs, HD, 1).astype(BF)


def penalty(scalars_ref, query_span, key_span):
    return jnp.where(key_span >= scalars_ref[16 + query_span], 0.0, -NEGATIVE).astype(F32)


def seen(scores):
    keys = lax.broadcasted_iota(jnp.int32, scores.shape, 0)
    queries = lax.broadcasted_iota(jnp.int32, scores.shape, 1)
    return jnp.where(keys <= queries, scores, NEGATIVE)


def store_parts(store_ref, saved_refs):
    lanes = (0, MIXED, MIXED + FF_HERE, MIXED + FF_HERE + 2 * HD)
    places = [
        store_ref.at[pl.ds(ROWS, ROWS), pl.ds(lane, ref.shape[1])]
        for lane, ref in zip(lanes, saved_refs)
    ]
    return places + [store_ref.at[pl.ds(0, ROWS)]]


def forward_kernel(n_chunks, stored, *refs):
    scalars_ref = refs[0]
    chunk_refs, refs = refs[1 : 1 + n_chunks], refs[1 + n_chunks :]
    w_in_ref, bias_ref, w_out_ref, cosine_ref, sine_ref = refs[:5]
    half_refs, log_sums_ref, refs = refs[5:7], refs[7], refs[8:]
    kept_hbm, kept_refs, refs = refs[:-9], refs[-9:-5], refs[-5:]
    mixed_ref, slope_ref, pairs_ref, values_ref = kept_refs
    queries_ref, keys_ref, turned_values_ref, ordered_ref, sems = refs
    copies = []
    if stored:
        kept_hbm = store_parts(kept_hbm[0], kept_refs)
        parts = []
        for k in range(16):
            source = chunk_refs[k // 8 * 4 + k % 4].at[pl.ds(k % 8 // 4 * BLOCK, BLOCK)]
            parts.append((source, kept_hbm[4].at[pl.ds(k * BLOCK, BLOCK)]))
        copies = started(parts, sems, 0)
    for group in range(SPANS):
        rows = slice(group * SPAN, (group + 1) * SPAN)
        projected = dot(chunk_of(chunk_refs, group), w_in_ref[...], 1, 1) + bias_ref[...]
        inner = projected[:, :FF_HERE]
        wave = 1.0 + lax.erf(inner * ROOT_HALF)
        mixed_ref[rows, :FF_HERE] = (0.5 * inner * wave).astype(BF)
        slope = 0.5 * wave + inner * jnp.exp(-0.5 * inner * inner) * INV_ROOT_TAU
        slope_ref[rows] = slope.astype(BF)
        for k in range(PER_SPAN):
            joined = projected[k * BLOCK : (k + 1) * BLOCK, FF_HERE:]
            place = block_of(scalars_ref[group * PER_SPAN + k])
            pairs = joined[:, : 2 * HD]
            pairs = pairs * cosine_ref[place] + turned(pairs) * sine_ref[place]
            pairs_ref[place] = pairs.astype(BF)
            queries_ref[place], keys_ref[place] = halves(pairs.astype(BF).astype(F32))
            values = joined[:, 2 * HD :]
            values_ref[place, :HD] = values.astype(BF)
            turned_values_ref[:, place] = values.T.astype(BF)
    copies += started(list(zip(kept_refs[1:], kept_hbm[1:4])), sems, 17)
    for i in range(SPANS):
        span = slice(i * SPAN, (i + 1) * SPAN)
        queries = queries_ref[span]
        scores, offsets, highest = [], [], None
        for j in range(i + 1):
            block = dot(keys_ref[j * SPAN : (j + 1) * SPAN], queries, 1, 1)
            block = seen(block) if i == j else block
            offset = 0.0 if i == j else penalty(scalars_ref, i, j)
            top = jnp.max(block, axis=0, keepdims=True) - offset
            highest = top if highest is None else jnp.maximum(highest, top)
            scores.append(block)
            offsets.append(offset)
        total, summed = 0.0, 0.0
        for j in range(i + 1):
            exponent = jnp.exp(scores[j] - (highest + offsets[j]))
            total = total + jnp.sum(exponent, axis=0, keepdims=True)
            summed = summed + dot(
                turned_values_ref[:, j * SPAN : (j + 1) * SPAN], exponent.astype(BF)
            )
        log_sums_ref[:, span] = highest + jnp.log(total)
        ordered_ref[span] = (summed / total).T.astype(BF)
    for group in range(SPANS):
        for k in range(PER_SPAN):
            index = group * PER_SPAN + k
            here = slice(index * BLOCK, (index + 1) * BLOCK)
            mixed_ref[here, FF_HERE:OUT] = ordered_ref[block_of(scalars_ref[index])]
        rows = slice(group * SPAN, (group + 1) * SPAN)
        half_of(half_refs, group)[...] = dot(mixed_ref[rows, :OUT], w_out_ref[...]).astype(BF)
    copies += started([(kept_refs[0], kept_hbm[0])], sems, 16)
    finished(copies)


def backward_kernel(separate, n_earlier, *refs):
    scalars_ref = refs[0]
    count = 16 if separate else 8
    chunk_refs, refs = refs[1 : 1 + count], refs[1 + count :]
    feature_refs, given_refs = [], None
    if separate:
        given_refs, refs = refs[:3], refs[3:]
    else:
        feature_refs, refs = refs[:16], refs[16:]

    w_in_ref, w_out_ref, kept_ref, norm_ref, log_sums_ref, cosine_ref, sine_ref = refs[:7]
    count = 5 if separate else 4
    n_saved = 1 if separate else 4
    saved_hbm, refs = refs[7 : 7 + n_saved], refs[7 + n_saved + n_earlier :]
    n_parts = 4 if separate else 2
    half_refs, quarter_refs, refs = refs[:2], refs[2 : 2 + n_parts], refs[2 + n_parts :]
    vectors_ref, refs = refs[0], refs[1:]
    saved_refs, refs = refs[:count], refs[count:]
    mixed_ref, slope_ref, pairs_ref, values_ref = saved_refs[:4]
    features_ref = saved_refs[-1]
    grad_in_ref, queries_ref, keys_ref, turned_keys_ref, grad_heads_ref, products_ref = refs[:6]
    grad_queries_ref, grad_keys_ref, grad_values_ref, grads_ref, sems = refs[6:]
    if separate:
        saved_hbm = store_parts(saved_hbm[0], saved_refs[:4])
    late = []
    if separate:
        lanes = [pl.ds(0, FF_HERE), pl.ds(FF_HERE, MIXED - FF_HERE)]
        mixed_parts = [(saved_hbm[0].at[:, part], mixed_ref.at[:, part]) for part in lanes]
        parts = [mixed_parts[1], (saved_hbm[1], slope_ref), (saved_hbm[2], pairs_ref)]
        finished(started(parts, sems, 0))
        parts = [(saved_hbm[3], values_ref), mixed_parts[0], (saved_hbm[4], features_ref)]
        late = started(parts, sems, 3)
    else:
        finished(started(list(zip(saved_hbm, saved_refs)), sems, 0))
    for group in range(SPANS):
        rows = slice(group * SPAN, (group + 1) * SPAN)
        grad_mixed = dot(chunk_of(chunk_refs, group), w_out_ref[...], 1, 1)
        grad_in_ref[rows, :FF_HERE] = (
            grad_mixed[:, :FF_HERE] * slope_ref[rows].astype(F32)
        ).astype(BF)
        for k in range(PER_SPAN):
            index = group * PER_SPAN + k
            here, place = slice(index * BLOCK, (index + 1) * BLOCK), block_of(scalars_ref[index])
            grad_heads = grad_mixed[k * BLOCK : (k + 1) * BLOCK, FF_HERE:].astype(BF)
            grad_heads_ref[place] = grad_heads
            product = grad_heads.astype(F32) * mixed_ref[here, FF_HERE:OUT].astype(F32)
            products_ref[:, place] = jnp.sum(product.T, axis=0, keepdims=True)
            queries_ref[here], keys = halves(pairs_ref[here].astype(F32))
            keys_ref[here] = keys
            turned_keys_ref[:, here] = keys[:, :HD].astype(F32).T.astype(BF)
    grad_queries_ref[...] = jnp.zeros_like(grad_queries_ref)
    finished(late[:1])
    for j in range(SPANS):
        key_span = slice(j * SPAN, (j + 1) * SPAN)
        keys, values = keys_ref[key_span], values_ref[key_span, :HD]
        grad_keys, grad_values = 0.0, 0.0
        for i in range(j, SPANS):
            span = slice(i * SPAN, (i + 1) * SPAN)
            queries, grad_heads = queries_ref[span], grad_heads_ref[span]
            scores = dot(keys, queries, 1, 1)
            scores = seen(scores) if i == j else scores
            offset = 0.0 if i == j else penalty(scalars_ref, i, j)
            probability = jnp.exp(scores - (log_sums_ref[:, span] + offset))
            grad_values += dot(probability.astype(BF), grad_heads)
            grad_probs = dot(values, grad_heads, 1, 1)
            grad_scores = (probability * (grad_probs - products_ref[:, span])).astype(BF)
            grad_keys += dot(grad_scores, queries)
            grad_queries_ref[:, span] += dot(turned_keys_ref[:, key_span], grad_scores)
        grad_keys_ref[key_span] = grad_keys
        grad_values_ref[key_span] = grad_values
    for group in range(SPANS):
        for k in range(PER_SPAN):
            index = group * PER_SPAN + k
            here, place = slice(index * BLOCK, (index + 1) * BLOCK), block_of(scalars_ref[index])
            grad_queries = (grad_queries_ref[:, place] * HD ** (-0.5)).T
            grad_pairs = jnp.concatenate([grad_queries, grad_keys_ref[place, :HD]], axis=1)
            grad_pairs = grad_pairs * cosine_ref[place] - turned(grad_pairs) * sine_ref[place]
            grad_in_ref[here, FF_HERE : FF_HERE + 2 * HD] = grad_pairs.astype(BF)
            grad_in_ref[here, FF_HERE + 2 * HD :] = grad_values_ref[place].astype(BF)
        rows = slice(group * SPAN, (group + 1) * SPAN)
        half_of(half_refs, group)[...] = dot(grad_in_ref[rows], w_in_ref[...]).astype(BF)
    finished(late[1:])
    raw, after, columns = 0.0, 0.0, 0.0
    ones = jnp.ones((SPAN, BLOCK), BF)
    total = jnp.zeros((1, IN), F32)
    for group in range(SPANS):
        rows = slice(group * SPAN, (group + 1) * SPAN)
        grad_in = grad_in_ref[rows]
        features = features_ref[rows] if separate else stacked(feature_refs, group, 0)
        raw += dot(grad_in, features, 0, 0)
        columns += dot(grad_in, ones, 0, 0)
        total += jnp.sum(grad_in.astype(F32), axis=0, keepdims=True)
        after += dot(mixed_ref[rows, :OUT], chunk_of(chunk_refs, group), 0, 0)
    kept = kept_ref[...].astype(F32)
    gain, shift = norm_ref[0:1], norm_ref[1:2]
    column = columns[:, :1]
    grads_ref[:IN] = (raw * gain + column * shift).astype(BF)
    grads_ref[IN : IN + 16] = jnp.zeros((16, 1024), BF)
    grads_ref[IN : IN + 1, :IN] = total.astype(BF)
    grads_ref[IN + 16 : PACKED] = after.astype(BF)
    grads_ref[PACKED:] = jnp.zeros((SUMMED - PACKED, 1024), BF)
    n = SUMMED // 4

    def quarter(index):
        return grads_ref[pl.ds(pl.multiple_of(index * n, 16), n)]

    here = scalars_ref[20]
    if separate:
        for ref, steps in zip(quarter_refs, (0, 1, 3, 2)):
            ref[...] = quarter(lax.rem(here + steps, 4))
    else:
        for ref, first in zip(quarter_refs, (here, here ^ 1)):
            ref[:n] = quarter(first)
            ref[n:] = quarter(first ^ 2)
    grad_gain = jnp.sum(raw * kept, axis=0, keepdims=True)
    grad_shift = jnp.sum(column * kept, axis=0, keepdims=True)
    if not separate:
        vectors_ref[0:1] = grad_gain
        vectors_ref[1:2] = grad_shift
        return
    row = lax.broadcasted_iota(jnp.int32, (8, 1024), 0)
    rows_ref, norm_1_ref, rows_1_ref = given_refs
    parts = (grad_gain, grad_shift, rows_ref[...], norm_1_ref[0:1], norm_1_ref[1:2], rows_1_ref[...])
    vectors = jnp.zeros((8, 1024), F32)
    for k, part in enumerate(parts):
        vectors = jnp.where(row == k, part, vectors)
    high = vectors.astype(BF).astype(F32)
    vectors = jnp.concatenate([high, vectors - high]).astype(BF)
    for ref in half_refs:
        ref[ROWS // 2 :] = vectors


def pack_kernel(*refs):
    up_hbm, qkv_hbm, down_hbm, out_hbm, b_up_ref, b_qkv_ref, gain_ref, shift_ref = refs[:8]
    b_out_ref, b_down_ref, unused_ref, *packed_hbm, up_ref, packed_ref, sems = refs[8:]
    parts = [
        (up_hbm, up_ref),
        (qkv_hbm, packed_ref.at[pl.ds(FF_HERE, QKV)]),
        (down_hbm, packed_ref.at[pl.ds(IN + 16, FF_HERE)]),
        (out_hbm, packed_ref.at[pl.ds(IN + 16 + FF_HERE, HD)]),
    ]
    copies = started(parts, sems, 0)
    biases = jnp.concatenate(
        [b_up_ref[...], b_qkv_ref[...], jnp.zeros((1, 1024 - IN), F32)], axis=1
    )
    rows = lax.broadcasted_iota(jnp.int32, (16, 1024), 0)
    small = jnp.zeros((16, 1024), F32)
    for value, high_row, low_row in (
        (biases, 0, 1),
        (gain_ref[...], 2, 5),
        (shift_ref[...], 3, 6),
        (b_out_ref[...] + b_down_ref[...], 4, 7),
    ):
        high = value.astype(BF).astype(F32)
        small = jnp.where(rows == high_row, high, small)
        small = jnp.where(rows == low_row, value - high, small)
    packed_ref[IN : IN + 16] = small.astype(BF)
    copies[0].wait()
    packed_ref[:FF_HERE] = up_ref[...].T
    finished(copies[1:])
    finished(started([(packed_ref, target) for target in packed_hbm], sems, 0))


def unpack_kernel(
    flag_ref, first_hbm, second_hbm, w_in_ref, kept_ref, w_out_ref, bias_ref, norm_ref, packed_ref, sem
):
    @pl.when(flag_ref[0] == 1)
    def _():
        copy = pltpu.make_async_copy(first_hbm, packed_ref, sem)
        copy.start()
        copy.wait()

    @pl.when(flag_ref[0] != 1)
    def _():
        copy = pltpu.make_async_copy(second_hbm, packed_ref, sem)
        copy.start()
        copy.wait()

    w_in = packed_ref[:IN]
    small = packed_ref[IN : IN + 16]
    shifts = dot(small, w_in, 1, 1)
    small = small.astype(F32)
    norm_ref[0:3] = small[2:5] + small[5:8]
    bias_ref[...] = small[0:1, :IN] + small[1:2, :IN] + shifts[3:4] + shifts[6:7]
    kept_ref[...] = w_in
    w_in_ref[...] = (w_in.astype(F32) * norm_ref[0:1]).astype(BF)
    w_out_ref[...] = packed_ref[IN + 16 : PACKED]


def finish_kernel(scalars_ref, *refs):
    up_ref, qkv_ref, down_ref, out_ref, b_up_ref, b_qkv_ref, whole_ref = refs[4:]
    n = SUMMED // 4
    for k in range(4):
        place = lax.rem(scalars_ref[20] + 4 - k, 4)
        whole_ref[pl.ds(pl.multiple_of(place * n, 16), n)] = refs[k][:n]
    up_ref[...] = whole_ref[:FF_HERE].astype(F32).T
    qkv_ref[...] = whole_ref[FF_HERE:IN].astype(F32)
    biases = whole_ref[IN : IN + 16].astype(F32)[0:1]
    b_up_ref[...] = biases[:, :FF_HERE]
    b_qkv_ref[...] = biases[:, FF_HERE:IN]
    down_ref[...] = whole_ref[IN + 16 : IN + 16 + FF_HERE].astype(F32)
    out_ref[...] = whole_ref[IN + 16 + FF_HERE : PACKED].astype(F32)


def vectors_kernel(*refs):
    n = SUMMED // 4
    total = 0.0
    for ref in refs[:4]:
        total += ref[n : n + 8].astype(F32) + ref[n + 8 :].astype(F32)
    refs[4][...] = total


def norms_kernel(flag_ref, mine_ref, there_ref, gain_ref, shift_ref, b_out_ref, b_down_ref):
    total = mine_ref[...] + there_ref[...]
    mine = jnp.where(flag_ref[0] == 1, total[0:3], total[3:6])
    gain_ref[...] = mine[0:1]
    shift_ref[...] = mine[1:2]
    b_out_ref[...] = mine[2:3]
    b_down_ref[...] = mine[2:3]


def add_kernel(n_out, with_vectors, *refs):
    own_ref, other_ref = refs[:2]
    out_refs = refs[-n_out:]
    count = 8 // n_out
    for k, ref in enumerate(out_refs):
        for part in range(count):
            index = k + part * n_out
            rows = slice(index * BLOCK, (index + 1) * BLOCK)
            value = own_ref[rows].astype(F32) + other_ref[rows].astype(F32)
            ref[part * BLOCK : (part + 1) * BLOCK] = value.astype(ref.dtype)
    if with_vectors:
        rows = slice(ROWS // 2, ROWS // 2 + 16)
        both = own_ref[rows].astype(F32) + other_ref[rows].astype(F32)
        vectors = both[:8] + both[8:]
        high = vectors.astype(BF).astype(F32)
        below = jnp.concatenate([high, vectors - high])
        for ref in out_refs:
            ref[count * BLOCK :] = below.astype(ref.dtype)


def total_of(refs):
    total = refs[0][:BLOCK]
    for ref in refs[1:]:
        total += ref[:BLOCK].astype(F32)
    return total


def close_forward_kernel(*refs):
    rows_ref, norm_ref, result_ref, rounded_ref, scaled_ref = refs[-5:]
    total = total_of(refs[:-5])
    result = rows_ref[...].astype(F32) + total + norm_ref[2:3]
    result_ref[...] = result
    rounded = result.astype(BF)
    rounded_ref[...] = rounded
    scaled_ref[...] = normalize(rounded.astype(F32))[0].astype(BF)


def close_backward_kernel(n_parts, *refs):
    rows_ref, grad_rows_ref = refs[n_parts : n_parts + 2]
    grad_ref, rounded_ref = refs[-2:]
    total = total_of(refs[:n_parts])
    grad = normalize_back(grad_rows_ref[...], total, rows_ref[...])
    grad_ref[...] = grad
    rounded_ref[...] = grad.astype(BF)


def fold_kernel(total_ref, *refs):
    mine_ref, pair_ref = refs[-2:]
    total = total_ref[...]
    for ref in refs[:3]:
        total += ref[...].astype(F32)
    size = mine_ref.shape[0]
    mine_ref[:BLOCK] = total[:BLOCK]
    pair_ref[:BLOCK] = total[BLOCK : 2 * BLOCK].astype(BF)
    if size > BLOCK:
        vectors = total[2 * BLOCK : 2 * BLOCK + 8] + total[2 * BLOCK + 8 :]
        high = vectors.astype(BF).astype(F32)
        mine_ref[BLOCK:] = jnp.concatenate([high, vectors - high])
        pair_ref[BLOCK:] = jnp.concatenate([high, vectors - high]).astype(BF)


def join_kernel(quarter_ref, mine_ref, pair_ref, joined_ref):
    n = SUMMED // 4
    joined_ref[:n] = quarter_ref[...]
    both = mine_ref[BLOCK:] + pair_ref[BLOCK:].astype(F32)
    vectors = both[:8] + both[8:]
    high = vectors.astype(BF).astype(F32)
    joined_ref[n:] = jnp.concatenate([high, vectors - high]).astype(BF)


def gate_kernel(*refs):
    pass


WHOLE = pl.BlockSpec(memory_space=pltpu.VMEM)
SCALARS = pl.BlockSpec(memory_space=pltpu.SMEM)
FAR = pl.BlockSpec(memory_space=pl.ANY)


def limit(size):
    return pltpu.CompilerParams(vmem_limit_bytes=size * 2**20)


SMALL = limit(12)
HALF = jax.ShapeDtypeStruct((ROWS // 2, 1024), BF)
SAVED = [
    jax.ShapeDtypeStruct((ROWS, width), BF) for width in (MIXED, FF_HERE, 2 * HD, 2 * HD, 1024)
]


STORE = jax.ShapeDtypeStruct((10 * ROWS, 1024), BF)


def like(shapes):
    return [pltpu.VMEM(shape.shape, shape.dtype) for shape in shapes]


def forward(chunks, layer, place, stored):
    saved = [STORE] if stored else SAVED[:4]
    outs = pl.pallas_call(
        functools.partial(forward_kernel, len(chunks), stored),
        out_shape=[HALF] * 2 + [jax.ShapeDtypeStruct((1, ROWS), F32)] + saved,
        in_specs=[SCALARS] + [WHOLE] * (len(chunks) + 5),
        out_specs=[WHOLE] * 3 + [FAR] * len(saved),
        scratch_shapes=like(SAVED[:4])
        + [
            pltpu.VMEM((ROWS, 2 * HD), BF),
            pltpu.VMEM((ROWS, 2 * HD), BF),
            pltpu.VMEM((HD, ROWS), BF),
            pltpu.VMEM((ROWS, HD), BF),
            pltpu.SemaphoreType.DMA((20,)),
        ],
        compiler_params=limit(F_LIMIT),
        cost_estimate=pl.CostEstimate(
            flops=12 * 10**9, bytes_accessed=2**24, transcendentals=ROWS * ROWS
        ),
        name="forward",
    )(
        place["scalars"],
        *chunks,
        layer["w_in"],
        layer["bias_in"],
        layer["w_out"],
        place["cosine"],
        place["sine"],
    )
    return outs[:2], outs[2:]


def backward(chunks, others, layer, saved, place, *earlier):
    separate = len(saved) == 2
    saved_shapes = SAVED if separate else SAVED[:4]
    half = (ROWS // 2 + 16 * separate, 1024)
    parts = 4 if separate else 2
    outs = pl.pallas_call(
        functools.partial(backward_kernel, separate, len(earlier)),
        out_shape=[jax.ShapeDtypeStruct(half, BF)] * 2
        + [jax.ShapeDtypeStruct((SUMMED // parts, 1024), BF)] * parts
        + [jax.ShapeDtypeStruct((2, 1024), F32)],
        in_specs=[SCALARS]
        + [WHOLE] * (len(chunks) + len(others) + 7)
        + [FAR] * (len(saved) - 1 + len(earlier)),
        out_specs=[WHOLE] * (3 + parts),
        scratch_shapes=like(saved_shapes)
        + [
            pltpu.VMEM((ROWS, IN), BF),
            pltpu.VMEM((ROWS, 2 * HD), BF),
            pltpu.VMEM((ROWS, 2 * HD), BF),
            pltpu.VMEM((HD, ROWS), BF),
            pltpu.VMEM((ROWS, HD), BF),
            pltpu.VMEM((1, ROWS), F32),
            pltpu.VMEM((HD, ROWS), F32),
            pltpu.VMEM((ROWS, 2 * HD), F32),
            pltpu.VMEM((ROWS, HD), F32),
            pltpu.VMEM((SUMMED, 1024), BF),
            pltpu.SemaphoreType.DMA((6,)),
        ],
        compiler_params=limit(B_LIMIT + 4 * separate),
        cost_estimate=pl.CostEstimate(
            flops=18 * 10**9, bytes_accessed=2**24, transcendentals=ROWS * ROWS
        ),
        name="backward",
    )(
        place["scalars"],
        *chunks,
        *others,
        layer["w_in"],
        layer["w_out"],
        layer["kept"],
        layer["norm"],
        saved[0],
        place["cosine"],
        place["sine"],
        *saved[1:],
        *earlier,
    )
    return outs[:2], outs[2:-1], outs[-1]


def pack(weights, vectors, earlier):
    return pl.pallas_call(
        pack_kernel,
        out_shape=[jax.ShapeDtypeStruct((PACKED, 1024), BF)] * 2,
        in_specs=[FAR] * 4 + [WHOLE] * 6 + [FAR],
        out_specs=[FAR] * 2,
        scratch_shapes=[
            pltpu.VMEM((1024, FF_HERE), BF),
            pltpu.VMEM((PACKED, 1024), BF),
            pltpu.SemaphoreType.DMA((4,)),
        ],
        compiler_params=limit(PACK_LIMIT),
        name="pack",
    )(*weights, *vectors, earlier)


def unpack(flag, first, second):
    w_in, kept, w_out, bias_in, norm = pl.pallas_call(
        unpack_kernel,
        out_shape=[
            jax.ShapeDtypeStruct((IN, 1024), BF),
            jax.ShapeDtypeStruct((IN, 1024), BF),
            jax.ShapeDtypeStruct((OUT, 1024), BF),
            jax.ShapeDtypeStruct((1, IN), F32),
            jax.ShapeDtypeStruct((3, 1024), F32),
        ],
        in_specs=[SCALARS] + [FAR] * 2,
        out_specs=[WHOLE] * 5,
        scratch_shapes=[pltpu.VMEM((PACKED, 1024), BF), pltpu.SemaphoreType.DMA],
        compiler_params=limit(16),
        name="unpack",
    )(flag, first, second)
    return {"w_in": w_in, "kept": kept, "w_out": w_out, "bias_in": bias_in, "norm": norm}


def finish(scalars, quarters):
    return pl.pallas_call(
        finish_kernel,
        out_shape=[
            jax.ShapeDtypeStruct((1024, FF_HERE), F32),
            jax.ShapeDtypeStruct((QKV, 1024), F32),
            jax.ShapeDtypeStruct((FF_HERE, 1024), F32),
            jax.ShapeDtypeStruct((HD, 1024), F32),
            jax.ShapeDtypeStruct((1, FF_HERE), F32),
            jax.ShapeDtypeStruct((1, QKV), F32),
        ],
        in_specs=[SCALARS] + [WHOLE] * 4,
        out_specs=[WHOLE] * 6,
        scratch_shapes=[pltpu.VMEM((SUMMED, 1024), BF)],
        compiler_params=limit(16),
        name="finish",
    )(scalars, *quarters)


def sum_vectors(quarters):
    return pl.pallas_call(
        vectors_kernel,
        out_shape=jax.ShapeDtypeStruct((8, 1024), F32),
        in_specs=[WHOLE] * 4,
        out_specs=WHOLE,
        compiler_params=SMALL,
        name="sum_vectors",
    )(*quarters)


def norm_grads(flag, mine, there):
    return pl.pallas_call(
        norms_kernel,
        out_shape=[jax.ShapeDtypeStruct((1, 1024), F32)] * 4,
        in_specs=[SCALARS] + [WHOLE] * 2,
        out_specs=[WHOLE] * 4,
        compiler_params=SMALL,
        name="norm_grads",
    )(flag, mine, there)


def gate(values, *earlier):
    n = len(values)
    return pl.pallas_call(
        gate_kernel,
        out_shape=[jax.ShapeDtypeStruct(value.shape, value.dtype) for value in values],
        in_specs=[FAR] * (n + len(earlier)),
        out_specs=[FAR] * n,
        input_output_aliases={k: k for k in range(n)},
        compiler_params=limit(1),
        name="gate",
    )(*values, *earlier)


def add(own, other, n_out, *earlier):
    with_vectors = own.shape[0] > ROWS // 2
    size = ROWS // 2 // n_out + 16 * with_vectors
    return pl.pallas_call(
        functools.partial(add_kernel, n_out, with_vectors),
        out_shape=[
            jax.ShapeDtypeStruct((size, 1024), BF if k else F32) for k in range(n_out)
        ],
        in_specs=[WHOLE] * 2 + [FAR] * len(earlier),
        out_specs=[WHOLE] * n_out,
        compiler_params=SMALL,
        cost_estimate=pl.CostEstimate(
            flops=ADD_COST, bytes_accessed=2**20, transcendentals=0
        ),
        name="add",
    )(own, other, *earlier)


def fold(total, arrived, *earlier):
    size = (total.shape[0] - 16) // 2 + 16 if total.shape[0] > 2 * BLOCK else BLOCK
    return pl.pallas_call(
        fold_kernel,
        out_shape=[
            jax.ShapeDtypeStruct((size, 1024), F32),
            jax.ShapeDtypeStruct((size, 1024), BF),
        ],
        in_specs=[WHOLE] * 4 + [FAR] * len(earlier),
        out_specs=[WHOLE] * 2,
        compiler_params=SMALL,
        cost_estimate=pl.CostEstimate(
            flops=FOLD_COST, bytes_accessed=2**20, transcendentals=0
        ),
        name="fold",
    )(total, *arrived, *earlier)


def join(quarter, mine, pair):
    return pl.pallas_call(
        join_kernel,
        out_shape=jax.ShapeDtypeStruct((SUMMED // 4 + 16, 1024), BF),
        in_specs=[WHOLE] * 3,
        out_specs=WHOLE,
        compiler_params=SMALL,
        name="join",
    )(quarter, mine, pair)


def close_forward(parts, rows, norm):
    shape = (BLOCK, 1024)
    return pl.pallas_call(
        close_forward_kernel,
        out_shape=[
            jax.ShapeDtypeStruct(shape, F32),
            jax.ShapeDtypeStruct(shape, BF),
            jax.ShapeDtypeStruct(shape, BF),
        ],
        in_specs=[WHOLE] * (len(parts) + 2),
        out_specs=[WHOLE] * 3,
        compiler_params=SMALL,
        name="close_forward",
    )(*parts, rows, norm)


def close_backward(parts, rows, grad_rows, *earlier):
    shape = (BLOCK, 1024)
    return pl.pallas_call(
        functools.partial(close_backward_kernel, len(parts)),
        out_shape=[jax.ShapeDtypeStruct(shape, F32), jax.ShapeDtypeStruct(shape, BF)],
        in_specs=[WHOLE] * (len(parts) + 2) + [FAR] * len(earlier),
        out_specs=[WHOLE] * 2,
        compiler_params=SMALL,
        name="close_backward",
    )(*parts, rows, grad_rows, *earlier)


def rotary_lanes(starts):
    lane = jnp.arange(2 * HD, dtype=jnp.int32) % HD
    inverse = jnp.power(10000.0, -2.0 * (lane % (ROT // 2)).astype(F32) / ROT)
    inverse = jnp.where(lane < ROT, inverse, 0.0)[None, :]
    coarse = (jnp.arange(0, ROWS, 64, dtype=jnp.int32) - starts[::64]).astype(F32)[:, None] * inverse
    fine = jnp.arange(64, dtype=jnp.int32).astype(F32)[:, None] * inverse
    cos_a, sin_a = jnp.cos(coarse)[:, None, :], jnp.sin(coarse)[:, None, :]
    cos_b, sin_b = jnp.cos(fine)[None], jnp.sin(fine)[None]
    shape = (ROWS, 2 * HD)
    return (
        (cos_a * cos_b - sin_a * sin_b).reshape(shape),
        (sin_a * cos_b + cos_a * sin_b).reshape(shape),
    )


def over_dp(part, steps):
    return lax.ppermute(part, "dp", [(i, (i + steps) % 4) for i in range(4)])


def shares_from_dp(shares):
    return [shares[0]] + [over_dp(part, steps) for part, steps in zip(shares[1:], (1, 3, 2))]


def exchanged(kept, given, flip):
    arrived = lax.ppermute(given, "dp", [(i, i ^ flip) for i in range(4)])
    return (kept.astype(F32) + arrived.astype(F32)).astype(BF)


def quarter_sum(shares):
    total = shares[0].astype(F32)
    for share in shares[1:]:
        total += share.astype(F32)
    return total.astype(BF)


def body(
    inputs,
    seq_lengths,
    cotangent,
    ln_gain,
    ln_bias,
    w_qkv,
    b_qkv,
    w_out,
    b_out,
    w_up,
    b_up,
    w_down,
    b_down,
):
    core, z, y = (lax.axis_index(name) for name in DEVICES)
    on_first = core == 0
    micro = jnp.where((y == 0) | (y == 3), 0, 1)
    on_micro_0 = micro == 0
    sent = jnp.where(on_first, micro, 1 - micro)

    def pick(value, index):
        return lax.dynamic_index_in_dim(value, index, 0, keepdims=False)

    sent_rows = pick(inputs, sent)
    scaled_rows = normalize(sent_rows.astype(F32))[0].astype(BF)
    scaled = from_arguments(scaled_rows, on_first)
    chunks_0 = gather_pieces(scaled)
    later_rows, later_grads = gate([sent_rows, pick(cotangent, sent)], scaled)
    rows_0 = jnp.where(on_first, later_rows, send(later_rows, OVER))
    both = from_arguments(later_grads, on_first)
    grad_rows_1 = both[:BLOCK]

    weights = (w_up[0], w_qkv.reshape(1024, QKV).T, w_down[0], w_out[0])
    small = (b_up, b_qkv[0], ln_gain, ln_bias, b_out, b_down)
    mine, again = pack(weights, small, scaled_rows)
    swapped = send(mine, SWAP)
    flag = jnp.where(on_first, 1, 0).astype(jnp.int32)
    layer_0 = unpack(flag[None], mine, swapped)

    starts = start_rows(pick(seq_lengths, micro), ROWS)
    cosine, sine = rotary_lanes(starts)
    scalars = [
        gathered_blocks(core, z, y),
        starts[::SPAN] // SPAN,
        lax.axis_index("dp")[None],
    ]
    place = {
        "scalars": jnp.concatenate([part.astype(jnp.int32) for part in scalars]),
        "cosine": cosine,
        "sine": sine,
    }

    (early,) = gate([both], chunks_0[2])
    pieces = [early] + [send(early, table(step(hops))) for hops in RING[:2]]
    halves_0, saved_0 = forward(chunks_0, layer_0, place, True)
    (other_0,) = gate([halves_0[1]], *pieces[1:])
    total, *blocks = add(halves_0[0], send(other_0, SIBLING), 8)
    arrived = scatter(blocks)
    result_0, rows_1, scaled_rows = close_forward([total] + arrived, rows_0, layer_0["norm"])
    (again,) = gate([again], rows_1)
    over = send(again, OVER)
    layer_1 = unpack(flag[None], swapped, over)
    chunks_1 = gather(scaled_rows)
    (late,) = gate([both], chunks_1[5])
    pieces.append(send(late, table(step(RING[2]))))
    halves_1, saved_1 = forward(chunks_1, layer_1, place, False)

    result_0_there = send(result_0, BACK_OVER)
    pieces[3:] = gate(pieces[3:], halves_1[0])
    grad_halves_1, halves_of_1, vectors_1 = backward(
        with_sibling(pieces), chunks_1, layer_1, saved_1, place, result_0_there
    )
    total, *blocks = add(grad_halves_1[0], send(grad_halves_1[1], SIBLING), 4)
    (other_1,) = gate([halves_1[1]], blocks[0])
    first, *pieces = add(halves_1[0], send(other_1, SIBLING), 4)
    (given,) = gate([halves_of_1[1]], blocks[0])
    half_1 = exchanged(halves_of_1[0], given, 1)
    mine, pair = fold(total, scatter_pieces(blocks))
    pair = send(pair, table(step(0, PAIR)))
    grad_input_1, grad_rows_0 = close_backward([mine, pair], rows_1, grad_rows_1)
    grad_chunks_0 = gather(grad_rows_0)
    n = SUMMED // 4
    share_1 = exchanged(half_1[:n], half_1[n:], 2)
    quarter_1 = (send(share_1, SIBLING).astype(F32) + send(share_1, OVER).astype(F32)).astype(BF)

    pieces = scatter_pieces(gate(pieces, grad_chunks_0[5]))
    grad_input_1_here = send(grad_input_1, SIBLING)
    grad_input_1_there = send(grad_input_1, OVER)

    rows_sums = [
        jnp.sum(rows.astype(F32), axis=0, keepdims=True) for rows in (grad_rows_0, grad_rows_1)
    ]
    grad_halves_0, shares_0, unused_vectors = backward(
        grad_chunks_0,
        [rows_sums[0], vectors_1, rows_sums[1]],
        layer_0,
        saved_0,
        place,
        quarter_1,
        grad_input_1_here,
        grad_input_1_there,
    )
    (other_0,) = gate([grad_halves_0[1]], *pieces)
    total, *blocks = add(grad_halves_0[0], send(other_0, SIBLING), 4)
    shares_0 = shares_from_dp(shares_0)
    share_0 = quarter_sum(shares_0)
    mine_0 = (share_0.astype(F32) + send(share_0, BACK_OVER).astype(F32)).astype(BF)
    quarter = jnp.where(on_first, mine_0, quarter_1)
    mine, pair = fold(total, scatter_pieces(blocks), *shares_0[1:])
    mine_1, pair_1 = fold(first, pieces)
    result_1, unused_rounded, unused_rows = close_forward(
        [mine_1, send(pair_1, table(step(0, PAIR)))], rows_1, layer_1["norm"]
    )
    pair = send(pair, table(step(0, PAIR)))
    grad_input_0, unused_rounded = close_backward([mine, pair], rows_0, grad_rows_0)
    quarter = join(quarter, mine, pair)
    quarters = [quarter] + [over_dp(quarter, steps) for steps in (1, 2, 3)]
    grad_input_0_there = send(grad_input_0, BACK_OVER)
    vectors = sum_vectors(quarters)
    grad_gain, grad_shift, grad_b_out, grad_b_down = norm_grads(
        flag[None], vectors, send(vectors, table(step(0, 1)))
    )
    grad_up, grad_qkv, grad_down, grad_out, grad_b_up, grad_b_qkv = finish(
        place["scalars"], quarters
    )

    def output_of(value_0, there_0, here_1, there_1):
        here = jnp.where(on_first, value_0, here_1)
        there = jnp.where(on_first, there_0, there_1)
        return jnp.stack(
            [jnp.where(on_micro_0, here, there), jnp.where(on_micro_0, there, here)]
        )[None]

    return (
        output_of(
            result_0, result_0_there, send(result_1, SIBLING), send(result_1, OVER)
        ),
        output_of(
            grad_input_0,
            grad_input_0_there,
            grad_input_1_here,
            grad_input_1_there,
        ),
        grad_gain,
        grad_shift,
        grad_qkv.T.reshape(1, 1024, 1, QKV),
        grad_b_qkv[None],
        grad_out[None],
        grad_b_out,
        grad_up[None],
        grad_b_up,
        grad_down[None],
        grad_b_down,
    )


def solution(mesh):
    rows = P("dp", ("z", "y"), None)
    layer_rows = P("pipe", "dp", ("z", "y"), None)
    heads = P("pipe", None, ("z", "y"), None)
    split = P("pipe", ("z", "y"), None)
    units = P("pipe", None, ("z", "y"))
    whole = P("pipe", None)
    unit_bias = P("pipe", ("z", "y"))
    return jax.shard_map(
        body,
        mesh=Mesh(mesh.devices.reshape(2, 4, 4, 4), ("pipe", "dp", "z", "y")),
        in_specs=(
            rows,
            P("dp", None),
            rows,
            whole,
            whole,
            heads,
            split,
            split,
            whole,
            units,
            unit_bias,
            split,
            whole,
        ),
        out_specs=(
            layer_rows,
            layer_rows,
            whole,
            whole,
            heads,
            split,
            split,
            whole,
            units,
            unit_bias,
            split,
            whole,
        ),
        check_vma=False,
    )
```
